256 devices in a mesh: gx: 16 (over x, y_hi, core), gy: 16 (over z, y_lo).
Axes of the slice: x: 4, y: 4 (y_hi: 2, y_lo: 2; y = y_hi * 2 + y_lo), z: 8, core: 2. Of those that a mesh axis runs over, the one named last changes fastest.
Arguments:
- scalars: float32 [2, 384, 512, 128], P(None, 'gx', 'gy'), may hold values from -10 to 10
- east_wind: float32 [384, 512, 128], P('gx', 'gy'), may hold values from -1 to 1
- north_wind: float32 [384, 512, 128], P('gx', 'gy'), may hold values from -1 to 1
- up_wind: float32 [384, 512, 128], P('gx', 'gy'), may hold values from -1 to 1
- diffusivity: float32 [384, 512, 128], P('gx', 'gy'), may hold values from 0.05 to 300
- target_profile: float32 [2, 128], replicated, may hold values from -6 to 6
Outputs:
- updated: float32 [2, 384, 512, 128], P(None, 'gx', 'gy')
The draws below stay inside these ranges and needn't reach their ends.
All inputs are finite; a program needn't handle non-finite values.
Results may differ from the reference program's by a relative error of at most 0.0003.
Values sent between devices are 32-bit elements; how exact they have to be, the bound alone decides.
A program may use at most 64 MiB of HBM per device.

```python
import math
import jax
import jax.numpy as jnp
from jax import lax

S = 2
CX = 24
NZ = 128
NX = 384
NY = 512
N_GX = 16


def draw_scalars(key, part):
    key = jax.random.fold_in(key, 11)
    key_prof, key_noise, key_scale = jax.random.split(key, 3)
    profile = jax.random.uniform(key_prof, (S, 1, 1, NZ), jnp.float32, -2.0, 2.0)
    ramp = 0.5 + jnp.arange(NX, dtype=jnp.float32).reshape(1, NX, 1, 1) / NX
    spread = jnp.exp(jax.random.uniform(key_scale, (S, NX, 1, 1), jnp.float32, math.log(0.3), math.log(3.0)))
    noise = jnp.clip(jax.random.normal(key_noise, (S, NX, NY, NZ), jnp.float32), -4.0, 4.0)
    return profile * ramp + 0.5 * spread * noise


def mixed_columns(key, strong_low, share):
    key_base, key_strong, key_pick = jax.random.split(key, 3)
    base = jnp.exp(jax.random.uniform(key_base, (NX, NY, NZ), jnp.float32, math.log(0.05), math.log(5.0)))
    strong = jnp.exp(jax.random.uniform(key_strong, (NX, NY, NZ), jnp.float32, math.log(strong_low), math.log(300.0)))
    pick = jax.random.uniform(key_pick, (NX, NY, 1), jnp.float32, 0.0, 1.0)
    return jnp.where(pick < share, strong, base)


def draw_diffusivity(key, part):
    key = jax.random.fold_in(key, 23)
    return mixed_columns(key, 20.0, 0.3)


def shard_levels(stream_key, extent, shards, low, high):
    gain = 1.0
    for position, shards_of in shards:
        draws = jax.random.uniform(jax.random.fold_in(jax.random.fold_in(stream_key, 6), position), (shards_of,), jnp.float32, low / len(shards), high / len(shards))
        gain = gain * jnp.repeat(jnp.exp(draws), extent[position] // shards_of).reshape((-1,) + (1,) * (len(extent) - 1 - position))
    return gain


def bell_draw(own_key, shape, scale, limit, kind=jnp.bfloat16):
    return jnp.clip(scale * jax.random.normal(own_key, shape, jnp.float32), -limit, limit).astype(kind)


def setup_inputs(seed: int = 0) -> dict:
    key_list = jax.random.split(jax.random.key(seed), 7)
    return {
        "scalars": draw_scalars(jax.random.fold_in(key_list[6], 71), 0),
        "east_wind": jnp.clip(jax.random.uniform(key_list[1], (NX, NY, NZ), jnp.float32, -1.0, 1.0) * shard_levels(key_list[1], (NX, NY, NZ), ((0, 16), (1, 16)), -0.4, 0.0), -1.0, 1.0),
        "north_wind": jnp.clip(jax.random.uniform(key_list[2], (NX, NY, NZ), jnp.float32, -1.0, 1.0) * shard_levels(key_list[2], (NX, NY, NZ), ((0, 16), (1, 16)), -0.4, 0.0), -1.0, 1.0),
        "up_wind": jnp.clip(jax.random.uniform(key_list[3], (NX, NY, NZ), jnp.float32, -1.0, 1.0) * shard_levels(key_list[3], (NX, NY, NZ), ((0, 16), (1, 16)), -0.4, 0.0), -1.0, 1.0),
        "diffusivity": draw_diffusivity(jax.random.fold_in(key_list[6], 71), 0),
        "target_profile": bell_draw(key_list[5], (S, NZ), 1.0, 6.0, jnp.float32),
    }


STEP = 0.3
RELAX = 0.5
EPSILON = 1e-6


def window(array, axis_num, start, length):
    return lax.slice_in_dim(array, start, start + length, axis=axis_num)


def weno_face(far_left, near_left, centre, near_right, far_right):
    cand_zero = (2.0 * far_left - 7.0 * near_left + 11.0 * centre) / 6.0
    cand_one = (-near_left + 5.0 * centre + 2.0 * near_right) / 6.0
    cand_two = (2.0 * centre + 5.0 * near_right - far_right) / 6.0
    first_a = far_left - 2.0 * near_left + centre
    first_b = far_left - 4.0 * near_left + 3.0 * centre
    second_a = near_left - 2.0 * centre + near_right
    second_b = near_left - near_right
    third_a = centre - 2.0 * near_right + far_right
    third_b = 3.0 * centre - 4.0 * near_right + far_right
    smooth_zero = 13.0 / 12.0 * first_a * first_a + 0.25 * first_b * first_b
    smooth_one = 13.0 / 12.0 * second_a * second_a + 0.25 * second_b * second_b
    smooth_two = 13.0 / 12.0 * third_a * third_a + 0.25 * third_b * third_b
    weight_zero = 0.1 / ((EPSILON + smooth_zero) * (EPSILON + smooth_zero))
    weight_one = 0.6 / ((EPSILON + smooth_one) * (EPSILON + smooth_one))
    weight_two = 0.3 / ((EPSILON + smooth_two) * (EPSILON + smooth_two))
    total = weight_zero * cand_zero + weight_one * cand_one + weight_two * cand_two
    return total / (weight_zero + weight_one + weight_two)


def face_flux(field, axis_num, first, count, speed):
    cells = [window(field, axis_num, first + offset, count) for offset in range(-3, 3)]
    from_low = weno_face(cells[0], cells[1], cells[2], cells[3], cells[4])
    from_high = weno_face(cells[5], cells[4], cells[3], cells[2], cells[1])
    return jnp.maximum(speed, 0.0) * from_low + jnp.minimum(speed, 0.0) * from_high


def tendency(field, field_margin, east, north, upward, wind_margin, inner):
    size_x = field.shape[1] - 2 * field_margin + 2 * inner
    size_y = field.shape[2] - 2 * field_margin + 2 * inner
    levels = field.shape[3]
    start = field_margin - inner
    wind_start = wind_margin - inner
    along_x = window(field, 2, start, size_y)
    speed_x = window(window(east, 1, wind_start, size_y), 0, wind_start, size_x + 1)
    flux_x = face_flux(along_x, 1, start, size_x + 1, speed_x)
    along_y = window(field, 1, start, size_x)
    speed_y = window(window(north, 0, wind_start, size_x), 1, wind_start, size_y + 1)
    flux_y = face_flux(along_y, 2, start, size_y + 1, speed_y)
    region = window(along_y, 2, start, size_y)
    speed_z = window(window(upward, 0, wind_start, size_x), 1, wind_start, size_y)
    above_ground = lax.broadcasted_iota(jnp.int32, speed_z.shape, 2) > 0
    speed_z = jnp.where(above_ground, speed_z, jnp.zeros_like(speed_z))
    speed_z = jnp.concatenate([speed_z, jnp.zeros_like(speed_z[:, :, :1])], axis=2)
    lowest = region[..., :1]
    highest = region[..., levels - 1:]
    padded = jnp.concatenate([lowest, lowest, lowest, region, highest, highest, highest], axis=3)
    flux_z = face_flux(padded, 3, 3, levels + 1, speed_z)
    return (-(flux_x[:, 1:] - flux_x[:, :-1]) - (flux_y[:, :, 1:] - flux_y[:, :, :-1])
            - (flux_z[..., 1:] - flux_z[..., :-1]))


def thomas(coupling, coupling_above, rhs):
    def forward(carry, inputs):
        prev_c, prev_d = carry
        low_k, up_k, rhs_k = inputs
        denom = 1.0 + low_k + up_k + low_k * prev_c
        new_c = -up_k / denom
        new_d = (rhs_k + low_k * prev_d) / denom
        return (new_c, new_d), (new_c, new_d)

    zeros = jnp.zeros(rhs.shape[1:], jnp.float32)
    done, (cps, dps) = lax.scan(forward, (zeros, zeros), (coupling, coupling_above, rhs))

    def backward(next_value, inputs):
        cp_k, dp_k = inputs
        value = dp_k - cp_k * next_value
        return value, value

    done, result = lax.scan(backward, zeros, (cps, dps), reverse=True)
    return result


def couplings(diffusivity):
    above_ground = lax.broadcasted_iota(jnp.int32, diffusivity.shape, 2) > 0
    coupling = jnp.where(above_ground, STEP * diffusivity, jnp.zeros_like(diffusivity))
    coupling_above = jnp.concatenate([coupling[..., 1:], jnp.zeros_like(coupling[..., :1])], axis=2)
    return coupling, coupling_above


def reference(scalars, east_wind, north_wind, up_wind, diffusivity, target_profile):
    east_pad = jnp.concatenate([east_wind, east_wind[:1]], axis=0)
    north_pad = jnp.concatenate([north_wind, north_wind[:, :1]], axis=1)

    def advect(field):
        padded = jnp.concatenate([field[:, -3:], field, field[:, :3]], axis=1)
        padded = jnp.concatenate([padded[:, :, -3:], padded, padded[:, :, :3]], axis=2)

        def one_block(block):
            start = (block * CX).astype(jnp.int32)
            field_block = lax.dynamic_slice_in_dim(padded, start, CX + 6, 1)
            east_block = lax.dynamic_slice_in_dim(east_pad, start, CX + 1, 0)
            north_block = lax.dynamic_slice_in_dim(north_pad, start, CX, 0)
            up_block = lax.dynamic_slice_in_dim(up_wind, start, CX, 0)
            return tendency(field_block, 3, east_block, north_block, up_block, 0, 0)

        pieces = lax.map(one_block, jnp.arange(N_GX, dtype=jnp.int32))
        return jnp.moveaxis(pieces, 0, 1).reshape(field.shape)

    current = scalars
    for fraction in (1.0 / 3.0, 0.5, 1.0):
        current = scalars + (STEP * fraction) * advect(current)
    level_mean = jnp.sum(scalars, axis=(1, 2)) / (NX * NY)
    nudged = current - RELAX * (level_mean - target_profile)[:, None, None, :]
    coupling, coupling_above = couplings(diffusivity)
    low_cols = jnp.transpose(coupling, (2, 0, 1)).reshape(NZ, -1)
    up_cols = jnp.transpose(coupling_above, (2, 0, 1)).reshape(NZ, -1)
    columns = jnp.transpose(nudged, (0, 3, 1, 2)).reshape(S, NZ, -1)
    solved = lax.map(lambda column_set: thomas(low_cols, up_cols, column_set), columns)
    return jnp.transpose(solved.reshape(S, NZ, NX, NY), (0, 2, 3, 1))
```

```python
import functools

import jax
import jax.numpy as jnp
from jax import lax
from jax.experimental import pallas as pl
from jax.experimental.pallas import tpu as pltpu
from jax.sharding import PartitionSpec as P

STEP = 0.3
RELAX = 0.5
EPSILON = 1e-06
EPS = 0.75 * EPSILON
EPS2 = EPS * EPS

CX, CY, NZ = 24, 32, 128
H = 3
XROWS = (CX + 2 * H) * CY
YROWS = (CY + 2 * H) * CX
CELLS = CX * CY
TILES = CELLS // 128
GROUP = 4
ZROWS = 96
PART = 24
LEVELS = 6 * PART
PLACES = (0, 1, 3)
MESH = pl.DeviceIdType.MESH


def cell(dm, em, dp, ep):
    g = dp - dm
    b = (g * g + EPS) + ep * dm
    g2 = g + g
    left = b - g2 * em
    right = b + g2 * ep
    return g, left * left, b * b, right * right


def face(u, total, g_low, g_high, t_low, t_mid, t_high, r2, r1, c1, c0, l0, l1):
    pos = u > 0.0
    b0 = jnp.where(pos, r2, l1)
    b1 = jnp.where(pos, c1, c0)
    b2 = jnp.where(pos, l0, r1)
    gs = jnp.where(pos, g_low, g_high)
    ts = jnp.where(pos, t_low, t_high)
    b0 = 3.0 * b0
    c2 = b2 + b2
    num = b1 * (c2 * ts + b0 * t_mid)
    den = b1 * (b2 + b0) + b0 * c2
    part = num * pl.reciprocal(den, approx=True)
    return u * (3.0 * total - gs) - jnp.abs(u) * part


def march(load_f, load_u, first, last):
    f, d, q, t = {}, {}, {}, {}

    def get_f(i):
        if i not in f:
            f[i] = load_f(i)
        return f[i]

    def get_d(i):
        if i not in d:
            diff = get_f(i) - get_f(i - 1)
            d[i] = (diff, 0.75 * diff)
        return d[i]

    def get_q(i):
        if i not in q:
            q[i] = cell(*get_d(i), *get_d(i + 1))
        return q[i]

    def get_t(i):
        if i not in t:
            t[i] = get_q(i)[0] - get_q(i - 1)[0]
        return t[i]

    out = []
    for j in range(first, last + 1):
        lo2, lo1, hi0, hi1 = get_q(j - 2), get_q(j - 1), get_q(j), get_q(j + 1)
        out.append(
            face(
                load_u(j), get_f(j - 1) + get_f(j), lo1[0], hi0[0], get_t(j - 1), get_t(j), get_t(j + 1),
                lo2[3], lo1[3], lo1[2], hi0[2], hi0[1], hi1[1],
            )
        )
    return out


def shifted_z(f, lane):
    below, below2, above = pltpu.roll(f, 1, 1), pltpu.roll(f, 2, 1), pltpu.roll(f, NZ - 1, 1)
    d = jnp.where(lane == 0, 0.0, f - below)
    d_low = jnp.where(lane <= 1, 0.0, below - below2)
    d_high = jnp.where(lane == NZ - 1, 0.0, above - f)
    g, left, mid, right = cell(d, 0.75 * d, d_high, 0.75 * d_high)
    g_low = d - d_low
    t = g - g_low
    return (
        f + below, g_low, g, pltpu.roll(t, 1, 1), t, pltpu.roll(t, NZ - 1, 1), pltpu.roll(right, 2, 1),
        pltpu.roll(right, 1, 1), pltpu.roll(mid, 1, 1), mid, left, pltpu.roll(left, NZ - 1, 1),
    )


def flux_z(u, parts, lane):
    total, g_low, g, t_low, t, t_high, r2, r1, c1, c0, l0, l1 = parts
    last = lane == NZ - 1
    t_high = jnp.where(last, -g, t_high)
    r2 = jnp.where(lane == 1, EPS2, r2)
    l1 = jnp.where(last, EPS2, l1)
    return face(u, total, g_low, g, t_low, t, t_high, r2, r1, c1, c0, l0, l1)


def digits(n):
    out, stride = [], 1
    while stride < n:
        radix = min(4, n // stride)
        out.append((stride, radix))
        stride *= radix
    return out


def kernel(
    n_x, n_y,
    scal, east, north, upw, diff, target, adv, shift, im, av, cp,
    xs, bs, ys, zs, fz, fr, tx, ty, ex, ny, nraw, uz, kd, tg, fk, es, aro, ari,
    lsem, hsend, hrecv, wsend, wrecv, asend, arecv,
):
    mx, my = lax.axis_index("gx"), lax.axis_index("gy")
    x_up, x_dn = lax.rem(mx + 1, n_x), lax.rem(mx + n_x - 1, n_x)
    y_up, y_dn = lax.rem(my + 1, n_y), lax.rem(my + n_y - 1, n_y)
    plan = [("x", d) for d in digits(n_x)] + [("y", d) for d in digits(n_y)]
    rounds = len(plan)

    def partner(r, k):
        axis, (stride, radix) = plan[r]
        me = mx if axis == "x" else my
        digit = lax.rem(lax.div(me, stride), radix)
        other = me + stride * (lax.rem(digit + k, radix) - digit)
        return (other, my) if axis == "x" else (mx, other)

    loads = [
        pltpu.make_async_copy(scal.at[0], xs.at[0, 0, pl.ds(H * CY, CELLS)], lsem.at[0]),
        pltpu.make_async_copy(scal.at[1], xs.at[0, 1, pl.ds(H * CY, CELLS)], lsem.at[1]),
        pltpu.make_async_copy(north, nraw, lsem.at[2]),
        pltpu.make_async_copy(east, ex.at[pl.ds(0, CELLS)], lsem.at[3]),
        pltpu.make_async_copy(diff, kd, lsem.at[4]),
        pltpu.make_async_copy(upw, uz, lsem.at[5]),
        pltpu.make_async_copy(target, tg, lsem.at[6]),
        pltpu.make_async_copy(scal, bs, lsem.at[7]),
    ]
    for load in loads:
        load.start()

    barrier = pltpu.get_barrier_semaphore()
    peers = [(x_up, my), (x_dn, my), (mx, y_up), (mx, y_dn)] + [
        partner(r, k) for r in range(rounds) for k in range(1, plan[r][1][1])
    ]
    for peer in peers:
        pl.semaphore_signal(barrier, inc=1, device_id=peer, device_id_type=MESH)

    def halo(t, way, plane=None):
        st, s = lax.div(t, 2), lax.rem(t, 2)
        size = CY if way < 2 else CX
        buffer, length = (xs, CX) if way < 2 else (ys, CY)
        to = ((x_up, my), (x_dn, my), (mx, y_up), (mx, y_dn))[way]
        source, target_row = ((length, 0), (H, length + H))[way % 2]
        first, count = (0, H) if plane is None else (plane, 1)
        return pltpu.make_async_remote_copy(
            src_ref=buffer.at[st, s, pl.ds((source + first) * size, count * size)],
            dst_ref=buffer.at[st, s, pl.ds((target_row + first) * size, count * size)],
            send_sem=hsend.at[t, way], recv_sem=hrecv.at[t, way], device_id=to, device_id_type=MESH,
        )

    def send_halos(t, ways):
        for plane in range(H):
            for way in ways:
                halo(t, way, plane).start()

    def exchange(r):
        return [
            pltpu.make_async_remote_copy(
                src_ref=aro.at[r], dst_ref=ari.at[r, k - 1], send_sem=asend.at[r, k - 1],
                recv_sem=arecv.at[r, k - 1], device_id=partner(r, k), device_id_type=MESH,
            )
            for k in range(1, plan[r][1][1])
        ]

    def send_sums(r):
        for copy in exchange(r):
            copy.start()

    def add_sums(r):
        total = aro[r]
        for k, copy in enumerate(exchange(r)):
            copy.wait_recv()
            total = total + ari[r, k]
        aro[r + 1] = total

    east_edge = pltpu.make_async_remote_copy(
        src_ref=ex.at[pl.ds(0, CY)], dst_ref=ex.at[pl.ds(CELLS, CY)], send_sem=wsend.at[0], recv_sem=wrecv.at[0],
        device_id=(x_dn, my), device_id_type=MESH,
    )
    north_edge = pltpu.make_async_remote_copy(
        src_ref=ny.at[pl.ds(0, CX)], dst_ref=ny.at[pl.ds(CELLS, CX)], send_sem=wsend.at[1], recv_sem=wrecv.at[1],
        device_id=(mx, y_dn), device_id_type=MESH,
    )

    def to_y(st, s, x, value):
        for i in range(CY // 8):
            ys[st, s, pl.ds((H + 8 * i) * CX + x, 8, stride=CX), :] = value[8 * i : 8 * i + 8]

    loads[0].wait()
    loads[1].wait()
    pl.semaphore_wait(barrier, len(peers))
    for s in range(2):
        send_halos(s, (0, 1))
    for s in range(2):

        def convert(g, total, s=s):
            values = [xs[0, s, pl.ds((H + g * GROUP + p) * CY, CY), :] for p in range(GROUP)]
            for p, value in enumerate(values):
                to_y(0, s, g * GROUP + p, value)
            return total + sum(values)

        total = lax.fori_loop(0, CX // GROUP, convert, jnp.zeros((CY, NZ), jnp.float32))
        aro[0, s : s + 1, :] = jnp.sum(total, axis=0, keepdims=True)
        send_halos(s, (2, 3))
    send_sums(0)

    loads[2].wait()

    def scale_north(g, _):
        values = [nraw[pl.ds((g * GROUP + p) * CY, CY), :] * (1.0 / 6.0) for p in range(GROUP)]
        for p, value in enumerate(values):
            for i in range(CY // 8):
                ny[pl.ds(8 * i * CX + g * GROUP + p, 8, stride=CX), :] = value[8 * i : 8 * i + 8]
        return 0

    lax.fori_loop(0, CX // GROUP, scale_north, 0)
    north_edge.start()
    loads[3].wait()

    def scale_east(g, _):
        rows = pl.ds(pl.multiple_of(g * GROUP * CY, CY), GROUP * CY)
        ex[rows, :] = ex[rows, :] * (1.0 / 6.0)
        return 0

    lax.fori_loop(0, CX // GROUP, scale_east, 0)
    east_edge.start()
    loads[5].wait()
    lane = lax.broadcasted_iota(jnp.int32, (8, NZ), 1)
    lane_all = lax.broadcasted_iota(jnp.int32, (GROUP * CY, NZ), 1)

    def scale_up(g, _):
        rows = pl.ds(pl.multiple_of(g * GROUP * CY, CY), GROUP * CY)
        uz[rows, :] = jnp.where(lane_all == 0, 0.0, uz[rows, :] * (1.0 / 6.0))
        return 0

    lax.fori_loop(0, CX // GROUP, scale_up, 0)

    loads[4].wait()
    loads[6].wait()
    loads[7].wait()
    for c in range(8):
        if c < TILES:
            levels = jnp.transpose(kd[pl.ds(c * 128, 128), :]) * STEP
        else:
            levels = jnp.zeros((NZ, 128), jnp.float32)
        fk[pl.ds(c, NZ, stride=8), :] = levels
    fk[pl.ds(0, 8), :] = jnp.zeros((8, 128), jnp.float32)
    fk[pl.ds(NZ * 8, (LEVELS - NZ + 1) * 8), :] = jnp.zeros(((LEVELS - NZ + 1) * 8, 128), jnp.float32)
    es[...] = jnp.zeros((8, 128), jnp.float32)

    def factor(part):
        base = pl.multiple_of(part * (PART * 8), 8)
        low = fk[pl.ds(base, 8), :]
        e = es[...]
        for i in range(PART):
            row = pl.ds(base + 8 * i, 8)
            above = fk[pl.ds(base + 8 * i + 8, 8), :]
            g = 1.0 + low * e
            inverse = pl.reciprocal(g + above, approx=True)
            e = g * inverse
            im[row, :] = inverse
            av[row, :] = low * inverse
            cp[row, :] = above * inverse
            low = above
        es[...] = e

    def x_faces(st, s, row, first, last):
        flux = march(
            lambda x: xs[st, s, pl.ds((H + x) * CY + row, 8), :],
            lambda x: ex[pl.ds(x * CY + row, 8), :],
            first, last,
        )
        for x in range(first, last):
            tx[pl.ds(x * CY + row, 8), :] = flux[x - first] - flux[x - first + 1]

    def y_faces(st, s, row, first, last):
        flux = march(
            lambda y: ys[st, s, pl.ds((H + y) * CX + row, 8), :],
            lambda y: ny[pl.ds(y * CX + row, 8), :],
            first, last,
        )
        for y in range(first, last):
            ty[pl.ds(row * CY + y, 8, stride=CY), :] = flux[y - first] - flux[y - first + 1]

    def z_faces(st, s):
        groups = CELLS // ZROWS

        def group(i, _):
            late = pl.multiple_of(lax.max(i - 1, 0) * ZROWS, ZROWS)
            now = pl.multiple_of(lax.min(i, groups - 1) * ZROWS, ZROWS)
            for v in range(ZROWS // 8):
                flux = flux_z(
                    uz[pl.ds(late + 8 * v, 8), :], [zs[part, 8 * v : 8 * v + 8, :] for part in range(12)], lane
                )
                fz[pl.ds(late + 8 * v, 8), :] = flux
                fr[pl.ds(late + 8 * v, 8), :] = pltpu.roll(flux, NZ - 1, 1)
            for v in range(ZROWS // 8):
                parts = shifted_z(xs[st, s, pl.ds(H * CY + now + 8 * v, 8), :], lane)
                for part in range(12):
                    zs[part, 8 * v : 8 * v + 8, :] = parts[part]
            return 0

        lax.fori_loop(0, groups + 1, group, 0)

    def columns(count, work):
        def block(i, _):
            work(pl.multiple_of(i * 8, 8))
            return 0

        lax.fori_loop(0, count, block, 0)

    def step(t, _):
        st, s = lax.div(t, 2), lax.rem(t, 2)
        factor(t)
        columns(CX // 8, lambda row: y_faces(st, s, row, H, CY - H))
        columns(CY // 8, lambda row: x_faces(st, s, row, H, CX - H))
        z_faces(st, s)
        for r, place in enumerate(PLACES[: rounds - 1]):

            @pl.when(t == place)
            def _(r=r):
                add_sums(r)
                send_sums(r + 1)


        @pl.when(t == 0)
        def _():
            north_edge.wait_recv()
            east_edge.wait_recv()

        halo(t, 2).wait_recv()
        halo(t, 3).wait_recv()
        columns(CX // 8, lambda row: (y_faces(st, s, row, 0, H), y_faces(st, s, row, CY - H, CY)))
        halo(t, 0).wait_recv()
        halo(t, 1).wait_recv()
        columns(CY // 8, lambda row: (x_faces(st, s, row, 0, H), x_faces(st, s, row, CX - H, CX)))
        coef = jnp.where(st == 0, STEP / 3.0, jnp.where(st == 1, STEP * 0.5, STEP)).astype(jnp.float32)

        def update(g, _):
            rows = pl.ds(pl.multiple_of(g * GROUP * CY, CY), GROUP * CY)
            value = bs[s, rows, :] + coef * (tx[rows, :] + ty[rows, :] + (fz[rows, :] - fr[rows, :]))
            xs[st + 1, s, pl.ds(pl.multiple_of((H + g * GROUP) * CY, CY), GROUP * CY), :] = value
            for p in range(GROUP):
                to_y(st + 1, s, g * GROUP + p, value[p * CY : (p + 1) * CY])
            return 0

        lax.fori_loop(0, CX // GROUP, update, 0)

        @pl.when(st < 2)
        def _():
            send_halos(t + 2, range(4))

        return 0

    lax.fori_loop(0, 6, step, 0)

    add_sums(rounds - 1)
    cells = float(n_x * CX * n_y * CY)
    shift[...] = RELAX * (aro[rounds] * (1.0 / cells) - tg[...])
    for s in range(2):
        adv[s] = xs[3, s, pl.ds(H * CY, CELLS), :]

    def drain(t, _):
        for way in range(4):
            halo(t, way).wait_send()
        return 0

    lax.fori_loop(0, 6, drain, 0)

    for r in range(rounds):
        for copy in exchange(r):
            copy.wait_send()
    east_edge.wait_send()
    north_edge.wait_send()


def solve(adv, shift, im, av, cp, out, rh, ob, osem):
    for s in range(2):
        for c in range(TILES):
            value = adv[s, pl.ds(c * 128, 128), :] - shift[s : s + 1, :]
            rh[s, pl.ds(c, NZ, stride=8), :] = jnp.transpose(value)

    zero = jnp.zeros((8, 128), jnp.float32)

    def forward(k8, carry):
        d0, d1 = carry
        base = pl.multiple_of(k8 * 64, 64)
        rows = [pl.ds(base + 8 * i, 8) for i in range(8)]
        data = [(im[r, :], av[r, :], rh[0, r, :], rh[1, r, :]) for r in rows]
        for i, (inverse, a, r0, r1) in enumerate(data):
            d0 = r0 * inverse + a * d0
            d1 = r1 * inverse + a * d1
            rh[0, rows[i], :] = d0
            rh[1, rows[i], :] = d1
        return d0, d1

    lax.fori_loop(0, NZ // 8, forward, (zero, zero))

    def backward(j8, carry):
        v0, v1 = carry
        base = pl.multiple_of((NZ // 8 - 1 - j8) * 64, 64)
        rows = [pl.ds(base + 56 - 8 * i, 8) for i in range(8)]
        data = [(cp[r, :], rh[0, r, :], rh[1, r, :]) for r in rows]
        for i, (c, r0, r1) in enumerate(data):
            v0 = r0 + c * v0
            v1 = r1 + c * v1
            rh[0, rows[i], :] = v0
            rh[1, rows[i], :] = v1
        return v0, v1

    lax.fori_loop(0, NZ // 8, backward, (zero, zero))
    stores = []
    for s in range(2):
        for c in range(TILES):
            rows = pl.ds(c * 128, 128)
            ob[s, rows, :] = jnp.transpose(rh[s, pl.ds(c, NZ, stride=8), :])
            store = pltpu.make_async_copy(ob.at[s, rows], out.at[s, rows], osem.at[s, c])
            store.start()
            stores.append(store)
    for store in stores:
        store.wait()


def in_hbm(value):
    return pltpu.with_memory_space_constraint(value, pltpu.HBM)


def body(n_x, n_y, scalars, east_wind, north_wind, up_wind, diffusivity, target_profile):
    rounds = len(digits(n_x)) + len(digits(n_y))
    hbm = pl.BlockSpec(memory_space=pltpu.HBM)
    f32 = jnp.float32
    vmem = pltpu.VMEM
    dma = pltpu.SemaphoreType.DMA
    resident = pl.BlockSpec(memory_space=pltpu.VMEM)
    columns = jax.ShapeDtypeStruct((LEVELS * 8, 128), f32)
    parts = pl.pallas_call(
        functools.partial(kernel, n_x, n_y),
        out_shape=[
            jax.ShapeDtypeStruct((2, CELLS, NZ), f32), jax.ShapeDtypeStruct((2, NZ), f32), columns, columns, columns,
        ],
        in_specs=[hbm] * 6,
        out_specs=[resident] * 5,
        scratch_shapes=[
            vmem((4, 2, XROWS, NZ), f32),
            vmem((2, CELLS, NZ), f32),
            vmem((4, 2, YROWS, NZ), f32),
            vmem((12, ZROWS, NZ), f32),
            vmem((CELLS, NZ), f32),
            vmem((CELLS, NZ), f32),
            vmem((CELLS, NZ), f32),
            vmem((CELLS, NZ), f32),
            vmem((CELLS + CY, NZ), f32),
            vmem((CELLS + CX, NZ), f32),
            vmem((CELLS, NZ), f32),
            vmem((CELLS, NZ), f32),
            vmem((CELLS, NZ), f32),
            vmem((2, NZ), f32),
            vmem(((LEVELS + 1) * 8, 128), f32),
            vmem((8, 128), f32),
            vmem((rounds + 1, 2, NZ), f32),
            vmem((rounds, 3, 2, NZ), f32),
            dma((8,)),
            dma((6, 4)),
            dma((6, 4)),
            dma((2,)),
            dma((2,)),
            dma((rounds, 3)),
            dma((rounds, 3)),
        ],
        compiler_params=pltpu.CompilerParams(
            collective_id=0, has_side_effects=True, vmem_limit_bytes=48 * 1024 * 1024
        ),
        cost_estimate=pl.CostEstimate(flops=80_000_000, bytes_accessed=4_000_000, transcendentals=0),
    )(
        in_hbm(scalars.reshape(2, CELLS, NZ)),
        in_hbm(east_wind.reshape(CELLS, NZ)),
        in_hbm(north_wind.reshape(CELLS, NZ)),
        in_hbm(up_wind.reshape(CELLS, NZ)),
        in_hbm(diffusivity.reshape(CELLS, NZ)),
        in_hbm(target_profile),
    )
    result = pl.pallas_call(
        solve,
        out_shape=jax.ShapeDtypeStruct((2, CELLS, NZ), f32),
        in_specs=[resident] * 5,
        out_specs=hbm,
        scratch_shapes=[
            vmem((2, NZ * 8, 128), f32),
            vmem((2, CELLS, NZ), f32),
            dma((2, TILES)),
        ],
        compiler_params=pltpu.CompilerParams(vmem_limit_bytes=32 * 1024 * 1024),
        cost_estimate=pl.CostEstimate(flops=2_000_000, bytes_accessed=4_000_000, transcendentals=0),
    )(*parts)
    return result.reshape(2, CX, CY, NZ)


def solution(mesh):
    placed = (
        P(None, "gx", "gy", None),
        P("gx", "gy", None),
        P("gx", "gy", None),
        P("gx", "gy", None),
        P("gx", "gy", None),
        P(),
    )
    return jax.shard_map(
        functools.partial(body, mesh.shape["gx"], mesh.shape["gy"]),
        mesh=mesh, in_specs=placed, out_specs=P(None, "gx", "gy", None), check_vma=False,
    )
```

```python
import functools

import jax
import jax.numpy as jnp
from jax import lax
from jax.experimental import pallas as pl
from jax.experimental.pallas import tpu as pltpu
from jax.sharding import PartitionSpec as P

STEP = 0.3
RELAX = 0.5
EPSILON = 1e-06
EPS = 0.75 * EPSILON
EPS2 = EPS * EPS

CX, CY, NZ = 24, 32, 128
H = 3
XROWS = (CX + 2 * H) * CY
YROWS = (CY + 2 * H) * CX
CELLS = CX * CY
TILES = CELLS // 128
GROUP = 4
ZROWS = 192
PART = 24
LEVELS = 6 * PART
UNROLL = PART // 4
PLACES = (0, 1, 3)
MESH = pl.DeviceIdType.MESH


def cell(dm, em, dp, ep):
    g = dp - dm
    b = (g * g + EPS) + ep * dm
    g2 = g + g
    left = b - g2 * em
    right = b + g2 * ep
    return g, left * left, b * b, right * right


def face(u, total, g_low, g_high, t_low, t_mid, t_high, r2, r1, c1, c0, l0, l1):
    pos = u > 0.0
    b0 = jnp.where(pos, r2, l1)
    b1 = jnp.where(pos, c1, c0)
    b2 = jnp.where(pos, l0, r1)
    gs = jnp.where(pos, g_low, g_high)
    ts = jnp.where(pos, t_low, t_high)
    b0 = 3.0 * b0
    c2 = b2 + b2
    num = b1 * (c2 * ts + b0 * t_mid)
    den = b1 * (b2 + b0) + b0 * c2
    part = num * pl.reciprocal(den, approx=True)
    return u * (3.0 * total - gs) - jnp.abs(u) * part


def march(load_f, load_u, first, last):
    f, d, q, t = {}, {}, {}, {}

    def get_f(i):
        if i not in f:
            f[i] = load_f(i)
        return f[i]

    def get_d(i):
        if i not in d:
            diff = get_f(i) - get_f(i - 1)
            d[i] = (diff, 0.75 * diff)
        return d[i]

    def get_q(i):
        if i not in q:
            q[i] = cell(*get_d(i), *get_d(i + 1))
        return q[i]

    def get_t(i):
        if i not in t:
            t[i] = get_q(i)[0] - get_q(i - 1)[0]
        return t[i]

    out = []
    for j in range(first, last + 1):
        lo2, lo1, hi0, hi1 = get_q(j - 2), get_q(j - 1), get_q(j), get_q(j + 1)
        out.append(
            face(
                load_u(j), get_f(j - 1) + get_f(j), lo1[0], hi0[0], get_t(j - 1), get_t(j), get_t(j + 1),
                lo2[3], lo1[3], lo1[2], hi0[2], hi0[1], hi1[1],
            )
        )
    return out


def shifted_z(f, lane):
    below, below2, above = pltpu.roll(f, 1, 1), pltpu.roll(f, 2, 1), pltpu.roll(f, NZ - 1, 1)
    d = jnp.where(lane == 0, 0.0, f - below)
    d_low = jnp.where(lane <= 1, 0.0, below - below2)
    d_high = jnp.where(lane == NZ - 1, 0.0, above - f)
    g, left, mid, right = cell(d, 0.75 * d, d_high, 0.75 * d_high)
    g_low = d - d_low
    t = g - g_low
    return (
        f + below, g_low, g, pltpu.roll(t, 1, 1), t, pltpu.roll(t, NZ - 1, 1), pltpu.roll(right, 2, 1),
        pltpu.roll(right, 1, 1), pltpu.roll(mid, 1, 1), mid, left, pltpu.roll(left, NZ - 1, 1),
    )


def flux_z(u, parts, lane):
    total, g_low, g, t_low, t, t_high, r2, r1, c1, c0, l0, l1 = parts
    u = jnp.where(lane == 0, 0.0, u)
    last = lane == NZ - 1
    t_high = jnp.where(last, -g, t_high)
    r2 = jnp.where(lane == 1, EPS2, r2)
    l1 = jnp.where(last, EPS2, l1)
    return face(u, total, g_low, g, t_low, t, t_high, r2, r1, c1, c0, l0, l1)


def digits(n):
    out, stride = [], 1
    while stride < n:
        radix = min(4, n // stride)
        out.append((stride, radix))
        stride *= radix
    return out


def kernel(
    n_x, n_y,
    scal, east, north, upw, diff, target, adv, shift, im, av, cp,
    xs, bs, ys, zs, fz, fr, tx, ty, ex, ny, nraw, uz, kd, tg, fk, es, aro, ari,
    lsem, hsend, hrecv, wsend, wrecv, asend, arecv,
):
    mx, my = lax.axis_index("gx"), lax.axis_index("gy")
    x_up, x_dn = lax.rem(mx + 1, n_x), lax.rem(mx + n_x - 1, n_x)
    y_up, y_dn = lax.rem(my + 1, n_y), lax.rem(my + n_y - 1, n_y)
    plan = [("x", d) for d in digits(n_x)] + [("y", d) for d in digits(n_y)]
    rounds = len(plan)

    def partner(r, k):
        axis, (stride, radix) = plan[r]
        me = mx if axis == "x" else my
        digit = lax.rem(lax.div(me, stride), radix)
        other = me + stride * (lax.rem(digit + k, radix) - digit)
        return (other, my) if axis == "x" else (mx, other)

    loads = [
        pltpu.make_async_copy(scal.at[0], xs.at[0, 0, pl.ds(H * CY, CELLS)], lsem.at[0]),
        pltpu.make_async_copy(scal.at[1], xs.at[0, 1, pl.ds(H * CY, CELLS)], lsem.at[1]),
        pltpu.make_async_copy(north, nraw, lsem.at[2]),
        pltpu.make_async_copy(east, ex.at[pl.ds(0, CELLS)], lsem.at[3]),
        pltpu.make_async_copy(diff, kd, lsem.at[4]),
        pltpu.make_async_copy(upw, uz, lsem.at[5]),
        pltpu.make_async_copy(target, tg, lsem.at[6]),
        pltpu.make_async_copy(scal, bs, lsem.at[7]),
    ]
    for load in loads:
        load.start()

    barrier = pltpu.get_barrier_semaphore()
    peers = [(x_up, my), (x_dn, my), (mx, y_up), (mx, y_dn)] + [
        partner(r, k) for r in range(rounds) for k in range(1, plan[r][1][1])
    ]
    for peer in peers:
        pl.semaphore_signal(barrier, inc=1, device_id=peer, device_id_type=MESH)

    def halo(t, way):
        st, s = lax.div(t, 2), lax.rem(t, 2)
        size = CY if way < 2 else CX
        buffer, length = (xs, CX) if way < 2 else (ys, CY)
        to = ((x_up, my), (x_dn, my), (mx, y_up), (mx, y_dn))[way]
        source, target_row = ((length, 0), (H, length + H))[way % 2]
        return pltpu.make_async_remote_copy(
            src_ref=buffer.at[st, s, pl.ds(source * size, H * size)],
            dst_ref=buffer.at[st, s, pl.ds(target_row * size, H * size)],
            send_sem=hsend.at[t, way], recv_sem=hrecv.at[t, way], device_id=to, device_id_type=MESH,
        )

    def send_halos(t, ways):
        for way in ways:
            halo(t, way).start()

    def exchange(r):
        return [
            pltpu.make_async_remote_copy(
                src_ref=aro.at[r], dst_ref=ari.at[r, k - 1], send_sem=asend.at[r, k - 1],
                recv_sem=arecv.at[r, k - 1], device_id=partner(r, k), device_id_type=MESH,
            )
            for k in range(1, plan[r][1][1])
        ]

    def send_sums(r):
        for copy in exchange(r):
            copy.start()

    def add_sums(r):
        total = aro[r]
        for k, copy in enumerate(exchange(r)):
            copy.wait_recv()
            total = total + ari[r, k]
        aro[r + 1] = total

    east_edge = pltpu.make_async_remote_copy(
        src_ref=ex.at[pl.ds(0, CY)], dst_ref=ex.at[pl.ds(CELLS, CY)], send_sem=wsend.at[0], recv_sem=wrecv.at[0],
        device_id=(x_dn, my), device_id_type=MESH,
    )
    north_edge = pltpu.make_async_remote_copy(
        src_ref=ny.at[pl.ds(0, CX)], dst_ref=ny.at[pl.ds(CELLS, CX)], send_sem=wsend.at[1], recv_sem=wrecv.at[1],
        device_id=(mx, y_dn), device_id_type=MESH,
    )

    def to_y(st, s, x, value):
        for i in range(CY // 8):
            ys[st, s, pl.ds((H + 8 * i) * CX + x, 8, stride=CX), :] = value[8 * i : 8 * i + 8]

    loads[0].wait()
    loads[1].wait()
    pl.semaphore_wait(barrier, len(peers))

    def first_field(s, _):
        send_halos(s, (0, 1))

        def convert(g, total):
            values = [xs[0, s, pl.ds(pl.multiple_of((H + g * GROUP + p) * CY, CY), CY), :] for p in range(GROUP)]
            for p, value in enumerate(values):
                to_y(0, s, g * GROUP + p, value)
            return total + sum(values)

        total = lax.fori_loop(0, CX // GROUP, convert, jnp.zeros((CY, NZ), jnp.float32))
        aro[0, pl.ds(s, 1), :] = jnp.sum(total, axis=0, keepdims=True)
        send_halos(s, (2, 3))
        return 0

    lax.fori_loop(0, 2, first_field, 0)
    send_sums(0)

    loads[2].wait()

    def turn_north(g, _):
        values = [nraw[pl.ds(pl.multiple_of((g * GROUP + p) * CY, CY), CY), :] for p in range(GROUP)]
        for p, value in enumerate(values):
            for i in range(CY // 8):
                ny[pl.ds(8 * i * CX + g * GROUP + p, 8, stride=CX), :] = value[8 * i : 8 * i + 8]
        return 0

    lax.fori_loop(0, CX // GROUP, turn_north, 0)
    north_edge.start()
    loads[3].wait()

    east_edge.start()
    loads[5].wait()
    lane = lax.broadcasted_iota(jnp.int32, (8, NZ), 1)

    loads[4].wait()
    loads[6].wait()
    loads[7].wait()

    def columns_to_lanes(c, _):
        rows = pl.ds(pl.multiple_of(c * 128, 128), 128)
        fk[pl.ds(c, NZ, stride=8), :] = jnp.transpose(kd[rows, :]) * STEP
        return 0

    fk[...] = jnp.zeros(fk.shape, jnp.float32)
    lax.fori_loop(0, TILES, columns_to_lanes, 0)
    fk[pl.ds(0, 8), :] = jnp.zeros((8, 128), jnp.float32)
    es[...] = jnp.zeros((8, 128), jnp.float32)

    def factor(first, e):
        base = pl.multiple_of(first * 8, 8)
        low = fk[pl.ds(base, 8), :]
        for i in range(UNROLL):
            row = pl.ds(base + 8 * i, 8)
            above = fk[pl.ds(base + 8 * i + 8, 8), :]
            g = 1.0 + low * e
            inverse = pl.reciprocal(g + above, approx=True)
            e = g * inverse
            im[row, :] = inverse
            av[row, :] = low * inverse
            cp[row, :] = above * inverse
            low = above
        return e

    def x_faces(st, s, row, first, last):
        flux = march(
            lambda x: xs[st, s, pl.ds((H + x) * CY + row, 8), :],
            lambda x: ex[pl.ds(x * CY + row, 8), :],
            first, last,
        )
        for x in range(first, last):
            tx[pl.ds(x * CY + row, 8), :] = flux[x - first] - flux[x - first + 1]

    def y_faces(st, s, row, first, last):
        flux = march(
            lambda y: ys[st, s, pl.ds((H + y) * CX + row, 8), :],
            lambda y: ny[pl.ds(y * CX + row, 8), :],
            first, last,
        )
        for y in range(first, last):
            ty[pl.ds(row * CY + y, 8, stride=CY), :] = flux[y - first] - flux[y - first + 1]

    def z_faces(st, s, first):
        for v in range(ZROWS // 8):
            parts = shifted_z(xs[st, s, pl.ds(H * CY + first + 8 * v, 8), :], lane)
            for part in range(12):
                zs[part, 8 * v : 8 * v + 8, :] = parts[part]
        for v in range(ZROWS // 8):
            rows = pl.ds(first + 8 * v, 8)
            flux = flux_z(uz[rows, :], [zs[part, 8 * v : 8 * v + 8, :] for part in range(12)], lane)
            fz[rows, :] = flux
            fr[rows, :] = pltpu.roll(flux, NZ - 1, 1)

    def step(t, _):
        st, s = lax.div(t, 2), lax.rem(t, 2)

        def interior(i, e):
            y_faces(st, s, pl.multiple_of(lax.min(i, CX // 8 - 1) * 8, 8), H, CY - H)
            x_faces(st, s, pl.multiple_of(i * 8, 8), H, CX - H)
            z_faces(st, s, pl.multiple_of(i * ZROWS, 8))
            return factor(t * PART + i * UNROLL, e)

        es[...] = lax.fori_loop(0, CELLS // ZROWS, interior, es[...])
        for r, place in enumerate(PLACES[: rounds - 1]):

            @pl.when(t == place)
            def _(r=r):
                add_sums(r)
                send_sums(r + 1)


        @pl.when(t == 0)
        def _():
            north_edge.wait_recv()
            east_edge.wait_recv()

        for way in range(4):
            halo(t, way).wait_recv()

        def boundary(i, _):
            for k in range(2):
                row = pl.multiple_of(i * 16 + 8 * k, 8)
                x_faces(st, s, row, 0, H)
                x_faces(st, s, row, CX - H, CX)
                row = pl.multiple_of(lax.min(2 * i + k, CX // 8 - 1) * 8, 8)
                y_faces(st, s, row, 0, H)
                y_faces(st, s, row, CY - H, CY)
            return 0

        lax.fori_loop(0, CY // 16, boundary, 0)
        coef = jnp.where(st == 0, STEP / 18.0, jnp.where(st == 1, STEP / 12.0, STEP / 6.0)).astype(jnp.float32)

        def update(g, _):
            rows = pl.ds(pl.multiple_of(g * GROUP * CY, CY), GROUP * CY)
            value = bs[s, rows, :] + coef * (tx[rows, :] + ty[rows, :] + (fz[rows, :] - fr[rows, :]))

            @pl.when(st < 2)
            def _():
                xs[st + 1, s, pl.ds(pl.multiple_of((H + g * GROUP) * CY, CY), GROUP * CY), :] = value
                for p in range(GROUP):
                    to_y(st + 1, s, g * GROUP + p, value[p * CY : (p + 1) * CY])

            @pl.when(st == 2)
            def _():
                adv[s, rows, :] = value

            return 0

        lax.fori_loop(0, CX // GROUP, update, 0)

        @pl.when(st < 2)
        def _():
            send_halos(t + 2, range(4))

        return 0

    lax.fori_loop(0, 6, step, 0)

    add_sums(rounds - 1)
    cells = float(n_x * CX * n_y * CY)
    shift[...] = RELAX * (aro[rounds] * (1.0 / cells) - tg[...])

    def drain(t, _):
        for way in range(4):
            halo(t, way).wait_send()
        return 0

    lax.fori_loop(0, 6, drain, 0)

    for r in range(rounds):
        for copy in exchange(r):
            copy.wait_send()
    east_edge.wait_send()
    north_edge.wait_send()


def solve(adv, shift, im, av, cp, out, rh, ob, osem):
    for s in range(2):
        for c in range(TILES):
            value = adv[s, pl.ds(c * 128, 128), :] - shift[s : s + 1, :]
            rh[s, pl.ds(c, NZ, stride=8), :] = jnp.transpose(value)

    zero = jnp.zeros((8, 128), jnp.float32)

    def forward(k8, carry):
        d0, d1 = carry
        base = pl.multiple_of(k8 * 64, 64)
        rows = [pl.ds(base + 8 * i, 8) for i in range(8)]
        data = [(im[r, :], av[r, :], rh[0, r, :], rh[1, r, :]) for r in rows]
        for i, (inverse, a, r0, r1) in enumerate(data):
            d0 = r0 * inverse + a * d0
            d1 = r1 * inverse + a * d1
            rh[0, rows[i], :] = d0
            rh[1, rows[i], :] = d1
        return d0, d1

    lax.fori_loop(0, NZ // 8, forward, (zero, zero))

    def backward(j8, carry):
        v0, v1 = carry
        base = pl.multiple_of((NZ // 8 - 1 - j8) * 64, 64)
        rows = [pl.ds(base + 56 - 8 * i, 8) for i in range(8)]
        data = [(cp[r, :], rh[0, r, :], rh[1, r, :]) for r in rows]
        for i, (c, r0, r1) in enumerate(data):
            v0 = r0 + c * v0
            v1 = r1 + c * v1
            rh[0, rows[i], :] = v0
            rh[1, rows[i], :] = v1
        return v0, v1

    lax.fori_loop(0, NZ // 8, backward, (zero, zero))
    stores = []
    for s in range(2):
        for c in range(TILES):
            rows = pl.ds(c * 128, 128)
            ob[s, rows, :] = jnp.transpose(rh[s, pl.ds(c, NZ, stride=8), :])
            store = pltpu.make_async_copy(ob.at[s, rows], out.at[s, rows], osem.at[s, c])
            store.start()
            stores.append(store)
    for store in stores:
        store.wait()


def in_hbm(value):
    return pltpu.with_memory_space_constraint(value, pltpu.HBM)


def body(n_x, n_y, scalars, east_wind, north_wind, up_wind, diffusivity, target_profile):
    rounds = len(digits(n_x)) + len(digits(n_y))
    hbm = pl.BlockSpec(memory_space=pltpu.HBM)
    f32 = jnp.float32
    vmem = pltpu.VMEM
    dma = pltpu.SemaphoreType.DMA
    resident = pl.BlockSpec(memory_space=pltpu.VMEM)
    columns = jax.ShapeDtypeStruct((LEVELS * 8, 128), f32)
    parts = pl.pallas_call(
        functools.partial(kernel, n_x, n_y),
        out_shape=[
            jax.ShapeDtypeStruct((2, CELLS, NZ), f32), jax.ShapeDtypeStruct((2, NZ), f32), columns, columns, columns,
        ],
        in_specs=[hbm] * 6,
        out_specs=[resident] * 5,
        scratch_shapes=[
            vmem((3, 2, XROWS, NZ), f32),
            vmem((2, CELLS, NZ), f32),
            vmem((3, 2, YROWS, NZ), f32),
            vmem((12, ZROWS, NZ), f32),
            vmem((CELLS, NZ), f32),
            vmem((CELLS, NZ), f32),
            vmem((CELLS, NZ), f32),
            vmem((CELLS, NZ), f32),
            vmem((CELLS + CY, NZ), f32),
            vmem((CELLS + CX, NZ), f32),
            vmem((CELLS, NZ), f32),
            vmem((CELLS, NZ), f32),
            vmem((CELLS, NZ), f32),
            vmem((2, NZ), f32),
            vmem(((LEVELS + 1) * 8, 128), f32),
            vmem((8, 128), f32),
            vmem((rounds + 1, 2, NZ), f32),
            vmem((rounds, 3, 2, NZ), f32),
            dma((8,)),
            dma((6, 4)),
            dma((6, 4)),
            dma((2,)),
            dma((2,)),
            dma((rounds, 3)),
            dma((rounds, 3)),
        ],
        compiler_params=pltpu.CompilerParams(
            collective_id=0, has_side_effects=True, vmem_limit_bytes=48 * 1024 * 1024
        ),
        cost_estimate=pl.CostEstimate(flops=80_000_000, bytes_accessed=4_000_000, transcendentals=0),
    )(
        in_hbm(scalars.reshape(2, CELLS, NZ)),
        in_hbm(east_wind.reshape(CELLS, NZ)),
        in_hbm(north_wind.reshape(CELLS, NZ)),
        in_hbm(up_wind.reshape(CELLS, NZ)),
        in_hbm(diffusivity.reshape(CELLS, NZ)),
        in_hbm(target_profile),
    )
    result = pl.pallas_call(
        solve,
        out_shape=jax.ShapeDtypeStruct((2, CELLS, NZ), f32),
        in_specs=[resident] * 5,
        out_specs=hbm,
        scratch_shapes=[
            vmem((2, NZ * 8, 128), f32),
            vmem((2, CELLS, NZ), f32),
            dma((2, TILES)),
        ],
        compiler_params=pltpu.CompilerParams(vmem_limit_bytes=32 * 1024 * 1024),
        cost_estimate=pl.CostEstimate(flops=2_000_000, bytes_accessed=4_000_000, transcendentals=0),
    )(*parts)
    return result.reshape(2, CX, CY, NZ)


def solution(mesh):
    placed = (
        P(None, "gx", "gy", None),
        P("gx", "gy", None),
        P("gx", "gy", None),
        P("gx", "gy", None),
        P("gx", "gy", None),
        P(),
    )
    return jax.shard_map(
        functools.partial(body, mesh.shape["gx"], mesh.shape["gy"]),
        mesh=mesh, in_specs=placed, out_specs=P(None, "gx", "gy", None), check_vma=False,
    )
```

```python
import functools

import jax
import jax.numpy as jnp
from jax import lax
from jax.experimental import pallas as pl
from jax.experimental.pallas import tpu as pltpu
from jax.sharding import PartitionSpec as P

STEP = 0.3
RELAX = 0.5
EPSILON = 1e-06
EPS = 0.75 * EPSILON
EPS2 = EPS * EPS

CX, CY, NZ = 24, 32, 128
H = 3
XROWS = (CX + 2 * H) * CY
YROWS = (CY + 2 * H) * CX
CELLS = CX * CY
TILES = CELLS // 128
GROUP = 8
ZROWS = 192
PART = 24
LEVELS = 6 * PART
UNROLL = PART // 4
PLACES = (0, 1, 3)
MESH = pl.DeviceIdType.MESH


def cell(dm, em, dp, ep):
    g = dp - dm
    b = (g * g + EPS) + ep * dm
    g2 = g + g
    left = b - g2 * em
    right = b + g2 * ep
    return g, left * left, b * b, right * right


def face(u, total, g_low, g_high, t_low, t_mid, t_high, r2, r1, c1, c0, l0, l1):
    pos = u > 0.0
    b0 = jnp.where(pos, r2, l1)
    b1 = jnp.where(pos, c1, c0)
    b2 = jnp.where(pos, l0, r1)
    gs = jnp.where(pos, g_low, g_high)
    ts = jnp.where(pos, t_low, t_high)
    b0 = 3.0 * b0
    c2 = b2 + b2
    num = b1 * (c2 * ts + b0 * t_mid)
    den = b1 * (b2 + b0) + b0 * c2
    part = num * pl.reciprocal(den, approx=True)
    return u * (3.0 * total - gs) - jnp.abs(u) * part


def march(load_f, load_u, first, last):
    f, d, q, t = {}, {}, {}, {}

    def get_f(i):
        if i not in f:
            f[i] = load_f(i)
        return f[i]

    def get_d(i):
        if i not in d:
            diff = get_f(i) - get_f(i - 1)
            d[i] = (diff, 0.75 * diff)
        return d[i]

    def get_q(i):
        if i not in q:
            q[i] = cell(*get_d(i), *get_d(i + 1))
        return q[i]

    def get_t(i):
        if i not in t:
            t[i] = get_q(i)[0] - get_q(i - 1)[0]
        return t[i]

    out = []
    for j in range(first, last + 1):
        lo2, lo1, hi0, hi1 = get_q(j - 2), get_q(j - 1), get_q(j), get_q(j + 1)
        out.append(
            face(
                load_u(j), get_f(j - 1) + get_f(j), lo1[0], hi0[0], get_t(j - 1), get_t(j), get_t(j + 1),
                lo2[3], lo1[3], lo1[2], hi0[2], hi0[1], hi1[1],
            )
        )
    return out


def joined(flux, part, edge, row):
    rows = pl.ds(row, 8)
    if part == 0:
        return flux + [edge[0, rows, :]]
    if part == 2:
        return [edge[1, rows, :]] + flux
    edge[0, rows, :] = flux[0]
    edge[1, rows, :] = flux[-1]
    return flux


def shifted_z(f, lane):
    below = pltpu.roll(f, 1, 1)
    d = jnp.where(lane == 0, 0.0, f - below)
    return (
        f + below, d, jnp.where(lane == 1, 0.0, pltpu.roll(d, 2, 1)), pltpu.roll(d, 1, 1), pltpu.roll(d, NZ - 1, 1),
        jnp.where(lane == NZ - 1, 0.0, pltpu.roll(d, NZ - 2, 1)),
    )


def flux_z(u, parts, lane):
    total, d3, low2, low1, high1, high2 = parts
    u = jnp.where(lane == 0, 0.0, u)
    pos = u > 0.0
    d1 = jnp.where(pos, low2, high2)
    d2 = jnp.where(pos, low1, high1)
    d4 = jnp.where(pos, high1, low1)
    g0, g1, g2 = d2 - d1, d3 - d2, d4 - d3
    e2, e3 = 0.75 * d2, 0.75 * d3
    b0 = (g0 * g0 + EPS) + e2 * (d2 + g0)
    b1 = (g1 * g1 + EPS) + e3 * d2
    b2 = (g2 * g2 + EPS) + e3 * (d3 - g2)
    b0 = 3.0 * (b0 * b0)
    b1 = b1 * b1
    b2 = b2 * b2
    c2 = b2 + b2
    num = b1 * (c2 * (g1 - g0) + b0 * (g2 - g1))
    den = b1 * (b2 + b0) + b0 * c2
    return u * (3.0 * total) - jnp.abs(u) * (g1 + num * pl.reciprocal(den, approx=True))


def digits(n):
    out, stride = [], 1
    while stride < n:
        radix = min(4, n // stride)
        out.append((stride, radix))
        stride *= radix
    return out


def kernel(
    n_x, n_y,
    scal, east, north, upw, diff, target, adv, shift, im, av, cp,
    xs, bs, ys, edge, tz, tx, ty, ex, ny, nraw, uz, kd, tg, fk, es, aro, ari,
    lsem, hsend, hrecv, wsend, wrecv, asend, arecv,
):
    mx, my = lax.axis_index("gx"), lax.axis_index("gy")
    x_up, x_dn = lax.rem(mx + 1, n_x), lax.rem(mx + n_x - 1, n_x)
    y_up, y_dn = lax.rem(my + 1, n_y), lax.rem(my + n_y - 1, n_y)
    plan = [("x", d) for d in digits(n_x)] + [("y", d) for d in digits(n_y)]
    rounds = len(plan)

    def partner(r, k):
        axis, (stride, radix) = plan[r]
        me = mx if axis == "x" else my
        digit = lax.rem(lax.div(me, stride), radix)
        other = me + stride * (lax.rem(digit + k, radix) - digit)
        return (other, my) if axis == "x" else (mx, other)

    loads = [
        pltpu.make_async_copy(scal.at[0], xs.at[0, 0, pl.ds(H * CY, CELLS)], lsem.at[0]),
        pltpu.make_async_copy(scal.at[1], xs.at[0, 1, pl.ds(H * CY, CELLS)], lsem.at[1]),
        pltpu.make_async_copy(north, nraw, lsem.at[2]),
        pltpu.make_async_copy(east, ex.at[pl.ds(0, CELLS)], lsem.at[3]),
        pltpu.make_async_copy(diff, kd, lsem.at[4]),
        pltpu.make_async_copy(upw, uz, lsem.at[5]),
        pltpu.make_async_copy(target, tg, lsem.at[6]),
        pltpu.make_async_copy(scal, bs, lsem.at[7]),
    ]
    for load in loads:
        load.start()

    barrier = pltpu.get_barrier_semaphore()
    peers = [(x_up, my), (x_dn, my), (mx, y_up), (mx, y_dn)] + [
        partner(r, k) for r in range(rounds) for k in range(1, plan[r][1][1])
    ]
    for peer in peers:
        pl.semaphore_signal(barrier, inc=1, device_id=peer, device_id_type=MESH)

    def halo(t, way):
        st, s = lax.div(t, 2), lax.rem(t, 2)
        size = CY if way < 2 else CX
        buffer, length = (xs, CX) if way < 2 else (ys, CY)
        to = ((x_up, my), (x_dn, my), (mx, y_up), (mx, y_dn))[way]
        source, target_row = ((length, 0), (H, length + H))[way % 2]
        return pltpu.make_async_remote_copy(
            src_ref=buffer.at[st, s, pl.ds(source * size, H * size)],
            dst_ref=buffer.at[st, s, pl.ds(target_row * size, H * size)],
            send_sem=hsend.at[t, way], recv_sem=hrecv.at[t, way], device_id=to, device_id_type=MESH,
        )

    def send_halos(t, ways):
        for way in ways:
            halo(t, way).start()

    def exchange(r):
        return [
            pltpu.make_async_remote_copy(
                src_ref=aro.at[r], dst_ref=ari.at[r, k - 1], send_sem=asend.at[r, k - 1],
                recv_sem=arecv.at[r, k - 1], device_id=partner(r, k), device_id_type=MESH,
            )
            for k in range(1, plan[r][1][1])
        ]

    def send_sums(r):
        for copy in exchange(r):
            copy.start()

    def add_sums(r):
        total = aro[r]
        for k, copy in enumerate(exchange(r)):
            copy.wait_recv()
            total = total + ari[r, k]
        aro[r + 1] = total

    east_edge = pltpu.make_async_remote_copy(
        src_ref=ex.at[pl.ds(0, CY)], dst_ref=ex.at[pl.ds(CELLS, CY)], send_sem=wsend.at[0], recv_sem=wrecv.at[0],
        device_id=(x_dn, my), device_id_type=MESH,
    )
    north_edge = pltpu.make_async_remote_copy(
        src_ref=ny.at[pl.ds(0, CX)], dst_ref=ny.at[pl.ds(CELLS, CX)], send_sem=wsend.at[1], recv_sem=wrecv.at[1],
        device_id=(mx, y_dn), device_id_type=MESH,
    )

    def to_y(st, s, x, value):
        for i in range(CY // 8):
            ys[st, s, pl.ds((H + 8 * i) * CX + x, 8, stride=CX), :] = value[8 * i : 8 * i + 8]

    loads[0].wait()
    loads[1].wait()
    pl.semaphore_wait(barrier, len(peers))

    def first_field(s, _):
        send_halos(s, (0, 1))

        def convert(g, total):
            values = [xs[0, s, pl.ds(pl.multiple_of((H + g * GROUP + p) * CY, CY), CY), :] for p in range(GROUP)]
            for p, value in enumerate(values):
                to_y(0, s, g * GROUP + p, value)
            return total + sum(values)

        total = lax.fori_loop(0, CX // GROUP, convert, jnp.zeros((CY, NZ), jnp.float32))
        aro[0, pl.ds(s, 1), :] = jnp.sum(total, axis=0, keepdims=True)
        send_halos(s, (2, 3))
        return 0

    lax.fori_loop(0, 2, first_field, 0)
    send_sums(0)

    loads[2].wait()

    def turn_north(g, _):
        values = [nraw[pl.ds(pl.multiple_of((g * GROUP + p) * CY, CY), CY), :] for p in range(GROUP)]
        for p, value in enumerate(values):
            for i in range(CY // 8):
                ny[pl.ds(8 * i * CX + g * GROUP + p, 8, stride=CX), :] = value[8 * i : 8 * i + 8]
        return 0

    lax.fori_loop(0, CX // GROUP, turn_north, 0)
    north_edge.start()
    loads[3].wait()

    east_edge.start()
    loads[5].wait()
    lane = lax.broadcasted_iota(jnp.int32, (8, NZ), 1)

    loads[4].wait()
    loads[6].wait()
    loads[7].wait()

    def columns_to_lanes(c, _):
        rows = pl.ds(pl.multiple_of(c * 128, 128), 128)
        fk[pl.ds(c, NZ, stride=8), :] = jnp.transpose(kd[rows, :]) * STEP
        return 0

    fk[...] = jnp.zeros(fk.shape, jnp.float32)
    lax.fori_loop(0, TILES, columns_to_lanes, 0)
    fk[pl.ds(0, 8), :] = jnp.zeros((8, 128), jnp.float32)
    es[...] = jnp.zeros((8, 128), jnp.float32)

    def factor(first, e):
        base = pl.multiple_of(first * 8, 8)
        low = fk[pl.ds(base, 8), :]
        for i in range(UNROLL):
            row = pl.ds(base + 8 * i, 8)
            above = fk[pl.ds(base + 8 * i + 8, 8), :]
            g = 1.0 + low * e
            inverse = pl.reciprocal(g + above, approx=True)
            e = g * inverse
            im[row, :] = inverse
            av[row, :] = low * inverse
            cp[row, :] = above * inverse
            low = above
        return e

    def x_faces(st, s, row, part):
        first, last = ((0, H), (H, CX - H), (CX - H, CX))[part]
        flux = march(
            lambda x: xs[st, s, pl.ds((H + x) * CY + row, 8), :],
            lambda x: ex[pl.ds(x * CY + row, 8), :],
            first + (part == 2), last - (part == 0),
        )
        flux = joined(flux, part, edge, row)
        for x in range(first, last):
            tx[pl.ds(x * CY + row, 8), :] = flux[x - first] - flux[x - first + 1]

    def y_faces(st, s, row, part):
        first, last = ((0, H), (H, CY - H), (CY - H, CY))[part]
        flux = march(
            lambda y: ys[st, s, pl.ds((H + y) * CX + row, 8), :],
            lambda y: ny[pl.ds(y * CX + row, 8), :],
            first + (part == 2), last - (part == 0),
        )
        flux = joined(flux, part, edge, CY + row)
        for y in range(first, last):
            ty[pl.ds(row * CY + y, 8, stride=CY), :] = flux[y - first] - flux[y - first + 1]

    def z_faces(st, s):
        def group(i, _):
            first = pl.multiple_of(i * ZROWS, ZROWS)
            rows = [pl.ds(first + 8 * v, 8) for v in range(ZROWS // 8)]
            parts = [shifted_z(xs[st, s, pl.ds(H * CY + first + 8 * v, 8), :], lane) for v in range(ZROWS // 8)]
            flux = [flux_z(uz[r, :], part, lane) for r, part in zip(rows, parts)]
            for r, value in zip(rows, flux):
                tz[r, :] = value - pltpu.roll(value, NZ - 1, 1)
            return 0

        lax.fori_loop(0, CELLS // ZROWS, group, 0)

    def step(t, _):
        st, s = lax.div(t, 2), lax.rem(t, 2)

        def y_inner(i, _):
            y_faces(st, s, pl.multiple_of(i * 8, 8), 1)
            return 0

        lax.fori_loop(0, CX // 8, y_inner, 0)

        def x_inner(i, e):
            x_faces(st, s, pl.multiple_of(i * 8, 8), 1)
            return factor(t * PART + i * UNROLL, e)

        es[...] = lax.fori_loop(0, CY // 8, x_inner, es[...])
        z_faces(st, s)
        for r, place in enumerate(PLACES[: rounds - 1]):

            @pl.when(t == place)
            def _(r=r):
                add_sums(r)
                send_sums(r + 1)


        @pl.when(t == 0)
        def _():
            north_edge.wait_recv()
            east_edge.wait_recv()

        halo(t, 2).wait_recv()
        halo(t, 3).wait_recv()
        for row in range(0, CX, 8):
            y_faces(st, s, row, 0)
            y_faces(st, s, row, 2)
        halo(t, 0).wait_recv()
        halo(t, 1).wait_recv()

        def x_outer(i, _):
            for k in range(2):
                x_faces(st, s, pl.multiple_of(i * 16 + 8 * k, 8), 0)
                x_faces(st, s, pl.multiple_of(i * 16 + 8 * k, 8), 2)
            return 0

        lax.fori_loop(0, CY // 16, x_outer, 0)
        coef = jnp.where(st == 0, STEP / 18.0, jnp.where(st == 1, STEP / 12.0, STEP / 6.0)).astype(jnp.float32)

        def update(g, _):
            rows = pl.ds(pl.multiple_of(g * GROUP * CY, CY), GROUP * CY)
            value = bs[s, rows, :] + coef * (tx[rows, :] + ty[rows, :] + tz[rows, :])

            @pl.when(st < 2)
            def _():
                xs[st + 1, s, pl.ds(pl.multiple_of((H + g * GROUP) * CY, CY), GROUP * CY), :] = value
                for p in range(GROUP):
                    to_y(st + 1, s, g * GROUP + p, value[p * CY : (p + 1) * CY])

            @pl.when(st == 2)
            def _():
                adv[s, rows, :] = value

            return 0

        lax.fori_loop(0, CX // GROUP, update, 0)

        @pl.when(st < 2)
        def _():
            send_halos(t + 2, range(4))

        return 0

    lax.fori_loop(0, 6, step, 0)

    add_sums(rounds - 1)
    cells = float(n_x * CX * n_y * CY)
    shift[...] = RELAX * (aro[rounds] * (1.0 / cells) - tg[...])

    def drain(t, _):
        for way in range(4):
            halo(t, way).wait_send()
        return 0

    lax.fori_loop(0, 6, drain, 0)

    for r in range(rounds):
        for copy in exchange(r):
            copy.wait_send()
    east_edge.wait_send()
    north_edge.wait_send()


def solve(adv, shift, im, av, cp, out, rh, ob, osem):
    for s in range(2):
        for c in range(TILES):
            value = adv[s, pl.ds(c * 128, 128), :] - shift[s : s + 1, :]
            rh[s, pl.ds(c, NZ, stride=8), :] = jnp.transpose(value)

    zero = jnp.zeros((8, 128), jnp.float32)

    def forward(k8, carry):
        d0, d1 = carry
        base = pl.multiple_of(k8 * 64, 64)
        rows = [pl.ds(base + 8 * i, 8) for i in range(8)]
        data = [(im[r, :], av[r, :], rh[0, r, :], rh[1, r, :]) for r in rows]
        for i, (inverse, a, r0, r1) in enumerate(data):
            d0 = r0 * inverse + a * d0
            d1 = r1 * inverse + a * d1
            rh[0, rows[i], :] = d0
            rh[1, rows[i], :] = d1
        return d0, d1

    lax.fori_loop(0, NZ // 8, forward, (zero, zero))

    def backward(j8, carry):
        v0, v1 = carry
        base = pl.multiple_of((NZ // 8 - 1 - j8) * 64, 64)
        rows = [pl.ds(base + 56 - 8 * i, 8) for i in range(8)]
        data = [(cp[r, :], rh[0, r, :], rh[1, r, :]) for r in rows]
        for i, (c, r0, r1) in enumerate(data):
            v0 = r0 + c * v0
            v1 = r1 + c * v1
            rh[0, rows[i], :] = v0
            rh[1, rows[i], :] = v1
        return v0, v1

    lax.fori_loop(0, NZ // 8, backward, (zero, zero))
    stores = []
    for s in range(2):
        for c in range(TILES):
            rows = pl.ds(c * 128, 128)
            ob[s, rows, :] = jnp.transpose(rh[s, pl.ds(c, NZ, stride=8), :])
            store = pltpu.make_async_copy(ob.at[s, rows], out.at[s, rows], osem.at[s, c])
            store.start()
            stores.append(store)
    for store in stores:
        store.wait()


def in_hbm(value):
    return pltpu.with_memory_space_constraint(value, pltpu.HBM)


def body(n_x, n_y, scalars, east_wind, north_wind, up_wind, diffusivity, target_profile):
    rounds = len(digits(n_x)) + len(digits(n_y))
    hbm = pl.BlockSpec(memory_space=pltpu.HBM)
    f32 = jnp.float32
    vmem = pltpu.VMEM
    dma = pltpu.SemaphoreType.DMA
    resident = pl.BlockSpec(memory_space=pltpu.VMEM)
    columns = jax.ShapeDtypeStruct((LEVELS * 8, 128), f32)
    parts = pl.pallas_call(
        functools.partial(kernel, n_x, n_y),
        out_shape=[
            jax.ShapeDtypeStruct((2, CELLS, NZ), f32), jax.ShapeDtypeStruct((2, NZ), f32), columns, columns, columns,
        ],
        in_specs=[hbm] * 6,
        out_specs=[resident] * 5,
        scratch_shapes=[
            vmem((3, 2, XROWS, NZ), f32),
            vmem((2, CELLS, NZ), f32),
            vmem((3, 2, YROWS, NZ), f32),
            vmem((2, CY + CX, NZ), f32),
            vmem((CELLS, NZ), f32),
            vmem((CELLS, NZ), f32),
            vmem((CELLS, NZ), f32),
            vmem((CELLS + CY, NZ), f32),
            vmem((CELLS + CX, NZ), f32),
            vmem((CELLS, NZ), f32),
            vmem((CELLS, NZ), f32),
            vmem((CELLS, NZ), f32),
            vmem((2, NZ), f32),
            vmem(((LEVELS + 1) * 8, 128), f32),
            vmem((8, 128), f32),
            vmem((rounds + 1, 2, NZ), f32),
            vmem((rounds, 3, 2, NZ), f32),
            dma((8,)),
            dma((6, 4)),
            dma((6, 4)),
            dma((2,)),
            dma((2,)),
            dma((rounds, 3)),
            dma((rounds, 3)),
        ],
        compiler_params=pltpu.CompilerParams(
            collective_id=0, has_side_effects=True, vmem_limit_bytes=48 * 1024 * 1024
        ),
        cost_estimate=pl.CostEstimate(flops=80_000_000, bytes_accessed=4_000_000, transcendentals=0),
    )(
        in_hbm(scalars.reshape(2, CELLS, NZ)),
        in_hbm(east_wind.reshape(CELLS, NZ)),
        in_hbm(north_wind.reshape(CELLS, NZ)),
        in_hbm(up_wind.reshape(CELLS, NZ)),
        in_hbm(diffusivity.reshape(CELLS, NZ)),
        in_hbm(target_profile),
    )
    result = pl.pallas_call(
        solve,
        out_shape=jax.ShapeDtypeStruct((2, CELLS, NZ), f32),
        in_specs=[resident] * 5,
        out_specs=hbm,
        scratch_shapes=[
            vmem((2, NZ * 8, 128), f32),
            vmem((2, CELLS, NZ), f32),
            dma((2, TILES)),
        ],
        compiler_params=pltpu.CompilerParams(vmem_limit_bytes=32 * 1024 * 1024),
        cost_estimate=pl.CostEstimate(flops=2_000_000, bytes_accessed=4_000_000, transcendentals=0),
    )(*parts)
    return result.reshape(2, CX, CY, NZ)


def solution(mesh):
    placed = (
        P(None, "gx", "gy", None),
        P("gx", "gy", None),
        P("gx", "gy", None),
        P("gx", "gy", None),
        P("gx", "gy", None),
        P(),
    )
    return jax.shard_map(
        functools.partial(body, mesh.shape["gx"], mesh.shape["gy"]),
        mesh=mesh, in_specs=placed, out_specs=P(None, "gx", "gy", None), check_vma=False,
    )
```

```python
import functools

import jax
import jax.numpy as jnp
from jax import lax
from jax.experimental import pallas as pl
from jax.experimental.pallas import tpu as pltpu
from jax.sharding import PartitionSpec as P

STEP = 0.3
RELAX = 0.5
EPSILON = 1e-06
EPS = 0.75 * EPSILON
EPS2 = EPS * EPS

CX, CY, NZ = 24, 32, 128
H = 3
HALF = H * 32 // 2
XROWS = (CX + 2 * H) * CY
YROWS = (CY + 2 * H) * CX
CELLS = CX * CY
TILES = CELLS // 128
GROUP = 8
ZROWS = 192
PART = 24
LEVELS = 6 * PART
UNROLL = PART // 4
PLACES = (0, 2, 4)
MESH = pl.DeviceIdType.MESH


def cell(dm, em, dp, ep):
    g = dp - dm
    b = (g * g + EPS) + ep * dm
    g2 = g + g
    left = b - g2 * em
    right = b + g2 * ep
    return g, left * left, b * b, right * right


def face(u, total, g_low, g_high, t_low, t_mid, t_high, r2, r1, c1, c0, l0, l1):
    pos = u > 0.0
    b0 = jnp.where(pos, r2, l1)
    b1 = jnp.where(pos, c1, c0)
    b2 = jnp.where(pos, l0, r1)
    gs = jnp.where(pos, g_low, g_high)
    ts = jnp.where(pos, t_low, t_high)
    b0 = 3.0 * b0
    c2 = b2 + b2
    num = b1 * (c2 * ts + b0 * t_mid)
    den = b1 * (b2 + b0) + b0 * c2
    part = num * pl.reciprocal(den, approx=True)
    return u * (3.0 * total - gs) - jnp.abs(u) * part


def march(load_f, load_u, first, last):
    f, d, q, t = {}, {}, {}, {}

    def get_f(i):
        if i not in f:
            f[i] = load_f(i)
        return f[i]

    def get_d(i):
        if i not in d:
            diff = get_f(i) - get_f(i - 1)
            d[i] = (diff, 0.75 * diff)
        return d[i]

    def get_q(i):
        if i not in q:
            q[i] = cell(*get_d(i), *get_d(i + 1))
        return q[i]

    def get_t(i):
        if i not in t:
            t[i] = get_q(i)[0] - get_q(i - 1)[0]
        return t[i]

    out = []
    for j in range(first, last + 1):
        lo2, lo1, hi0, hi1 = get_q(j - 2), get_q(j - 1), get_q(j), get_q(j + 1)
        out.append(
            face(
                load_u(j), get_f(j - 1) + get_f(j), lo1[0], hi0[0], get_t(j - 1), get_t(j), get_t(j + 1),
                lo2[3], lo1[3], lo1[2], hi0[2], hi0[1], hi1[1],
            )
        )
    return out


def joined(flux, part, edge, row):
    rows = pl.ds(row, 8)
    if part == 0:
        return flux + [edge[0, rows, :]]
    if part == 2:
        return [edge[1, rows, :]] + flux
    edge[0, rows, :] = flux[0]
    edge[1, rows, :] = flux[-1]
    return flux


def shifted_z(f, lane):
    below = pltpu.roll(f, 1, 1)
    d = jnp.where(lane == 0, 0.0, f - below)
    return (
        f + below, d, jnp.where(lane == 1, 0.0, pltpu.roll(d, 2, 1)), pltpu.roll(d, 1, 1), pltpu.roll(d, NZ - 1, 1),
        jnp.where(lane == NZ - 1, 0.0, pltpu.roll(d, NZ - 2, 1)),
    )


def flux_z(u, parts, lane):
    total, d3, low2, low1, high1, high2 = parts
    u = jnp.where(lane == 0, 0.0, u)
    pos = u > 0.0
    d1 = jnp.where(pos, low2, high2)
    d2 = jnp.where(pos, low1, high1)
    d4 = jnp.where(pos, high1, low1)
    g0, g1, g2 = d2 - d1, d3 - d2, d4 - d3
    e2, e3 = 0.75 * d2, 0.75 * d3
    b0 = (g0 * g0 + EPS) + e2 * (d2 + g0)
    b1 = (g1 * g1 + EPS) + e3 * d2
    b2 = (g2 * g2 + EPS) + e3 * (d3 - g2)
    b0 = 3.0 * (b0 * b0)
    b1 = b1 * b1
    b2 = b2 * b2
    c2 = b2 + b2
    num = b1 * (c2 * (g1 - g0) + b0 * (g2 - g1))
    den = b1 * (b2 + b0) + b0 * c2
    return u * (3.0 * total) - jnp.abs(u) * (g1 + num * pl.reciprocal(den, approx=True))


def digits(n):
    out, stride = [], 1
    while stride < n:
        radix = min(4, n // stride)
        out.append((stride, radix))
        stride *= radix
    return out


def kernel(
    n_x, n_y,
    scal, east, north, upw, diff, target, adv, shift, im, av, cp,
    xs, bs, ys, edge, tz, tx, ty, ex, ny, nraw, uz, kd, tg, fk, es, aro, ari, held,
    lsem, hsend, hrecv, nsend, nrecv, fsend, frecv, gsend, grecv, wsend, wrecv, asend, arecv,
):
    mx, my = lax.axis_index("gx"), lax.axis_index("gy")
    x_up, x_dn = lax.rem(mx + 1, n_x), lax.rem(mx + n_x - 1, n_x)
    y_up, y_dn = lax.rem(my + 1, n_y), lax.rem(my + n_y - 1, n_y)
    plan = [("x", d) for d in digits(n_x)] + [("y", d) for d in digits(n_y)]
    rounds = len(plan)
    core = lax.rem(mx, 2)
    my_side = my + 1 - 2 * lax.rem(my, 2)
    flip = mx + 2 - 4 * lax.rem(lax.div(mx, 2), 2)

    def far(index):
        return lax.rem(index + 2 * core - 1 + n_x, n_x)

    near, beyond = mx + 1 - 2 * core, far(mx)
    flip_back = beyond + 2 - 4 * lax.rem(lax.div(beyond, 2), 2)

    def partner(r, k):
        axis, (stride, radix) = plan[r]
        me = mx if axis == "x" else my
        digit = lax.rem(lax.div(me, stride), radix)
        other = me + stride * (lax.rem(digit + k, radix) - digit)
        return (other, my) if axis == "x" else (mx, other)

    loads = [
        pltpu.make_async_copy(scal.at[0], xs.at[0, 0, pl.ds(H * CY, CELLS)], lsem.at[0]),
        pltpu.make_async_copy(scal.at[1], xs.at[0, 1, pl.ds(H * CY, CELLS)], lsem.at[1]),
        pltpu.make_async_copy(north, nraw, lsem.at[2]),
        pltpu.make_async_copy(east, ex.at[pl.ds(0, CELLS)], lsem.at[3]),
        pltpu.make_async_copy(diff, kd, lsem.at[4]),
        pltpu.make_async_copy(upw, uz, lsem.at[5]),
        pltpu.make_async_copy(target, tg, lsem.at[6]),
        pltpu.make_async_copy(scal, bs, lsem.at[7]),
    ]
    for load in loads:
        load.start()

    barrier = pltpu.get_barrier_semaphore()
    sums = [partner(r, k) for r in range(rounds) for k in range(1, plan[r][1][1])]
    both = [(near, my), (mx, my_side), (flip, my_side), (beyond, my_side), (mx, y_up), (mx, y_dn)] + sums
    sources = both + [(x_up, my), (flip_back, my_side)]
    targets = both + [(x_dn, my), (far(flip), my_side)]
    for source in sources:
        pl.semaphore_signal(barrier, inc=1, device_id=source, device_id_type=MESH)

    def remote(src, dst, send, recv, to):
        return pltpu.make_async_remote_copy(
            src_ref=src, dst_ref=dst, send_sem=send, recv_sem=recv, device_id=to, device_id_type=MESH
        )

    def x_rows(t, plane, first, count):
        row = pl.multiple_of(plane * CY + first, 8)
        return xs.at[lax.div(t, 2), lax.rem(t, 2), pl.ds(row, count)]

    def x_near(t):
        src = x_rows(t, H + (1 - core) * (CX - H), 0, H * CY)
        return remote(src, x_rows(t, core * (CX + H), 0, H * CY), nsend.at[t], nrecv.at[t], (near, my))

    def x_first(t, half):
        src = x_rows(t, H + core * (CX - H), half * HALF, HALF)
        to = ((mx, my_side), (flip, my_side))[half]
        return remote(src, held.at[t, half], fsend.at[t, half], frecv.at[t, half], to)

    def x_second(t, half):
        dst = x_rows(t, (1 - core) * (CX + H), half * HALF, HALF)
        to = ((beyond, my_side), (far(flip), my_side))[half]
        return remote(held.at[t, half], dst, gsend.at[t, half], grecv.at[t, half], to)

    def y_halo(t, way):
        st, s = lax.div(t, 2), lax.rem(t, 2)
        source, target_row = ((CY, 0), (H, CY + H))[way]
        return remote(
            ys.at[st, s, pl.ds(source * CX, H * CX)], ys.at[st, s, pl.ds(target_row * CX, H * CX)],
            hsend.at[t, way], hrecv.at[t, way], (mx, (y_up, y_dn)[way]),
        )

    def send_x(t):
        x_first(t, 0).start()
        x_first(t, 1).start()
        x_near(t).start()

    def send_y(t):
        y_halo(t, 0).start()
        y_halo(t, 1).start()

    def forward(t):
        for half in range(2):
            x_first(t, half).wait_recv()
            x_second(t, half).start()

    def exchange(r):
        return [
            pltpu.make_async_remote_copy(
                src_ref=aro.at[r], dst_ref=ari.at[r, k - 1], send_sem=asend.at[r, k - 1],
                recv_sem=arecv.at[r, k - 1], device_id=partner(r, k), device_id_type=MESH,
            )
            for k in range(1, plan[r][1][1])
        ]

    def send_sums(r):
        for copy in exchange(r):
            copy.start()

    def add_sums(r):
        total = aro[r]
        for k, copy in enumerate(exchange(r)):
            copy.wait_recv()
            total = total + ari[r, k]
        aro[r + 1] = total

    east_edge = pltpu.make_async_remote_copy(
        src_ref=ex.at[pl.ds(0, CY)], dst_ref=ex.at[pl.ds(CELLS, CY)], send_sem=wsend.at[0], recv_sem=wrecv.at[0],
        device_id=(x_dn, my), device_id_type=MESH,
    )
    north_edge = pltpu.make_async_remote_copy(
        src_ref=ny.at[pl.ds(0, CX)], dst_ref=ny.at[pl.ds(CELLS, CX)], send_sem=wsend.at[1], recv_sem=wrecv.at[1],
        device_id=(mx, y_dn), device_id_type=MESH,
    )

    def to_y(st, s, x, value):
        for i in range(CY // 8):
            ys[st, s, pl.ds((H + 8 * i) * CX + x, 8, stride=CX), :] = value[8 * i : 8 * i + 8]

    loads[0].wait()
    loads[1].wait()
    pl.semaphore_wait(barrier, len(targets))

    def first_field(s, _):
        send_x(s)

        def convert(g, total):
            values = [xs[0, s, pl.ds(pl.multiple_of((H + g * GROUP + p) * CY, CY), CY), :] for p in range(GROUP)]
            for p, value in enumerate(values):
                to_y(0, s, g * GROUP + p, value)
            return total + sum(values)

        total = lax.fori_loop(0, CX // GROUP, convert, jnp.zeros((CY, NZ), jnp.float32))
        aro[0, pl.ds(s, 1), :] = jnp.sum(total, axis=0, keepdims=True)
        send_y(s)
        return 0

    lax.fori_loop(0, 2, first_field, 0)
    send_sums(0)

    loads[2].wait()

    def turn_north(g, _):
        values = [nraw[pl.ds(pl.multiple_of((g * GROUP + p) * CY, CY), CY), :] for p in range(GROUP)]
        for p, value in enumerate(values):
            for i in range(CY // 8):
                ny[pl.ds(8 * i * CX + g * GROUP + p, 8, stride=CX), :] = value[8 * i : 8 * i + 8]
        return 0

    lax.fori_loop(0, CX // GROUP, turn_north, 0)
    north_edge.start()
    loads[3].wait()

    east_edge.start()
    loads[5].wait()
    lane = lax.broadcasted_iota(jnp.int32, (8, NZ), 1)

    loads[4].wait()
    loads[6].wait()
    loads[7].wait()

    def columns_to_lanes(c, _):
        rows = pl.ds(pl.multiple_of(c * 128, 128), 128)
        fk[pl.ds(c, NZ, stride=8), :] = jnp.transpose(kd[rows, :]) * STEP
        return 0

    fk[...] = jnp.zeros(fk.shape, jnp.float32)
    lax.fori_loop(0, TILES, columns_to_lanes, 0)
    fk[pl.ds(0, 8), :] = jnp.zeros((8, 128), jnp.float32)
    es[...] = jnp.zeros((8, 128), jnp.float32)

    def factor(first, e):
        base = pl.multiple_of(first * 8, 8)
        low = fk[pl.ds(base, 8), :]
        for i in range(UNROLL):
            row = pl.ds(base + 8 * i, 8)
            above = fk[pl.ds(base + 8 * i + 8, 8), :]
            g = 1.0 + low * e
            inverse = pl.reciprocal(g + above, approx=True)
            e = g * inverse
            im[row, :] = inverse
            av[row, :] = low * inverse
            cp[row, :] = above * inverse
            low = above
        return e

    def x_faces(st, s, row, part):
        first, last = ((0, H), (H, CX - H), (CX - H, CX))[part]
        flux = march(
            lambda x: xs[st, s, pl.ds((H + x) * CY + row, 8), :],
            lambda x: ex[pl.ds(x * CY + row, 8), :],
            first + (part == 2), last - (part == 0),
        )
        flux = joined(flux, part, edge, row)
        for x in range(first, last):
            tx[pl.ds(x * CY + row, 8), :] = flux[x - first] - flux[x - first + 1]

    def y_faces(st, s, row, part):
        first, last = ((0, H), (H, CY - H), (CY - H, CY))[part]
        flux = march(
            lambda y: ys[st, s, pl.ds((H + y) * CX + row, 8), :],
            lambda y: ny[pl.ds(y * CX + row, 8), :],
            first + (part == 2), last - (part == 0),
        )
        flux = joined(flux, part, edge, CY + row)
        for y in range(first, last):
            ty[pl.ds(row * CY + y, 8, stride=CY), :] = flux[y - first] - flux[y - first + 1]

    def z_faces(st, s):
        def group(i, _):
            first = pl.multiple_of(i * ZROWS, ZROWS)
            rows = [pl.ds(first + 8 * v, 8) for v in range(ZROWS // 8)]
            parts = [shifted_z(xs[st, s, pl.ds(H * CY + first + 8 * v, 8), :], lane) for v in range(ZROWS // 8)]
            flux = [flux_z(uz[r, :], part, lane) for r, part in zip(rows, parts)]
            for r, value in zip(rows, flux):
                tz[r, :] = value - pltpu.roll(value, NZ - 1, 1)
            return 0

        lax.fori_loop(0, CELLS // ZROWS, group, 0)

    forward(0)

    def step(t, _):
        st, s = lax.div(t, 2), lax.rem(t, 2)

        def y_inner(i, _):
            y_faces(st, s, pl.multiple_of(i * 8, 8), 1)
            return 0

        lax.fori_loop(0, CX // 8, y_inner, 0)

        def x_inner(i, e):
            x_faces(st, s, pl.multiple_of(i * 8, 8), 1)
            return factor(t * PART + i * UNROLL, e)

        es[...] = lax.fori_loop(0, CY // 8, x_inner, es[...])
        z_faces(st, s)
        @pl.when(t < 5)
        def _():
            forward(t + 1)

        for r, place in enumerate(PLACES[: rounds - 1]):

            @pl.when(t == place)
            def _(r=r):
                add_sums(r)
                send_sums(r + 1)


        @pl.when(t == 0)
        def _():
            north_edge.wait_recv()
            east_edge.wait_recv()

        y_halo(t, 0).wait_recv()
        y_halo(t, 1).wait_recv()
        for row in range(0, CX, 8):
            y_faces(st, s, row, 0)
            y_faces(st, s, row, 2)
        x_near(t).wait_recv()
        x_second(t, 0).wait_recv()
        x_second(t, 1).wait_recv()

        def x_outer(i, _):
            for k in range(2):
                x_faces(st, s, pl.multiple_of(i * 16 + 8 * k, 8), 0)
                x_faces(st, s, pl.multiple_of(i * 16 + 8 * k, 8), 2)
            return 0

        lax.fori_loop(0, CY // 16, x_outer, 0)
        coef = jnp.where(st == 0, STEP / 18.0, jnp.where(st == 1, STEP / 12.0, STEP / 6.0)).astype(jnp.float32)

        def update(g, _):
            rows = pl.ds(pl.multiple_of(g * GROUP * CY, CY), GROUP * CY)
            value = bs[s, rows, :] + coef * (tx[rows, :] + ty[rows, :] + tz[rows, :])

            @pl.when(st < 2)
            def _():
                xs[st + 1, s, pl.ds(pl.multiple_of((H + g * GROUP) * CY, CY), GROUP * CY), :] = value
                for p in range(GROUP):
                    to_y(st + 1, s, g * GROUP + p, value[p * CY : (p + 1) * CY])

            @pl.when(st == 2)
            def _():
                adv[s, rows, :] = value

            return 0

        lax.fori_loop(0, CX // GROUP, update, 0)

        @pl.when(st < 2)
        def _():
            send_x(t + 2)
            send_y(t + 2)

        return 0

    lax.fori_loop(0, 6, step, 0)

    add_sums(rounds - 1)
    cells = float(n_x * CX * n_y * CY)
    shift[...] = RELAX * (aro[rounds] * (1.0 / cells) - tg[...])

    def drain(t, _):
        x_near(t).wait_send()
        for k in range(2):
            x_first(t, k).wait_send()
            x_second(t, k).wait_send()
            y_halo(t, k).wait_send()
        return 0

    lax.fori_loop(0, 6, drain, 0)

    for r in range(rounds):
        for copy in exchange(r):
            copy.wait_send()
    east_edge.wait_send()
    north_edge.wait_send()


def solve(adv, shift, im, av, cp, out, rh, ob, osem):
    for s in range(2):
        for c in range(TILES):
            value = adv[s, pl.ds(c * 128, 128), :] - shift[s : s + 1, :]
            rh[s, pl.ds(c, NZ, stride=8), :] = jnp.transpose(value)

    zero = jnp.zeros((8, 128), jnp.float32)

    def forward(k8, carry):
        d0, d1 = carry
        base = pl.multiple_of(k8 * 64, 64)
        rows = [pl.ds(base + 8 * i, 8) for i in range(8)]
        data = [(im[r, :], av[r, :], rh[0, r, :], rh[1, r, :]) for r in rows]
        for i, (inverse, a, r0, r1) in enumerate(data):
            d0 = r0 * inverse + a * d0
            d1 = r1 * inverse + a * d1
            rh[0, rows[i], :] = d0
            rh[1, rows[i], :] = d1
        return d0, d1

    lax.fori_loop(0, NZ // 8, forward, (zero, zero))

    def backward(j8, carry):
        v0, v1 = carry
        base = pl.multiple_of((NZ // 8 - 1 - j8) * 64, 64)
        rows = [pl.ds(base + 56 - 8 * i, 8) for i in range(8)]
        data = [(cp[r, :], rh[0, r, :], rh[1, r, :]) for r in rows]
        for i, (c, r0, r1) in enumerate(data):
            v0 = r0 + c * v0
            v1 = r1 + c * v1
            rh[0, rows[i], :] = v0
            rh[1, rows[i], :] = v1
        return v0, v1

    lax.fori_loop(0, NZ // 8, backward, (zero, zero))
    stores = []
    for s in range(2):
        for c in range(TILES):
            rows = pl.ds(c * 128, 128)
            ob[s, rows, :] = jnp.transpose(rh[s, pl.ds(c, NZ, stride=8), :])
            store = pltpu.make_async_copy(ob.at[s, rows], out.at[s, rows], osem.at[s, c])
            store.start()
            stores.append(store)
    for store in stores:
        store.wait()


def in_hbm(value):
    return pltpu.with_memory_space_constraint(value, pltpu.HBM)


def body(n_x, n_y, scalars, east_wind, north_wind, up_wind, diffusivity, target_profile):
    rounds = len(digits(n_x)) + len(digits(n_y))
    hbm = pl.BlockSpec(memory_space=pltpu.HBM)
    f32 = jnp.float32
    vmem = pltpu.VMEM
    dma = pltpu.SemaphoreType.DMA
    resident = pl.BlockSpec(memory_space=pltpu.VMEM)
    columns = jax.ShapeDtypeStruct((LEVELS * 8, 128), f32)
    parts = pl.pallas_call(
        functools.partial(kernel, n_x, n_y),
        out_shape=[
            jax.ShapeDtypeStruct((2, CELLS, NZ), f32), jax.ShapeDtypeStruct((2, NZ), f32), columns, columns, columns,
        ],
        in_specs=[hbm] * 6,
        out_specs=[resident] * 5,
        scratch_shapes=[
            vmem((3, 2, XROWS, NZ), f32),
            vmem((2, CELLS, NZ), f32),
            vmem((3, 2, YROWS, NZ), f32),
            vmem((2, CY + CX, NZ), f32),
            vmem((CELLS, NZ), f32),
            vmem((CELLS, NZ), f32),
            vmem((CELLS, NZ), f32),
            vmem((CELLS + CY, NZ), f32),
            vmem((CELLS + CX, NZ), f32),
            vmem((CELLS, NZ), f32),
            vmem((CELLS, NZ), f32),
            vmem((CELLS, NZ), f32),
            vmem((2, NZ), f32),
            vmem(((LEVELS + 1) * 8, 128), f32),
            vmem((8, 128), f32),
            vmem((rounds + 1, 2, NZ), f32),
            vmem((rounds, 3, 2, NZ), f32),
            vmem((6, 2, HALF, NZ), f32),
            dma((8,)),
            dma((6, 2)),
            dma((6, 2)),
            dma((6,)),
            dma((6,)),
            dma((6, 2)),
            dma((6, 2)),
            dma((6, 2)),
            dma((6, 2)),
            dma((2,)),
            dma((2,)),
            dma((rounds, 3)),
            dma((rounds, 3)),
        ],
        compiler_params=pltpu.CompilerParams(
            collective_id=0, has_side_effects=True, vmem_limit_bytes=48 * 1024 * 1024
        ),
        cost_estimate=pl.CostEstimate(flops=80_000_000, bytes_accessed=4_000_000, transcendentals=0),
    )(
        in_hbm(scalars.reshape(2, CELLS, NZ)),
        in_hbm(east_wind.reshape(CELLS, NZ)),
        in_hbm(north_wind.reshape(CELLS, NZ)),
        in_hbm(up_wind.reshape(CELLS, NZ)),
        in_hbm(diffusivity.reshape(CELLS, NZ)),
        in_hbm(target_profile),
    )
    result = pl.pallas_call(
        solve,
        out_shape=jax.ShapeDtypeStruct((2, CELLS, NZ), f32),
        in_specs=[resident] * 5,
        out_specs=hbm,
        scratch_shapes=[
            vmem((2, NZ * 8, 128), f32),
            vmem((2, CELLS, NZ), f32),
            dma((2, TILES)),
        ],
        compiler_params=pltpu.CompilerParams(vmem_limit_bytes=32 * 1024 * 1024),
        cost_estimate=pl.CostEstimate(flops=2_000_000, bytes_accessed=4_000_000, transcendentals=0),
    )(*parts)
    return result.reshape(2, CX, CY, NZ)


def solution(mesh):
    placed = (
        P(None, "gx", "gy", None),
        P("gx", "gy", None),
        P("gx", "gy", None),
        P("gx", "gy", None),
        P("gx", "gy", None),
        P(),
    )
    return jax.shard_map(
        functools.partial(body, mesh.shape["gx"], mesh.shape["gy"]),
        mesh=mesh, in_specs=placed, out_specs=P(None, "gx", "gy", None), check_vma=False,
    )
```

```python
import functools

import jax
import jax.numpy as jnp
from jax import lax
from jax.experimental import pallas as pl
from jax.experimental.pallas import tpu as pltpu
from jax.sharding import PartitionSpec as P

STEP = 0.3
RELAX = 0.5
EPSILON = 1e-06
EPS = 0.75 * EPSILON
EPS2 = EPS * EPS

CX, CY, NZ = 24, 32, 128
H = 3
XROWS = (CX + 2 * H) * CY
YROWS = (CY + 2 * H) * CX
CELLS = CX * CY
TILES = CELLS // 128
GROUP = 8
ZROWS = 192
PART = 48
LEVELS = 3 * PART
UNROLL = PART // 8
MESH = pl.DeviceIdType.MESH


def cell(dm, em, dp, ep):
    g = dp - dm
    b = (g * g + EPS) + ep * dm
    g2 = g + g
    left = b - g2 * em
    right = b + g2 * ep
    return g, left * left, b * b, right * right


def face(u, total, g_low, g_high, t_low, t_mid, t_high, r2, r1, c1, c0, l0, l1):
    pos = u > 0.0
    b0 = jnp.where(pos, r2, l1)
    b1 = jnp.where(pos, c1, c0)
    b2 = jnp.where(pos, l0, r1)
    gs = jnp.where(pos, g_low, g_high)
    ts = jnp.where(pos, t_low, t_high)
    b0 = 3.0 * b0
    c2 = b2 + b2
    num = b1 * (c2 * ts + b0 * t_mid)
    den = b1 * (b2 + b0) + b0 * c2
    part = num * pl.reciprocal(den, approx=True)
    return u * (3.0 * total - gs) - jnp.abs(u) * part


def march(load_f, load_u, first, last):
    f, d, q, t = {}, {}, {}, {}

    def get_f(i):
        if i not in f:
            f[i] = load_f(i)
        return f[i]

    def get_d(i):
        if i not in d:
            diff = get_f(i) - get_f(i - 1)
            d[i] = (diff, 0.75 * diff)
        return d[i]

    def get_q(i):
        if i not in q:
            q[i] = cell(*get_d(i), *get_d(i + 1))
        return q[i]

    def get_t(i):
        if i not in t:
            t[i] = get_q(i)[0] - get_q(i - 1)[0]
        return t[i]

    out = []
    for j in range(first, last + 1):
        lo2, lo1, hi0, hi1 = get_q(j - 2), get_q(j - 1), get_q(j), get_q(j + 1)
        out.append(
            face(
                load_u(j), get_f(j - 1) + get_f(j), lo1[0], hi0[0], get_t(j - 1), get_t(j), get_t(j + 1),
                lo2[3], lo1[3], lo1[2], hi0[2], hi0[1], hi1[1],
            )
        )
    return out


def joined(flux, part, edge, row):
    rows = pl.ds(row, 8)
    if part == 0:
        return flux + [edge[0, rows, :]]
    if part == 2:
        return [edge[1, rows, :]] + flux
    edge[0, rows, :] = flux[0]
    edge[1, rows, :] = flux[-1]
    return flux


def shifted_z(f, lane):
    below = pltpu.roll(f, 1, 1)
    d = jnp.where(lane == 0, 0.0, f - below)
    return (
        f + below, d, jnp.where(lane == 1, 0.0, pltpu.roll(d, 2, 1)), pltpu.roll(d, 1, 1), pltpu.roll(d, NZ - 1, 1),
        jnp.where(lane == NZ - 1, 0.0, pltpu.roll(d, NZ - 2, 1)),
    )


def flux_z(u, parts, lane):
    total, d3, low2, low1, high1, high2 = parts
    u = jnp.where(lane == 0, 0.0, u)
    pos = u > 0.0
    d1 = jnp.where(pos, low2, high2)
    d2 = jnp.where(pos, low1, high1)
    d4 = jnp.where(pos, high1, low1)
    g0, g1, g2 = d2 - d1, d3 - d2, d4 - d3
    e2, e3 = 0.75 * d2, 0.75 * d3
    b0 = (g0 * g0 + EPS) + e2 * (d2 + g0)
    b1 = (g1 * g1 + EPS) + e3 * d2
    b2 = (g2 * g2 + EPS) + e3 * (d3 - g2)
    b0 = 3.0 * (b0 * b0)
    b1 = b1 * b1
    b2 = b2 * b2
    c2 = b2 + b2
    num = b1 * (c2 * (g1 - g0) + b0 * (g2 - g1))
    den = b1 * (b2 + b0) + b0 * c2
    return u * (3.0 * total) - jnp.abs(u) * (g1 + num * pl.reciprocal(den, approx=True))


def digits(n):
    radix, count = min(4, n), 1
    while radix**count < n:
        count += 1
    return count, radix


def kernel(
    n_x, n_y,
    scal, east, north, upw, diff, target, adv, shift, im, av, cp,
    xs, bs, ys, edge, tz, tx, ty, ex, ny, nraw, uz, kd, tg, fk, es, aro, ari,
    lsem, hsend, hrecv, wsend, wrecv, asend, arecv,
):
    mx, my = lax.axis_index("gx"), lax.axis_index("gy")
    x_up, x_dn = lax.rem(mx + 1, n_x), lax.rem(mx + n_x - 1, n_x)
    y_up, y_dn = lax.rem(my + 1, n_y), lax.rem(my + n_y - 1, n_y)
    per_axis, radix = digits(n_x)
    rounds = 2 * per_axis

    def partner(r, k):
        on_x, stride = 1 - r // per_axis, 1 + (r % per_axis) * (radix - 1)
        me = on_x * mx + (1 - on_x) * my
        digit = lax.rem(lax.div(me, stride), radix)
        other = me + stride * (lax.rem(digit + k, radix) - digit)
        return on_x * other + (1 - on_x) * mx, on_x * my + (1 - on_x) * other

    loads = [
        pltpu.make_async_copy(scal.at[0], xs.at[0, 0, pl.ds(H * CY, CELLS)], lsem.at[0]),
        pltpu.make_async_copy(scal.at[1], xs.at[0, 1, pl.ds(H * CY, CELLS)], lsem.at[1]),
        pltpu.make_async_copy(north, nraw, lsem.at[2]),
        pltpu.make_async_copy(east, ex.at[pl.ds(0, CELLS)], lsem.at[3]),
        pltpu.make_async_copy(diff, kd, lsem.at[4]),
        pltpu.make_async_copy(upw, uz, lsem.at[5]),
        pltpu.make_async_copy(target, tg, lsem.at[6]),
        pltpu.make_async_copy(scal, bs, lsem.at[7]),
    ]
    for load in loads:
        load.start()

    barrier = pltpu.get_barrier_semaphore()
    peers = [(x_up, my), (x_dn, my), (mx, y_up), (mx, y_dn)] + [
        partner(r, k) for r in range(rounds) for k in range(1, radix)
    ]
    for peer in peers:
        pl.semaphore_signal(barrier, inc=1, device_id=peer, device_id_type=MESH)

    def halo(t, way):
        st, s = lax.div(t, 2), lax.rem(t, 2)
        size = CY if way < 2 else CX
        buffer, length = (xs, CX) if way < 2 else (ys, CY)
        to = ((x_up, my), (x_dn, my), (mx, y_up), (mx, y_dn))[way]
        source, target_row = ((length, 0), (H, length + H))[way % 2]
        return pltpu.make_async_remote_copy(
            src_ref=buffer.at[st, s, pl.ds(source * size, H * size)],
            dst_ref=buffer.at[st, s, pl.ds(target_row * size, H * size)],
            send_sem=hsend.at[t, way], recv_sem=hrecv.at[t, way], device_id=to, device_id_type=MESH,
        )

    def send_halos(t, ways):
        for way in ways:
            halo(t, way).start()

    def exchange(r):
        return [
            pltpu.make_async_remote_copy(
                src_ref=aro.at[r], dst_ref=ari.at[r, k - 1], send_sem=asend.at[r, k - 1],
                recv_sem=arecv.at[r, k - 1], device_id=partner(r, k), device_id_type=MESH,
            )
            for k in range(1, radix)
        ]

    def send_sums(r):
        for copy in exchange(r):
            copy.start()

    def add_sums(r):
        total = aro[r]
        for k, copy in enumerate(exchange(r)):
            copy.wait_recv()
            total = total + ari[r, k]
        aro[r + 1] = total

    east_edge = pltpu.make_async_remote_copy(
        src_ref=ex.at[pl.ds(0, CY)], dst_ref=ex.at[pl.ds(CELLS, CY)], send_sem=wsend.at[0], recv_sem=wrecv.at[0],
        device_id=(x_dn, my), device_id_type=MESH,
    )
    north_edge = pltpu.make_async_remote_copy(
        src_ref=ny.at[pl.ds(0, CX)], dst_ref=ny.at[pl.ds(CELLS, CX)], send_sem=wsend.at[1], recv_sem=wrecv.at[1],
        device_id=(mx, y_dn), device_id_type=MESH,
    )

    def to_y(st, s, x, value):
        for i in range(CY // 8):
            ys[st, s, pl.ds((H + 8 * i) * CX + x, 8, stride=CX), :] = value[8 * i : 8 * i + 8]

    loads[0].wait()
    loads[1].wait()
    pl.semaphore_wait(barrier, len(peers))

    def first_field(s, _):
        send_halos(s, (0, 1))

        def convert(g, total):
            values = [xs[0, s, pl.ds(pl.multiple_of((H + g * GROUP + p) * CY, CY), CY), :] for p in range(GROUP)]
            for p, value in enumerate(values):
                to_y(0, s, g * GROUP + p, value)
            return total + sum(values)

        total = lax.fori_loop(0, CX // GROUP, convert, jnp.zeros((CY, NZ), jnp.float32))
        aro[0, pl.ds(s, 1), :] = jnp.sum(total, axis=0, keepdims=True)
        send_halos(s, (2, 3))
        return 0

    lax.fori_loop(0, 2, first_field, 0)
    send_sums(0)

    loads[2].wait()

    def turn_north(g, _):
        values = [nraw[pl.ds(pl.multiple_of((g * GROUP + p) * CY, CY), CY), :] for p in range(GROUP)]
        for p, value in enumerate(values):
            for i in range(CY // 8):
                ny[pl.ds(8 * i * CX + g * GROUP + p, 8, stride=CX), :] = value[8 * i : 8 * i + 8]
        return 0

    lax.fori_loop(0, CX // GROUP, turn_north, 0)
    north_edge.start()
    loads[3].wait()

    east_edge.start()
    loads[5].wait()
    lane = lax.broadcasted_iota(jnp.int32, (8, NZ), 1)

    loads[4].wait()
    loads[6].wait()
    loads[7].wait()

    def columns_to_lanes(c, _):
        rows = pl.ds(pl.multiple_of(c * 128, 128), 128)
        fk[pl.ds(c, NZ, stride=8), :] = jnp.transpose(kd[rows, :]) * STEP
        return 0

    fk[...] = jnp.zeros(fk.shape, jnp.float32)
    lax.fori_loop(0, TILES, columns_to_lanes, 0)
    fk[pl.ds(0, 8), :] = jnp.zeros((8, 128), jnp.float32)
    es[...] = jnp.zeros((8, 128), jnp.float32)

    def factor(first, e):
        base = pl.multiple_of(first * 8, 8)
        low = fk[pl.ds(base, 8), :]
        for i in range(UNROLL):
            row = pl.ds(base + 8 * i, 8)
            above = fk[pl.ds(base + 8 * i + 8, 8), :]
            g = 1.0 + low * e
            inverse = pl.reciprocal(g + above, approx=True)
            e = g * inverse
            im[row, :] = inverse
            av[row, :] = low * inverse
            cp[row, :] = above * inverse
            low = above
        return e

    def x_faces(st, s, row, part):
        first, last = ((0, H), (H, CX - H), (CX - H, CX))[part]
        flux = march(
            lambda x: xs[st, s, pl.ds((H + x) * CY + row, 8), :],
            lambda x: ex[pl.ds(x * CY + row, 8), :],
            first + (part == 2), last - (part == 0),
        )
        flux = joined(flux, part, edge.at[s], row)
        for x in range(first, last):
            tx[s, pl.ds(x * CY + row, 8), :] = flux[x - first] - flux[x - first + 1]

    def y_faces(st, s, row, part):
        first, last = ((0, H), (H, CY - H), (CY - H, CY))[part]
        flux = march(
            lambda y: ys[st, s, pl.ds((H + y) * CX + row, 8), :],
            lambda y: ny[pl.ds(y * CX + row, 8), :],
            first + (part == 2), last - (part == 0),
        )
        flux = joined(flux, part, edge.at[s], CY + row)
        for y in range(first, last):
            ty[s, pl.ds(row * CY + y, 8, stride=CY), :] = flux[y - first] - flux[y - first + 1]

    def z_faces(st, s, first):
        rows = [pl.ds(first + 8 * v, 8) for v in range(ZROWS // 8)]
        parts = [shifted_z(xs[st, s, pl.ds(H * CY + first + 8 * v, 8), :], lane) for v in range(ZROWS // 8)]
        flux = [flux_z(uz[r, :], part, lane) for r, part in zip(rows, parts)]
        for r, value in zip(rows, flux):
            tz[s, r, :] = value - pltpu.roll(value, NZ - 1, 1)

    def columns(count, work, carry):
        return lax.fori_loop(0, 2 * count, lambda i, c: work(lax.div(i, count), lax.rem(i, count), c), carry)

    def stage(st, _):
        def y_inner(s, i, _):
            y_faces(st, s, pl.multiple_of(i * 8, 8), 1)
            return 0

        def x_inner(s, i, e):
            x_faces(st, s, pl.multiple_of(i * 8, 8), 1)
            return factor(st * PART + (s * (CY // 8) + i) * UNROLL, e)

        def z_all(s, i, _):
            z_faces(st, s, pl.multiple_of(i * ZROWS, ZROWS))
            return 0

        columns(CX // 8, y_inner, 0)
        es[...] = columns(CY // 8, x_inner, es[...])
        columns(CELLS // ZROWS, z_all, 0)

        @pl.when(st < rounds - 1)
        def _():
            add_sums(st)
            send_sums(st + 1)

        @pl.when(st == 0)
        def _():
            north_edge.wait_recv()
            east_edge.wait_recv()

        coef = jnp.where(st == 0, STEP / 18.0, jnp.where(st == 1, STEP / 12.0, STEP / 6.0)).astype(jnp.float32)

        def finish(s, _):
            t = 2 * st + s

            def y_outer(i, _):
                y_faces(st, s, pl.multiple_of(i * 8, 8), 0)
                y_faces(st, s, pl.multiple_of(i * 8, 8), 2)
                return 0

            def x_outer(i, _):
                x_faces(st, s, pl.multiple_of(i * 8, 8), 0)
                x_faces(st, s, pl.multiple_of(i * 8, 8), 2)
                return 0

            def update(g, _):
                rows = pl.ds(pl.multiple_of(g * GROUP * CY, CY), GROUP * CY)
                value = bs[s, rows, :] + coef * (tx[s, rows, :] + ty[s, rows, :] + tz[s, rows, :])

                @pl.when(st < 2)
                def _():
                    xs[st + 1, s, pl.ds(pl.multiple_of((H + g * GROUP) * CY, CY), GROUP * CY), :] = value
                    for p in range(GROUP):
                        to_y(st + 1, s, g * GROUP + p, value[p * CY : (p + 1) * CY])

                @pl.when(st == 2)
                def _():
                    adv[s, rows, :] = value

                return 0

            halo(t, 2).wait_recv()
            halo(t, 3).wait_recv()
            lax.fori_loop(0, CX // 8, y_outer, 0)
            halo(t, 0).wait_recv()
            halo(t, 1).wait_recv()
            lax.fori_loop(0, CY // 8, x_outer, 0)
            lax.fori_loop(0, CX // GROUP, update, 0)

            @pl.when(st < 2)
            def _():
                send_halos(t + 2, range(4))

            return 0

        lax.fori_loop(0, 2, finish, 0)
        return 0

    lax.fori_loop(0, 3, stage, 0)

    add_sums(rounds - 1)
    cells = float(n_x * CX * n_y * CY)
    shift[...] = RELAX * (aro[rounds] * (1.0 / cells) - tg[...])

    def drain(t, _):
        for way in range(4):
            halo(t, way).wait_send()
        return 0

    lax.fori_loop(0, 6, drain, 0)

    for r in range(rounds):
        for copy in exchange(r):
            copy.wait_send()
    east_edge.wait_send()
    north_edge.wait_send()


def solve(adv, shift, im, av, cp, out, rh, ob, osem):
    for s in range(2):
        for c in range(TILES):
            value = adv[s, pl.ds(c * 128, 128), :] - shift[s : s + 1, :]
            rh[s, pl.ds(c, NZ, stride=8), :] = jnp.transpose(value)

    zero = jnp.zeros((8, 128), jnp.float32)

    def forward(k8, carry):
        d0, d1 = carry
        base = pl.multiple_of(k8 * 64, 64)
        rows = [pl.ds(base + 8 * i, 8) for i in range(8)]
        data = [(im[r, :], av[r, :], rh[0, r, :], rh[1, r, :]) for r in rows]
        for i, (inverse, a, r0, r1) in enumerate(data):
            d0 = r0 * inverse + a * d0
            d1 = r1 * inverse + a * d1
            rh[0, rows[i], :] = d0
            rh[1, rows[i], :] = d1
        return d0, d1

    lax.fori_loop(0, NZ // 8, forward, (zero, zero))

    def backward(j8, carry):
        v0, v1 = carry
        base = pl.multiple_of((NZ // 8 - 1 - j8) * 64, 64)
        rows = [pl.ds(base + 56 - 8 * i, 8) for i in range(8)]
        data = [(cp[r, :], rh[0, r, :], rh[1, r, :]) for r in rows]
        for i, (c, r0, r1) in enumerate(data):
            v0 = r0 + c * v0
            v1 = r1 + c * v1
            rh[0, rows[i], :] = v0
            rh[1, rows[i], :] = v1
        return v0, v1

    lax.fori_loop(0, NZ // 8, backward, (zero, zero))
    stores = []
    for s in range(2):
        for c in range(TILES):
            rows = pl.ds(c * 128, 128)
            ob[s, rows, :] = jnp.transpose(rh[s, pl.ds(c, NZ, stride=8), :])
            store = pltpu.make_async_copy(ob.at[s, rows], out.at[s, rows], osem.at[s, c])
            store.start()
            stores.append(store)
    for store in stores:
        store.wait()


def in_hbm(value):
    return pltpu.with_memory_space_constraint(value, pltpu.HBM)


def body(n_x, n_y, scalars, east_wind, north_wind, up_wind, diffusivity, target_profile):
    rounds = 2 * digits(n_x)[0]
    hbm = pl.BlockSpec(memory_space=pltpu.HBM)
    f32 = jnp.float32
    vmem = pltpu.VMEM
    dma = pltpu.SemaphoreType.DMA
    resident = pl.BlockSpec(memory_space=pltpu.VMEM)
    columns = jax.ShapeDtypeStruct((LEVELS * 8, 128), f32)
    parts = pl.pallas_call(
        functools.partial(kernel, n_x, n_y),
        out_shape=[
            jax.ShapeDtypeStruct((2, CELLS, NZ), f32), jax.ShapeDtypeStruct((2, NZ), f32), columns, columns, columns,
        ],
        in_specs=[hbm] * 6,
        out_specs=[resident] * 5,
        scratch_shapes=[
            vmem((3, 2, XROWS, NZ), f32),
            vmem((2, CELLS, NZ), f32),
            vmem((3, 2, YROWS, NZ), f32),
            vmem((2, 2, CY + CX, NZ), f32),
            vmem((2, CELLS, NZ), f32),
            vmem((2, CELLS, NZ), f32),
            vmem((2, CELLS, NZ), f32),
            vmem((CELLS + CY, NZ), f32),
            vmem((CELLS + CX, NZ), f32),
            vmem((CELLS, NZ), f32),
            vmem((CELLS, NZ), f32),
            vmem((CELLS, NZ), f32),
            vmem((2, NZ), f32),
            vmem(((LEVELS + 1) * 8, 128), f32),
            vmem((8, 128), f32),
            vmem((rounds + 1, 2, NZ), f32),
            vmem((rounds, 3, 2, NZ), f32),
            dma((8,)),
            dma((6, 4)),
            dma((6, 4)),
            dma((2,)),
            dma((2,)),
            dma((rounds, 3)),
            dma((rounds, 3)),
        ],
        compiler_params=pltpu.CompilerParams(
            collective_id=0, has_side_effects=True, vmem_limit_bytes=48 * 1024 * 1024
        ),
        cost_estimate=pl.CostEstimate(flops=80_000_000, bytes_accessed=4_000_000, transcendentals=0),
    )(
        in_hbm(scalars.reshape(2, CELLS, NZ)),
        in_hbm(east_wind.reshape(CELLS, NZ)),
        in_hbm(north_wind.reshape(CELLS, NZ)),
        in_hbm(up_wind.reshape(CELLS, NZ)),
        in_hbm(diffusivity.reshape(CELLS, NZ)),
        in_hbm(target_profile),
    )
    result = pl.pallas_call(
        solve,
        out_shape=jax.ShapeDtypeStruct((2, CELLS, NZ), f32),
        in_specs=[resident] * 5,
        out_specs=hbm,
        scratch_shapes=[
            vmem((2, NZ * 8, 128), f32),
            vmem((2, CELLS, NZ), f32),
            dma((2, TILES)),
        ],
        compiler_params=pltpu.CompilerParams(vmem_limit_bytes=32 * 1024 * 1024),
        cost_estimate=pl.CostEstimate(flops=2_000_000, bytes_accessed=4_000_000, transcendentals=0),
    )(*parts)
    return result.reshape(2, CX, CY, NZ)


def solution(mesh):
    placed = (
        P(None, "gx", "gy", None),
        P("gx", "gy", None),
        P("gx", "gy", None),
        P("gx", "gy", None),
        P("gx", "gy", None),
        P(),
    )
    return jax.shard_map(
        functools.partial(body, mesh.shape["gx"], mesh.shape["gy"]),
        mesh=mesh, in_specs=placed, out_specs=P(None, "gx", "gy", None), check_vma=False,
    )
```

```python
import functools

import jax
import jax.numpy as jnp
from jax import lax
from jax.experimental import pallas as pl
from jax.experimental.pallas import tpu as pltpu
from jax.sharding import PartitionSpec as P

STEP = 0.3
RELAX = 0.5
EPSILON = 1e-06
EPS = 0.75 * EPSILON
EPS2 = EPS * EPS

CX, CY, NZ = 24, 32, 128
H = 3
YROWS = (CY + 2 * H) * CX
CELLS = CX * CY
TILES = CELLS // 128
GROUP = 8
ZROWS = 192
TURN = 16
PART = 48
LEVELS = 3 * PART
UNROLL = PART // 8
MESH = pl.DeviceIdType.MESH


def cell(dm, em, dp, ep):
    g = dp - dm
    b = (g * g + EPS) + ep * dm
    g2 = g + g
    left = b - g2 * em
    right = b + g2 * ep
    return g, left * left, b * b, right * right


def face(u, total, g_low, g_high, t_low, t_mid, t_high, r2, r1, c1, c0, l0, l1):
    pos = u > 0.0
    b0 = jnp.where(pos, r2, l1)
    b1 = jnp.where(pos, c1, c0)
    b2 = jnp.where(pos, l0, r1)
    gs = jnp.where(pos, g_low, g_high)
    ts = jnp.where(pos, t_low, t_high)
    b0 = 3.0 * b0
    c2 = b2 + b2
    num = b1 * (c2 * ts + b0 * t_mid)
    den = b1 * (b2 + b0) + b0 * c2
    part = num * pl.reciprocal(den, approx=True)
    return u * (3.0 * total - gs) - jnp.abs(u) * part


def march(load_f, load_u, cells, emit):
    f, d, q, t = {}, {}, {}, {}

    def get_f(i):
        if i not in f:
            f[i] = load_f(i)
        return f[i]

    def get_d(i):
        if i not in d:
            diff = get_f(i) - get_f(i - 1)
            d[i] = (diff, 0.75 * diff)
        return d[i]

    def get_q(i):
        if i not in q:
            q[i] = cell(*get_d(i), *get_d(i + 1))
        return q[i]

    def get_t(i):
        if i not in t:
            t[i] = get_q(i)[0] - get_q(i - 1)[0]
        return t[i]

    lower = None
    for j in range(cells + 1):
        lo2, lo1, hi0, hi1 = get_q(j - 2), get_q(j - 1), get_q(j), get_q(j + 1)
        upper = face(
            load_u(j), get_f(j - 1) + get_f(j), lo1[0], hi0[0], get_t(j - 1), get_t(j), get_t(j + 1),
            lo2[3], lo1[3], lo1[2], hi0[2], hi0[1], hi1[1],
        )
        if j > 0:
            emit(j - 1, lower - upper)
        lower = upper


def shifted_z(f, lane):
    below = pltpu.roll(f, 1, 1)
    d = jnp.where(lane == 0, 0.0, f - below)
    return (
        f + below, d, jnp.where(lane == 1, 0.0, pltpu.roll(d, 2, 1)), pltpu.roll(d, 1, 1), pltpu.roll(d, NZ - 1, 1),
        jnp.where(lane == NZ - 1, 0.0, pltpu.roll(d, NZ - 2, 1)),
    )


def flux_z(u, parts, lane):
    total, d3, low2, low1, high1, high2 = parts
    u = jnp.where(lane == 0, 0.0, u)
    pos = u > 0.0
    d1 = jnp.where(pos, low2, high2)
    d2 = jnp.where(pos, low1, high1)
    d4 = jnp.where(pos, high1, low1)
    g0, g1, g2 = d2 - d1, d3 - d2, d4 - d3
    e2, e3 = 0.75 * d2, 0.75 * d3
    b0 = (g0 * g0 + EPS) + e2 * (d2 + g0)
    b1 = (g1 * g1 + EPS) + e3 * d2
    b2 = (g2 * g2 + EPS) + e3 * (d3 - g2)
    b0 = 3.0 * (b0 * b0)
    b1 = b1 * b1
    b2 = b2 * b2
    c2 = b2 + b2
    num = b1 * (c2 * (g1 - g0) + b0 * (g2 - g1))
    den = b1 * (b2 + b0) + b0 * c2
    return u * (3.0 * total) - jnp.abs(u) * (g1 + num * pl.reciprocal(den, approx=True))


def digits(n):
    radix, count = min(4, n), 1
    while radix**count < n:
        count += 1
    return count, radix


def kernel(
    n_x, n_y,
    scal, east, north, upw, diff, target, adv, shift, im, av, cp,
    xf, xh, bs, ys, tz, ty, ex, ny, nraw, uz, kd, tg, fk, es, aro, ari,
    lsem, csem, hsend, hrecv, wsend, wrecv, asend, arecv,
):
    mx, my = lax.axis_index("gx"), lax.axis_index("gy")
    x_up, x_dn = lax.rem(mx + 1, n_x), lax.rem(mx + n_x - 1, n_x)
    y_up, y_dn = lax.rem(my + 1, n_y), lax.rem(my + n_y - 1, n_y)
    per_axis, radix = digits(n_x)
    rounds = 2 * per_axis

    def partner(r, k):
        on_x, stride = 1 - r // per_axis, 1 + (r % per_axis) * (radix - 1)
        me = on_x * mx + (1 - on_x) * my
        digit = lax.rem(lax.div(me, stride), radix)
        other = me + stride * (lax.rem(digit + k, radix) - digit)
        return on_x * other + (1 - on_x) * mx, on_x * my + (1 - on_x) * other

    loads = [
        pltpu.make_async_copy(scal.at[0], xf.at[0], lsem.at[0]),
        pltpu.make_async_copy(scal.at[1], xf.at[1], lsem.at[1]),
        pltpu.make_async_copy(north, nraw, lsem.at[2]),
        pltpu.make_async_copy(east, ex.at[pl.ds(0, CELLS)], lsem.at[3]),
        pltpu.make_async_copy(diff, kd, lsem.at[4]),
        pltpu.make_async_copy(upw, uz, lsem.at[5]),
        pltpu.make_async_copy(target, tg, lsem.at[6]),
        pltpu.make_async_copy(scal, bs, lsem.at[7]),
    ]
    for load in loads:
        load.start()

    barrier = pltpu.get_barrier_semaphore()
    peers = [(x_up, my), (x_dn, my), (mx, y_up), (mx, y_dn)] + [
        partner(r, k) for r in range(rounds) for k in range(1, radix)
    ]
    for peer in peers:
        pl.semaphore_signal(barrier, inc=1, device_id=peer, device_id_type=MESH)

    def halo(t, way, field=adv):
        st, s = lax.div(t, 2), lax.rem(t, 2)
        to = ((x_up, my), (x_dn, my), (mx, y_up), (mx, y_dn))[way]
        if way < 2:
            src, dst = field.at[s, pl.ds((CELLS - H * CY, 0)[way], H * CY)], xh.at[t, way]
        else:
            src = ys.at[st, s, pl.ds((CY, H)[way - 2] * CX, H * CX)]
            dst = ys.at[st, s, pl.ds((0, CY + H)[way - 2] * CX, H * CX)]
        return pltpu.make_async_remote_copy(
            src_ref=src, dst_ref=dst, send_sem=hsend.at[t, way], recv_sem=hrecv.at[t, way],
            device_id=to, device_id_type=MESH,
        )

    def exchange(r):
        return [
            pltpu.make_async_remote_copy(
                src_ref=aro.at[r], dst_ref=ari.at[r, k - 1], send_sem=asend.at[r, k - 1],
                recv_sem=arecv.at[r, k - 1], device_id=partner(r, k), device_id_type=MESH,
            )
            for k in range(1, radix)
        ]

    def send_sums(r):
        for copy in exchange(r):
            copy.start()

    def add_sums(r):
        total = aro[r]
        for k, copy in enumerate(exchange(r)):
            copy.wait_recv()
            total = total + ari[r, k]
        aro[r + 1] = total

    east_edge = pltpu.make_async_remote_copy(
        src_ref=ex.at[pl.ds(0, CY)], dst_ref=ex.at[pl.ds(CELLS, CY)], send_sem=wsend.at[0], recv_sem=wrecv.at[0],
        device_id=(x_dn, my), device_id_type=MESH,
    )
    north_edge = pltpu.make_async_remote_copy(
        src_ref=ny.at[pl.ds(0, CX)], dst_ref=ny.at[pl.ds(CELLS, CX)], send_sem=wsend.at[1], recv_sem=wrecv.at[1],
        device_id=(mx, y_dn), device_id_type=MESH,
    )

    def to_y(st, s, x, value):
        for i in range(CY // 8):
            ys[st, s, pl.ds((H + 8 * i) * CX + x, 8, stride=CX), :] = value[8 * i : 8 * i + 8]

    loads[0].wait()
    loads[1].wait()
    pl.semaphore_wait(barrier, len(peers))

    def first_field(s, _):
        halo(s, 0, xf).start()
        halo(s, 1, xf).start()

        def convert(g, total):
            values = [xf[s, pl.ds(pl.multiple_of((g * GROUP + p) * CY, CY), CY), :] for p in range(GROUP)]
            for p, value in enumerate(values):
                to_y(0, s, g * GROUP + p, value)
            return total + sum(values)

        total = lax.fori_loop(0, CX // GROUP, convert, jnp.zeros((CY, NZ), jnp.float32))
        aro[0, pl.ds(s, 1), :] = jnp.sum(total, axis=0, keepdims=True)
        halo(s, 2).start()
        halo(s, 3).start()
        return 0

    lax.fori_loop(0, 2, first_field, 0)
    send_sums(0)

    loads[2].wait()

    def turn_north(g, _):
        values = [nraw[pl.ds(pl.multiple_of((g * GROUP + p) * CY, CY), CY), :] for p in range(GROUP)]
        for p, value in enumerate(values):
            for i in range(CY // 8):
                ny[pl.ds(8 * i * CX + g * GROUP + p, 8, stride=CX), :] = value[8 * i : 8 * i + 8]
        return 0

    lax.fori_loop(0, CX // GROUP, turn_north, 0)
    north_edge.start()
    loads[3].wait()

    east_edge.start()
    loads[5].wait()
    lane = lax.broadcasted_iota(jnp.int32, (8, NZ), 1)

    loads[4].wait()
    loads[6].wait()
    loads[7].wait()

    def columns_to_lanes(c, _):
        rows = pl.ds(pl.multiple_of(c * 128, 128), 128)
        fk[pl.ds(c, NZ, stride=8), :] = jnp.transpose(kd[rows, :]) * STEP
        return 0

    fk[pl.ds(NZ * 8, fk.shape[0] - NZ * 8), :] = jnp.zeros((fk.shape[0] - NZ * 8, 128), jnp.float32)
    lax.fori_loop(0, TILES, columns_to_lanes, 0)
    fk[pl.ds(0, 8), :] = jnp.zeros((8, 128), jnp.float32)
    es[...] = jnp.zeros((8, 128), jnp.float32)

    def factor(first, e):
        base = pl.multiple_of(first * 8, 8)
        low = fk[pl.ds(base, 8), :]
        for i in range(UNROLL):
            row = pl.ds(base + 8 * i, 8)
            above = fk[pl.ds(base + 8 * i + 8, 8), :]
            g = 1.0 + low * e
            inverse = pl.reciprocal(g + above, approx=True)
            e = g * inverse
            im[row, :] = inverse
            av[row, :] = low * inverse
            cp[row, :] = above * inverse
            low = above
        return e

    def y_column(st, s, row):
        def keep(y, diff):
            ty[pl.ds(row * CY + y, 8, stride=CY), :] = diff

        march(
            lambda y: ys[st, s, pl.ds((H + y) * CX + row, 8), :],
            lambda y: ny[pl.ds(y * CX + row, 8), :],
            CY, keep,
        )

    def x_column(st, s, row, coef):
        t = 2 * st + s

        def load(x):
            if x < 0:
                return xh[t, 0, pl.ds((x + H) * CY + row, 8), :]
            if x >= CX:
                return xh[t, 1, pl.ds((x - CX) * CY + row, 8), :]
            return xf[s, pl.ds(x * CY + row, 8), :]

        def keep(x, diff):
            rows = pl.ds(x * CY + row, 8)
            value = bs[s, rows, :] + coef * (diff + ty[rows, :] + tz[s, rows, :])
            adv[s, rows, :] = value
            ys[st + 1, s, pl.ds((H + row) * CX + x, 8, stride=CX), :] = value

        march(load, lambda x: ex[pl.ds(x * CY + row, 8), :], CX, keep)

    def z_faces(s, first):
        rows = [pl.ds(first + 8 * v, 8) for v in range(ZROWS // 8)]
        parts = [shifted_z(xf[s, pl.ds(first + 8 * v, 8), :], lane) for v in range(ZROWS // 8)]
        flux = [flux_z(uz[r, :], part, lane) for r, part in zip(rows, parts)]
        for r, value in zip(rows, flux):
            tz[s, r, :] = value - pltpu.roll(value, NZ - 1, 1)

    def back(s):
        return pltpu.make_async_copy(adv.at[s], xf.at[s], csem.at[s])

    def stage(st, _):
        coef = jnp.where(st == 0, STEP / 18.0, jnp.where(st == 1, STEP / 12.0, STEP / 6.0)).astype(jnp.float32)

        def z_pass(s, _):
            @pl.when(st > 0)
            def _():
                back(s).wait()

            def group(i, _):
                z_faces(s, pl.multiple_of(i * ZROWS, ZROWS))
                return 0

            lax.fori_loop(0, CELLS // ZROWS, group, 0)
            return 0

        lax.fori_loop(0, 2, z_pass, 0)

        @pl.when(st < rounds - 1)
        def _():
            add_sums(st)
            send_sums(st + 1)

        @pl.when(st == 0)
        def _():
            north_edge.wait_recv()
            east_edge.wait_recv()

        def finish(s, _):
            t = 2 * st + s

            def y_pass(i, _):
                y_column(st, s, pl.multiple_of(i * 8, 8))
                return 0

            def x_pass(i, e):
                x_column(st, s, pl.multiple_of(i * 8, 8), coef)
                return factor(st * PART + (s * (CY // 8) + i) * UNROLL, e)

            halo(t, 2).wait_recv()
            halo(t, 3).wait_recv()
            lax.fori_loop(0, CX // 8, y_pass, 0)
            for way in range(2):
                halo(t, way).wait_recv()
                halo(t, way).wait_send()
            es[...] = lax.fori_loop(0, CY // 8, x_pass, es[...])

            @pl.when(st < 2)
            def _():
                for way in (2, 3, 0, 1):
                    halo(t + 2, way).start()
                back(s).start()

            return 0

        lax.fori_loop(0, 2, finish, 0)
        return 0

    lax.fori_loop(0, 3, stage, 0)

    add_sums(rounds - 1)
    cells = float(n_x * CX * n_y * CY)
    shift[...] = RELAX * (aro[rounds] * (1.0 / cells) - tg[...])

    def drain(t, _):
        for way in (2, 3):
            halo(t, way).wait_send()
        return 0

    lax.fori_loop(0, 6, drain, 0)

    for r in range(rounds):
        for copy in exchange(r):
            copy.wait_send()
    east_edge.wait_send()
    north_edge.wait_send()


def solve(adv, shift, im, av, cp, out, rh, ob, osem):
    for s in range(2):
        for c in range(TILES):
            value = adv[s, pl.ds(c * 128, 128), :] - shift[s : s + 1, :]
            rh[s, pl.ds(c, NZ, stride=8), :] = jnp.transpose(value)

    zero = jnp.zeros((8, 128), jnp.float32)

    def forward(k8, carry):
        d0, d1 = carry
        base = pl.multiple_of(k8 * (TURN * 8), TURN * 8)
        rows = [pl.ds(base + 8 * i, 8) for i in range(TURN)]
        data = [(im[r, :], av[r, :], rh[0, r, :], rh[1, r, :]) for r in rows]
        for i, (inverse, a, r0, r1) in enumerate(data):
            d0 = r0 * inverse + a * d0
            d1 = r1 * inverse + a * d1
            rh[0, rows[i], :] = d0
            rh[1, rows[i], :] = d1
        return d0, d1

    lax.fori_loop(0, NZ // TURN, forward, (zero, zero))

    def backward(j8, carry):
        v0, v1 = carry
        base = pl.multiple_of((NZ // TURN - 1 - j8) * (TURN * 8), TURN * 8)
        rows = [pl.ds(base + 8 * (TURN - 1 - i), 8) for i in range(TURN)]
        data = [(cp[r, :], rh[0, r, :], rh[1, r, :]) for r in rows]
        for i, (c, r0, r1) in enumerate(data):
            v0 = r0 + c * v0
            v1 = r1 + c * v1
            rh[0, rows[i], :] = v0
            rh[1, rows[i], :] = v1
        return v0, v1

    lax.fori_loop(0, NZ // TURN, backward, (zero, zero))
    stores = []
    for s in range(2):
        for c in range(TILES):
            rows = pl.ds(c * 128, 128)
            ob[s, rows, :] = jnp.transpose(rh[s, pl.ds(c, NZ, stride=8), :])
            store = pltpu.make_async_copy(ob.at[s, rows], out.at[s, rows], osem.at[s, c])
            store.start()
            stores.append(store)
    for store in stores:
        store.wait()


def in_hbm(value):
    return pltpu.with_memory_space_constraint(value, pltpu.HBM)


def body(n_x, n_y, scalars, east_wind, north_wind, up_wind, diffusivity, target_profile):
    rounds = 2 * digits(n_x)[0]
    hbm = pl.BlockSpec(memory_space=pltpu.HBM)
    f32 = jnp.float32
    vmem = pltpu.VMEM
    dma = pltpu.SemaphoreType.DMA
    resident = pl.BlockSpec(memory_space=pltpu.VMEM)
    columns = jax.ShapeDtypeStruct((LEVELS * 8, 128), f32)
    parts = pl.pallas_call(
        functools.partial(kernel, n_x, n_y),
        out_shape=[
            jax.ShapeDtypeStruct((2, CELLS, NZ), f32), jax.ShapeDtypeStruct((2, NZ), f32), columns, columns, columns,
        ],
        in_specs=[hbm] * 6,
        out_specs=[resident] * 5,
        scratch_shapes=[
            vmem((2, CELLS, NZ), f32),
            vmem((6, 2, H * CY, NZ), f32),
            vmem((2, CELLS, NZ), f32),
            vmem((4, 2, YROWS, NZ), f32),
            vmem((2, CELLS, NZ), f32),
            vmem((CELLS, NZ), f32),
            vmem((CELLS + CY, NZ), f32),
            vmem((CELLS + CX, NZ), f32),
            vmem((CELLS, NZ), f32),
            vmem((CELLS, NZ), f32),
            vmem((CELLS, NZ), f32),
            vmem((2, NZ), f32),
            vmem(((LEVELS + 1) * 8, 128), f32),
            vmem((8, 128), f32),
            vmem((rounds + 1, 2, NZ), f32),
            vmem((rounds, 3, 2, NZ), f32),
            dma((8,)),
            dma((2,)),
            dma((6, 4)),
            dma((6, 4)),
            dma((2,)),
            dma((2,)),
            dma((rounds, 3)),
            dma((rounds, 3)),
        ],
        compiler_params=pltpu.CompilerParams(
            collective_id=0, has_side_effects=True, vmem_limit_bytes=48 * 1024 * 1024
        ),
        cost_estimate=pl.CostEstimate(flops=80_000_000, bytes_accessed=4_000_000, transcendentals=0),
    )(
        in_hbm(scalars.reshape(2, CELLS, NZ)),
        in_hbm(east_wind.reshape(CELLS, NZ)),
        in_hbm(north_wind.reshape(CELLS, NZ)),
        in_hbm(up_wind.reshape(CELLS, NZ)),
        in_hbm(diffusivity.reshape(CELLS, NZ)),
        in_hbm(target_profile),
    )
    result = pl.pallas_call(
        solve,
        out_shape=jax.ShapeDtypeStruct((2, CELLS, NZ), f32),
        in_specs=[resident] * 5,
        out_specs=hbm,
        scratch_shapes=[
            vmem((2, NZ * 8, 128), f32),
            vmem((2, CELLS, NZ), f32),
            dma((2, TILES)),
        ],
        compiler_params=pltpu.CompilerParams(vmem_limit_bytes=32 * 1024 * 1024),
        cost_estimate=pl.CostEstimate(flops=2_000_000, bytes_accessed=4_000_000, transcendentals=0),
    )(*parts)
    return result.reshape(2, CX, CY, NZ)


def solution(mesh):
    placed = (
        P(None, "gx", "gy", None),
        P("gx", "gy", None),
        P("gx", "gy", None),
        P("gx", "gy", None),
        P("gx", "gy", None),
        P(),
    )
    return jax.shard_map(
        functools.partial(body, mesh.shape["gx"], mesh.shape["gy"]),
        mesh=mesh, in_specs=placed, out_specs=P(None, "gx", "gy", None), check_vma=False,
    )
```

```python
import functools

import jax
import jax.numpy as jnp
from jax import lax
from jax.experimental import pallas as pl
from jax.experimental.pallas import tpu as pltpu
from jax.sharding import PartitionSpec as P

STEP = 0.3
RELAX = 0.5
EPSILON = 1e-06
EPS = 0.75 * EPSILON
EPS2 = EPS * EPS

CX, CY, NZ = 24, 32, 128
H = 3
YROWS = (CY + 2 * H) * CX
CELLS = CX * CY
TILES = CELLS // 128
GROUP = 8
ZROWS = 192
TURN = 16
PART = 48
LEVELS = 3 * PART
UNROLL = PART // 8
MESH = pl.DeviceIdType.MESH


def cell(dm, em, dp, ep):
    g = dp - dm
    b = (g * g + EPS) + ep * dm
    g2 = g + g
    left = b - g2 * em
    right = b + g2 * ep
    return g, left * left, b * b, right * right


def face(u, total, g_low, g_high, t_low, t_mid, t_high, r2, r1, c1, c0, l0, l1):
    pos = u > 0.0
    b0 = jnp.where(pos, r2, l1)
    b1 = jnp.where(pos, c1, c0)
    b2 = jnp.where(pos, l0, r1)
    gs = jnp.where(pos, g_low, g_high)
    ts = jnp.where(pos, t_low, t_high)
    b0 = 3.0 * b0
    c2 = b2 + b2
    num = b1 * (c2 * ts + b0 * t_mid)
    den = b1 * (b2 + b0) + b0 * c2
    part = num * pl.reciprocal(den, approx=True)
    return u * (3.0 * total - gs) - jnp.abs(u) * part


def march(load_f, load_u, cells, emit):
    f, d, q, t = {}, {}, {}, {}

    def get_f(i):
        if i not in f:
            f[i] = load_f(i)
        return f[i]

    def get_d(i):
        if i not in d:
            diff = get_f(i) - get_f(i - 1)
            d[i] = (diff, 0.75 * diff)
        return d[i]

    def get_q(i):
        if i not in q:
            q[i] = cell(*get_d(i), *get_d(i + 1))
        return q[i]

    def get_t(i):
        if i not in t:
            t[i] = get_q(i)[0] - get_q(i - 1)[0]
        return t[i]

    lower = None
    for j in range(cells + 1):
        lo2, lo1, hi0, hi1 = get_q(j - 2), get_q(j - 1), get_q(j), get_q(j + 1)
        upper = face(
            load_u(j), get_f(j - 1) + get_f(j), lo1[0], hi0[0], get_t(j - 1), get_t(j), get_t(j + 1),
            lo2[3], lo1[3], lo1[2], hi0[2], hi0[1], hi1[1],
        )
        if j > 0:
            emit(j - 1, lower - upper)
        lower = upper


def shifted_z(f, lane):
    below = pltpu.roll(f, 1, 1)
    d = jnp.where(lane == 0, 0.0, f - below)
    return (
        f + below, d, jnp.where(lane == 1, 0.0, pltpu.roll(d, 2, 1)), pltpu.roll(d, 1, 1), pltpu.roll(d, NZ - 1, 1),
        jnp.where(lane == NZ - 1, 0.0, pltpu.roll(d, NZ - 2, 1)),
    )


def flux_z(u, parts, lane):
    total, d3, low2, low1, high1, high2 = parts
    u = jnp.where(lane == 0, 0.0, u)
    pos = u > 0.0
    d1 = jnp.where(pos, low2, high2)
    d2 = jnp.where(pos, low1, high1)
    d4 = jnp.where(pos, high1, low1)
    g0, g1, g2 = d2 - d1, d3 - d2, d4 - d3
    e2, e3 = 0.75 * d2, 0.75 * d3
    b0 = (g0 * g0 + EPS) + e2 * (d2 + g0)
    b1 = (g1 * g1 + EPS) + e3 * d2
    b2 = (g2 * g2 + EPS) + e3 * (d3 - g2)
    b0 = 3.0 * (b0 * b0)
    b1 = b1 * b1
    b2 = b2 * b2
    c2 = b2 + b2
    num = b1 * (c2 * (g1 - g0) + b0 * (g2 - g1))
    den = b1 * (b2 + b0) + b0 * c2
    return u * (3.0 * total) - jnp.abs(u) * (g1 + num * pl.reciprocal(den, approx=True))


def digits(n):
    radix, count = min(4, n), 1
    while radix**count < n:
        count += 1
    return count, radix


def kernel(
    n_x, n_y,
    scal, east, north, upw, diff, target, adv, shift, im, av, cp,
    xf, xh, bs, ys, tz, ty, ex, ny, nraw, uz, kd, tg, fk, es, aro, ari,
    lsem, csem, hsend, hrecv, wsend, wrecv, asend, arecv,
):
    mx, my = lax.axis_index("gx"), lax.axis_index("gy")
    x_up, x_dn = lax.rem(mx + 1, n_x), lax.rem(mx + n_x - 1, n_x)
    y_up, y_dn = lax.rem(my + 1, n_y), lax.rem(my + n_y - 1, n_y)
    per_axis, radix = digits(n_x)
    rounds = 2 * per_axis

    def partner(r, k):
        on_x, stride = 1 - r // per_axis, 1 + (r % per_axis) * (radix - 1)
        me = on_x * mx + (1 - on_x) * my
        digit = lax.rem(lax.div(me, stride), radix)
        other = me + stride * (lax.rem(digit + k, radix) - digit)
        return on_x * other + (1 - on_x) * mx, on_x * my + (1 - on_x) * other

    loads = [
        pltpu.make_async_copy(scal.at[0], xf.at[0], lsem.at[0]),
        pltpu.make_async_copy(scal.at[1], xf.at[1], lsem.at[1]),
        pltpu.make_async_copy(north, nraw, lsem.at[2]),
        pltpu.make_async_copy(east, ex.at[pl.ds(0, CELLS)], lsem.at[3]),
        pltpu.make_async_copy(diff, kd, lsem.at[4]),
        pltpu.make_async_copy(upw, uz, lsem.at[5]),
        pltpu.make_async_copy(target, tg, lsem.at[6]),
        pltpu.make_async_copy(scal, bs, lsem.at[7]),
    ]
    for load in loads:
        load.start()

    barrier = pltpu.get_barrier_semaphore()
    peers = [(x_up, my), (x_dn, my), (mx, y_up), (mx, y_dn)] + [
        partner(r, k) for r in range(rounds) for k in range(1, radix)
    ]
    for peer in peers:
        pl.semaphore_signal(barrier, inc=1, device_id=peer, device_id_type=MESH)

    def halo(t, way, field=adv):
        st, s = lax.div(t, 2), lax.rem(t, 2)
        to = ((x_up, my), (x_dn, my), (mx, y_up), (mx, y_dn))[way]
        if way < 2:
            src, dst = field.at[s, pl.ds((CELLS - H * CY, 0)[way], H * CY)], xh.at[t, way]
        else:
            src = ys.at[st, s, pl.ds((CY, H)[way - 2] * CX, H * CX)]
            dst = ys.at[st, s, pl.ds((0, CY + H)[way - 2] * CX, H * CX)]
        return pltpu.make_async_remote_copy(
            src_ref=src, dst_ref=dst, send_sem=hsend.at[t, way], recv_sem=hrecv.at[t, way],
            device_id=to, device_id_type=MESH,
        )

    def exchange(r):
        return [
            pltpu.make_async_remote_copy(
                src_ref=aro.at[r], dst_ref=ari.at[r, k - 1], send_sem=asend.at[r, k - 1],
                recv_sem=arecv.at[r, k - 1], device_id=partner(r, k), device_id_type=MESH,
            )
            for k in range(1, radix)
        ]

    def send_sums(r):
        for copy in exchange(r):
            copy.start()

    def add_sums(r):
        total = aro[r]
        for k, copy in enumerate(exchange(r)):
            copy.wait_recv()
            total = total + ari[r, k]
        aro[r + 1] = total

    def next_sums(r):
        @pl.when(r < rounds - 1)
        def _():
            add_sums(r)
            send_sums(r + 1)

    east_edge = pltpu.make_async_remote_copy(
        src_ref=ex.at[pl.ds(0, CY)], dst_ref=ex.at[pl.ds(CELLS, CY)], send_sem=wsend.at[0], recv_sem=wrecv.at[0],
        device_id=(x_dn, my), device_id_type=MESH,
    )
    north_edge = pltpu.make_async_remote_copy(
        src_ref=ny.at[pl.ds(0, CX)], dst_ref=ny.at[pl.ds(CELLS, CX)], send_sem=wsend.at[1], recv_sem=wrecv.at[1],
        device_id=(mx, y_dn), device_id_type=MESH,
    )

    def to_y(st, s, x, value):
        for i in range(CY // 8):
            ys[st, s, pl.ds((H + 8 * i) * CX + x, 8, stride=CX), :] = value[8 * i : 8 * i + 8]

    loads[0].wait()
    loads[1].wait()
    pl.semaphore_wait(barrier, len(peers))

    def first_field(s, _):
        halo(s, 0, xf).start()
        halo(s, 1, xf).start()

        def convert(g, total):
            values = [xf[s, pl.ds(pl.multiple_of((g * GROUP + p) * CY, CY), CY), :] for p in range(GROUP)]
            for p, value in enumerate(values):
                to_y(0, s, g * GROUP + p, value)
            return total + sum(values)

        total = lax.fori_loop(0, CX // GROUP, convert, jnp.zeros((CY, NZ), jnp.float32))
        aro[0, pl.ds(s, 1), :] = jnp.sum(total, axis=0, keepdims=True)
        halo(s, 2).start()
        halo(s, 3).start()
        return 0

    lax.fori_loop(0, 2, first_field, 0)
    send_sums(0)

    loads[2].wait()

    def turn_north(g, _):
        values = [nraw[pl.ds(pl.multiple_of((g * GROUP + p) * CY, CY), CY), :] for p in range(GROUP)]
        for p, value in enumerate(values):
            for i in range(CY // 8):
                ny[pl.ds(8 * i * CX + g * GROUP + p, 8, stride=CX), :] = value[8 * i : 8 * i + 8]
        return 0

    lax.fori_loop(0, CX // GROUP, turn_north, 0)
    north_edge.start()
    loads[3].wait()

    east_edge.start()
    loads[5].wait()
    lane = lax.broadcasted_iota(jnp.int32, (8, NZ), 1)

    loads[4].wait()
    loads[6].wait()
    loads[7].wait()

    def columns_to_lanes(c, _):
        rows = pl.ds(pl.multiple_of(c * 128, 128), 128)
        fk[pl.ds(c, NZ, stride=8), :] = jnp.transpose(kd[rows, :]) * STEP
        return 0

    fk[pl.ds(NZ * 8, fk.shape[0] - NZ * 8), :] = jnp.zeros((fk.shape[0] - NZ * 8, 128), jnp.float32)
    lax.fori_loop(0, TILES, columns_to_lanes, 0)
    fk[pl.ds(0, 8), :] = jnp.zeros((8, 128), jnp.float32)
    es[...] = jnp.zeros((8, 128), jnp.float32)

    def factor(first, e):
        base = pl.multiple_of(first * 8, 8)
        low = fk[pl.ds(base, 8), :]
        for i in range(UNROLL):
            row = pl.ds(base + 8 * i, 8)
            above = fk[pl.ds(base + 8 * i + 8, 8), :]
            g = 1.0 + low * e
            inverse = pl.reciprocal(g + above, approx=True)
            e = g * inverse
            im[row, :] = inverse
            av[row, :] = low * inverse
            cp[row, :] = above * inverse
            low = above
        return e

    def y_column(st, s, row):
        def keep(y, diff):
            ty[pl.ds(row * CY + y, 8, stride=CY), :] = diff

        march(
            lambda y: ys[st, s, pl.ds((H + y) * CX + row, 8), :],
            lambda y: ny[pl.ds(y * CX + row, 8), :],
            CY, keep,
        )

    def x_column(st, s, row, coef):
        t = 2 * st + s

        def load(x):
            if x < 0:
                return xh[t, 0, pl.ds((x + H) * CY + row, 8), :]
            if x >= CX:
                return xh[t, 1, pl.ds((x - CX) * CY + row, 8), :]
            return xf[s, pl.ds(x * CY + row, 8), :]

        def keep(x, diff):
            rows = pl.ds(x * CY + row, 8)
            value = bs[s, rows, :] + coef * (diff + ty[rows, :] + tz[s, rows, :])
            adv[s, rows, :] = value
            ys[st + 1, s, pl.ds((H + row) * CX + x, 8, stride=CX), :] = value

        march(load, lambda x: ex[pl.ds(x * CY + row, 8), :], CX, keep)

    def z_faces(s, first):
        rows = [pl.ds(first + 8 * v, 8) for v in range(ZROWS // 8)]
        parts = [shifted_z(xf[s, pl.ds(first + 8 * v, 8), :], lane) for v in range(ZROWS // 8)]
        flux = [flux_z(uz[r, :], part, lane) for r, part in zip(rows, parts)]
        for r, value in zip(rows, flux):
            tz[s, r, :] = value - pltpu.roll(value, NZ - 1, 1)

    def back(s):
        return pltpu.make_async_copy(adv.at[s], xf.at[s], csem.at[s])

    def stage(st, _):
        coef = jnp.where(st == 0, STEP / 18.0, jnp.where(st == 1, STEP / 12.0, STEP / 6.0)).astype(jnp.float32)

        def z_pass(s, _):
            @pl.when(st > 0)
            def _():
                back(s).wait()

            def group(i, _):
                z_faces(s, pl.multiple_of(i * ZROWS, ZROWS))
                return 0

            lax.fori_loop(0, CELLS // ZROWS, group, 0)
            return 0

        lax.fori_loop(0, 2, z_pass, 0)

        next_sums(2 * st)

        @pl.when(st == 0)
        def _():
            north_edge.wait_recv()
            east_edge.wait_recv()

        def finish(s, _):
            t = 2 * st + s

            def y_pass(i, _):
                y_column(st, s, pl.multiple_of(i * 8, 8))
                return 0

            def x_pass(i, e):
                x_column(st, s, pl.multiple_of(i * 8, 8), coef)
                return factor(st * PART + (s * (CY // 8) + i) * UNROLL, e)

            halo(t, 2).wait_recv()
            halo(t, 3).wait_recv()
            lax.fori_loop(0, CX // 8, y_pass, 0)
            for way in range(2):
                halo(t, way).wait_recv()
                halo(t, way).wait_send()
            es[...] = lax.fori_loop(0, CY // 8, x_pass, es[...])

            @pl.when(st < 2)
            def _():
                for way in (2, 3, 0, 1):
                    halo(t + 2, way).start()
                back(s).start()

            return 0

        lax.fori_loop(0, 2, finish, 0)
        next_sums(2 * st + 1)
        return 0

    lax.fori_loop(0, 3, stage, 0)

    add_sums(rounds - 1)
    cells = float(n_x * CX * n_y * CY)
    shift[...] = RELAX * (aro[rounds] * (1.0 / cells) - tg[...])

    def drain(t, _):
        for way in (2, 3):
            halo(t, way).wait_send()
        return 0

    lax.fori_loop(0, 6, drain, 0)

    for r in range(rounds):
        for copy in exchange(r):
            copy.wait_send()
    east_edge.wait_send()
    north_edge.wait_send()


def solve(adv, shift, im, av, cp, out, rh, ob, osem):
    for s in range(2):
        for c in range(TILES):
            value = adv[s, pl.ds(c * 128, 128), :] - shift[s : s + 1, :]
            rh[s, pl.ds(c, NZ, stride=8), :] = jnp.transpose(value)

    zero = jnp.zeros((8, 128), jnp.float32)

    def forward(k8, carry):
        d0, d1 = carry
        base = pl.multiple_of(k8 * (TURN * 8), TURN * 8)
        rows = [pl.ds(base + 8 * i, 8) for i in range(TURN)]
        data = [(im[r, :], av[r, :], rh[0, r, :], rh[1, r, :]) for r in rows]
        for i, (inverse, a, r0, r1) in enumerate(data):
            d0 = r0 * inverse + a * d0
            d1 = r1 * inverse + a * d1
            rh[0, rows[i], :] = d0
            rh[1, rows[i], :] = d1
        return d0, d1

    lax.fori_loop(0, NZ // TURN, forward, (zero, zero))

    def backward(j8, carry):
        v0, v1 = carry
        base = pl.multiple_of((NZ // TURN - 1 - j8) * (TURN * 8), TURN * 8)
        rows = [pl.ds(base + 8 * (TURN - 1 - i), 8) for i in range(TURN)]
        data = [(cp[r, :], rh[0, r, :], rh[1, r, :]) for r in rows]
        for i, (c, r0, r1) in enumerate(data):
            v0 = r0 + c * v0
            v1 = r1 + c * v1
            rh[0, rows[i], :] = v0
            rh[1, rows[i], :] = v1
        return v0, v1

    lax.fori_loop(0, NZ // TURN, backward, (zero, zero))
    stores = []
    for s in range(2):
        for c in range(TILES):
            rows = pl.ds(c * 128, 128)
            ob[s, rows, :] = jnp.transpose(rh[s, pl.ds(c, NZ, stride=8), :])
            store = pltpu.make_async_copy(ob.at[s, rows], out.at[s, rows], osem.at[s, c])
            store.start()
            stores.append(store)
    for store in stores:
        store.wait()


def in_hbm(value):
    return pltpu.with_memory_space_constraint(value, pltpu.HBM)


def body(n_x, n_y, scalars, east_wind, north_wind, up_wind, diffusivity, target_profile):
    rounds = 2 * digits(n_x)[0]
    hbm = pl.BlockSpec(memory_space=pltpu.HBM)
    f32 = jnp.float32
    vmem = pltpu.VMEM
    dma = pltpu.SemaphoreType.DMA
    resident = pl.BlockSpec(memory_space=pltpu.VMEM)
    columns = jax.ShapeDtypeStruct((LEVELS * 8, 128), f32)
    parts = pl.pallas_call(
        functools.partial(kernel, n_x, n_y),
        out_shape=[
            jax.ShapeDtypeStruct((2, CELLS, NZ), f32), jax.ShapeDtypeStruct((2, NZ), f32), columns, columns, columns,
        ],
        in_specs=[hbm] * 6,
        out_specs=[resident] * 5,
        scratch_shapes=[
            vmem((2, CELLS, NZ), f32),
            vmem((6, 2, H * CY, NZ), f32),
            vmem((2, CELLS, NZ), f32),
            vmem((4, 2, YROWS, NZ), f32),
            vmem((2, CELLS, NZ), f32),
            vmem((CELLS, NZ), f32),
            vmem((CELLS + CY, NZ), f32),
            vmem((CELLS + CX, NZ), f32),
            vmem((CELLS, NZ), f32),
            vmem((CELLS, NZ), f32),
            vmem((CELLS, NZ), f32),
            vmem((2, NZ), f32),
            vmem(((LEVELS + 1) * 8, 128), f32),
            vmem((8, 128), f32),
            vmem((rounds + 1, 2, NZ), f32),
            vmem((rounds, 3, 2, NZ), f32),
            dma((8,)),
            dma((2,)),
            dma((6, 4)),
            dma((6, 4)),
            dma((2,)),
            dma((2,)),
            dma((rounds, 3)),
            dma((rounds, 3)),
        ],
        compiler_params=pltpu.CompilerParams(
            collective_id=0, has_side_effects=True, vmem_limit_bytes=48 * 1024 * 1024
        ),
        cost_estimate=pl.CostEstimate(flops=80_000_000, bytes_accessed=4_000_000, transcendentals=0),
    )(
        in_hbm(scalars.reshape(2, CELLS, NZ)),
        in_hbm(east_wind.reshape(CELLS, NZ)),
        in_hbm(north_wind.reshape(CELLS, NZ)),
        in_hbm(up_wind.reshape(CELLS, NZ)),
        in_hbm(diffusivity.reshape(CELLS, NZ)),
        in_hbm(target_profile),
    )
    result = pl.pallas_call(
        solve,
        out_shape=jax.ShapeDtypeStruct((2, CELLS, NZ), f32),
        in_specs=[resident] * 5,
        out_specs=hbm,
        scratch_shapes=[
            vmem((2, NZ * 8, 128), f32),
            vmem((2, CELLS, NZ), f32),
            dma((2, TILES)),
        ],
        compiler_params=pltpu.CompilerParams(vmem_limit_bytes=32 * 1024 * 1024),
        cost_estimate=pl.CostEstimate(flops=2_000_000, bytes_accessed=4_000_000, transcendentals=0),
    )(*parts)
    return result.reshape(2, CX, CY, NZ)


def solution(mesh):
    placed = (
        P(None, "gx", "gy", None),
        P("gx", "gy", None),
        P("gx", "gy", None),
        P("gx", "gy", None),
        P("gx", "gy", None),
        P(),
    )
    return jax.shard_map(
        functools.partial(body, mesh.shape["gx"], mesh.shape["gy"]),
        mesh=mesh, in_specs=placed, out_specs=P(None, "gx", "gy", None), check_vma=False,
    )
```

```python
import functools

import jax
import jax.numpy as jnp
from jax import lax
from jax.experimental import pallas as pl
from jax.experimental.pallas import tpu as pltpu
from jax.sharding import PartitionSpec as P

STEP = 0.3
RELAX = 0.5
EPSILON = 1e-06
EPS = 0.75 * EPSILON
EPS2 = EPS * EPS

CX, CY, NZ = 24, 32, 128
H = 3
YROWS = (CY + 2 * H) * CX
CELLS = CX * CY
TILES = CELLS // 128
GROUP = 8
ZROWS = 192
TURN = 16
PART = 48
LEVELS = 3 * PART
UNROLL = PART // 8
MESH = pl.DeviceIdType.MESH


def cell(dm, em, dp, ep):
    g = dp - dm
    b = (g * g + EPS) + ep * dm
    g2 = g + g
    left = b - g2 * em
    right = b + g2 * ep
    return g, left * left, b * b, right * right


def face(u, total, g_low, g_high, t_low, t_mid, t_high, r2, r1, c1, c0, l0, l1):
    pos = u > 0.0
    b0 = jnp.where(pos, r2, l1)
    b1 = jnp.where(pos, c1, c0)
    b2 = jnp.where(pos, l0, r1)
    gs = jnp.where(pos, g_low, g_high)
    ts = jnp.where(pos, t_low, t_high)
    b0 = 3.0 * b0
    c2 = b2 + b2
    num = b1 * (c2 * ts + b0 * t_mid)
    den = b1 * (b2 + b0) + b0 * c2
    part = num * pl.reciprocal(den, approx=True)
    return u * (3.0 * total - gs) - jnp.abs(u) * part


def march(load_f, load_u, cells, emit):
    f, d, q, t = {}, {}, {}, {}

    def get_f(i):
        if i not in f:
            f[i] = load_f(i)
        return f[i]

    def get_d(i):
        if i not in d:
            diff = get_f(i) - get_f(i - 1)
            d[i] = (diff, 0.75 * diff)
        return d[i]

    def get_q(i):
        if i not in q:
            q[i] = cell(*get_d(i), *get_d(i + 1))
        return q[i]

    def get_t(i):
        if i not in t:
            t[i] = get_q(i)[0] - get_q(i - 1)[0]
        return t[i]

    lower = None
    for j in range(cells + 1):
        lo2, lo1, hi0, hi1 = get_q(j - 2), get_q(j - 1), get_q(j), get_q(j + 1)
        upper = face(
            load_u(j), get_f(j - 1) + get_f(j), lo1[0], hi0[0], get_t(j - 1), get_t(j), get_t(j + 1),
            lo2[3], lo1[3], lo1[2], hi0[2], hi0[1], hi1[1],
        )
        if j > 0:
            emit(j - 1, lower - upper)
        lower = upper


def shifted_z(f, lane):
    below = pltpu.roll(f, 1, 1)
    d = jnp.where(lane == 0, 0.0, f - below)
    return (
        f + below, d, jnp.where(lane == 1, 0.0, pltpu.roll(d, 2, 1)), pltpu.roll(d, 1, 1), pltpu.roll(d, NZ - 1, 1),
        jnp.where(lane == NZ - 1, 0.0, pltpu.roll(d, NZ - 2, 1)),
    )


def flux_z(u, parts, lane):
    total, d3, low2, low1, high1, high2 = parts
    u = jnp.where(lane == 0, 0.0, u)
    pos = u > 0.0
    d1 = jnp.where(pos, low2, high2)
    d2 = jnp.where(pos, low1, high1)
    d4 = jnp.where(pos, high1, low1)
    g0, g1, g2 = d2 - d1, d3 - d2, d4 - d3
    e2, e3 = 0.75 * d2, 0.75 * d3
    b0 = (g0 * g0 + EPS) + e2 * (d2 + g0)
    b1 = (g1 * g1 + EPS) + e3 * d2
    b2 = (g2 * g2 + EPS) + e3 * (d3 - g2)
    b0 = 3.0 * (b0 * b0)
    b1 = b1 * b1
    b2 = b2 * b2
    c2 = b2 + b2
    num = b1 * (c2 * (g1 - g0) + b0 * (g2 - g1))
    den = b1 * (b2 + b0) + b0 * c2
    return u * (3.0 * total) - jnp.abs(u) * (g1 + num * pl.reciprocal(den, approx=True))


def digits(n):
    out, stride = [], 1
    while stride < n:
        out.append((stride, min(4, n // stride)))
        stride *= out[-1][1]
    return out


def kernel(
    n_x, n_y,
    scal, east, north, upw, diff, target, adv, shift, im, av, cp,
    xf, xh, bs, ys, tz, ty, ex, ny, nraw, uz, kd, tg, fk, es, aro, ari,
    lsem, csem, hsend, hrecv, wsend, wrecv, asend, arecv,
):
    mx, my = lax.axis_index("gx"), lax.axis_index("gy")
    x_up, x_dn = lax.rem(mx + 1, n_x), lax.rem(mx + n_x - 1, n_x)
    y_up, y_dn = lax.rem(my + 1, n_y), lax.rem(my + n_y - 1, n_y)
    plan = digits(n_x) + [(1, n_y)]
    rounds = len(plan)

    def partner(r, k):
        stride, size = plan[r]
        me = my if r == rounds - 1 else mx
        digit = lax.rem(lax.div(me, stride), size)
        other = me + stride * (lax.rem(digit + k, size) - digit)
        return (mx, other) if r == rounds - 1 else (other, my)

    def for_peers(r, work):
        def one(k, _):
            work(k)
            return 0

        lax.fori_loop(1, plan[r][1], one, 0)

    loads = [
        pltpu.make_async_copy(scal.at[0], xf.at[0], lsem.at[0]),
        pltpu.make_async_copy(scal.at[1], xf.at[1], lsem.at[1]),
        pltpu.make_async_copy(north, nraw, lsem.at[2]),
        pltpu.make_async_copy(east, ex.at[pl.ds(0, CELLS)], lsem.at[3]),
        pltpu.make_async_copy(diff, kd, lsem.at[4]),
        pltpu.make_async_copy(upw, uz, lsem.at[5]),
        pltpu.make_async_copy(target, tg, lsem.at[6]),
        pltpu.make_async_copy(scal, bs, lsem.at[7]),
    ]
    for load in loads:
        load.start()

    barrier = pltpu.get_barrier_semaphore()
    peers = [(x_up, my), (x_dn, my), (mx, y_up), (mx, y_dn)] + [
        partner(r, k) for r in range(rounds - 1) for k in range(1, plan[r][1])
    ]
    def greet(peer):
        pl.semaphore_signal(barrier, inc=1, device_id=peer, device_id_type=MESH)

    for peer in peers:
        greet(peer)
    for_peers(rounds - 1, lambda k: greet(partner(rounds - 1, k)))

    def halo(t, way, field=adv):
        st, s = lax.div(t, 2), lax.rem(t, 2)
        to = ((x_up, my), (x_dn, my), (mx, y_up), (mx, y_dn))[way]
        if way < 2:
            src, dst = field.at[s, pl.ds((CELLS - H * CY, 0)[way], H * CY)], xh.at[t, way]
        else:
            src = ys.at[st, s, pl.ds((CY, H)[way - 2] * CX, H * CX)]
            dst = ys.at[st, s, pl.ds((0, CY + H)[way - 2] * CX, H * CX)]
        return pltpu.make_async_remote_copy(
            src_ref=src, dst_ref=dst, send_sem=hsend.at[t, way], recv_sem=hrecv.at[t, way],
            device_id=to, device_id_type=MESH,
        )

    def exchange(r, k):
        return pltpu.make_async_remote_copy(
            src_ref=aro.at[r], dst_ref=ari.at[r, k - 1], send_sem=asend.at[r, k - 1],
            recv_sem=arecv.at[r, k - 1], device_id=partner(r, k), device_id_type=MESH,
        )

    def send_sums(r):
        for_peers(r, lambda k: exchange(r, k).start())

    def add_sums(r):
        def add(k, total):
            exchange(r, k).wait_recv()
            return total + ari[r, k - 1]

        aro[r + 1] = lax.fori_loop(1, plan[r][1], add, aro[r])

    east_edge = pltpu.make_async_remote_copy(
        src_ref=ex.at[pl.ds(0, CY)], dst_ref=ex.at[pl.ds(CELLS, CY)], send_sem=wsend.at[0], recv_sem=wrecv.at[0],
        device_id=(x_dn, my), device_id_type=MESH,
    )
    north_edge = pltpu.make_async_remote_copy(
        src_ref=ny.at[pl.ds(0, CX)], dst_ref=ny.at[pl.ds(CELLS, CX)], send_sem=wsend.at[1], recv_sem=wrecv.at[1],
        device_id=(mx, y_dn), device_id_type=MESH,
    )

    def to_y(st, s, x, value):
        for i in range(CY // 8):
            ys[st, s, pl.ds((H + 8 * i) * CX + x, 8, stride=CX), :] = value[8 * i : 8 * i + 8]

    loads[0].wait()
    loads[1].wait()
    pl.semaphore_wait(barrier, len(peers) + n_y - 1)

    def first_field(s, _):
        halo(s, 0, xf).start()
        halo(s, 1, xf).start()

        def convert(g, total):
            values = [xf[s, pl.ds(pl.multiple_of((g * GROUP + p) * CY, CY), CY), :] for p in range(GROUP)]
            for p, value in enumerate(values):
                to_y(0, s, g * GROUP + p, value)
            return total + sum(values)

        total = lax.fori_loop(0, CX // GROUP, convert, jnp.zeros((CY, NZ), jnp.float32))
        aro[0, pl.ds(s, 1), :] = jnp.sum(total, axis=0, keepdims=True)
        halo(s, 2).start()
        halo(s, 3).start()
        return 0

    lax.fori_loop(0, 2, first_field, 0)
    send_sums(0)

    loads[2].wait()

    def turn_north(g, _):
        values = [nraw[pl.ds(pl.multiple_of((g * GROUP + p) * CY, CY), CY), :] for p in range(GROUP)]
        for p, value in enumerate(values):
            for i in range(CY // 8):
                ny[pl.ds(8 * i * CX + g * GROUP + p, 8, stride=CX), :] = value[8 * i : 8 * i + 8]
        return 0

    lax.fori_loop(0, CX // GROUP, turn_north, 0)
    north_edge.start()
    loads[3].wait()

    east_edge.start()
    loads[5].wait()
    lane = lax.broadcasted_iota(jnp.int32, (8, NZ), 1)

    loads[4].wait()
    loads[6].wait()
    loads[7].wait()

    def columns_to_lanes(c, _):
        rows = pl.ds(pl.multiple_of(c * 128, 128), 128)
        fk[pl.ds(c, NZ, stride=8), :] = jnp.transpose(kd[rows, :]) * STEP
        return 0

    fk[pl.ds(NZ * 8, fk.shape[0] - NZ * 8), :] = jnp.zeros((fk.shape[0] - NZ * 8, 128), jnp.float32)
    lax.fori_loop(0, TILES, columns_to_lanes, 0)
    fk[pl.ds(0, 8), :] = jnp.zeros((8, 128), jnp.float32)
    es[...] = jnp.zeros((8, 128), jnp.float32)

    def factor(first, e):
        base = pl.multiple_of(first * 8, 8)
        low = fk[pl.ds(base, 8), :]
        for i in range(UNROLL):
            row = pl.ds(base + 8 * i, 8)
            above = fk[pl.ds(base + 8 * i + 8, 8), :]
            g = 1.0 + low * e
            inverse = pl.reciprocal(g + above, approx=True)
            e = g * inverse
            im[row, :] = inverse
            av[row, :] = low * inverse
            cp[row, :] = above * inverse
            low = above
        return e

    def y_column(st, s, row):
        def keep(y, diff):
            ty[pl.ds(row * CY + y, 8, stride=CY), :] = diff

        march(
            lambda y: ys[st, s, pl.ds((H + y) * CX + row, 8), :],
            lambda y: ny[pl.ds(y * CX + row, 8), :],
            CY, keep,
        )

    def x_column(st, s, row, coef):
        t = 2 * st + s

        def load(x):
            if x < 0:
                return xh[t, 0, pl.ds((x + H) * CY + row, 8), :]
            if x >= CX:
                return xh[t, 1, pl.ds((x - CX) * CY + row, 8), :]
            return xf[s, pl.ds(x * CY + row, 8), :]

        def keep(x, diff):
            rows = pl.ds(x * CY + row, 8)
            value = bs[s, rows, :] + coef * (diff + ty[rows, :] + tz[s, rows, :])
            adv[s, rows, :] = value
            ys[st + 1, s, pl.ds((H + row) * CX + x, 8, stride=CX), :] = value

        march(load, lambda x: ex[pl.ds(x * CY + row, 8), :], CX, keep)

    def z_faces(s, first):
        rows = [pl.ds(first + 8 * v, 8) for v in range(ZROWS // 8)]
        parts = [shifted_z(xf[s, pl.ds(first + 8 * v, 8), :], lane) for v in range(ZROWS // 8)]
        flux = [flux_z(uz[r, :], part, lane) for r, part in zip(rows, parts)]
        for r, value in zip(rows, flux):
            tz[s, r, :] = value - pltpu.roll(value, NZ - 1, 1)

    def back(s):
        return pltpu.make_async_copy(adv.at[s], xf.at[s], csem.at[s])

    def stage(st, _):
        coef = jnp.where(st == 0, STEP / 18.0, jnp.where(st == 1, STEP / 12.0, STEP / 6.0)).astype(jnp.float32)

        def z_pass(s, _):
            @pl.when(st > 0)
            def _():
                back(s).wait()

            def group(i, _):
                z_faces(s, pl.multiple_of(i * ZROWS, ZROWS))
                return 0

            lax.fori_loop(0, CELLS // ZROWS, group, 0)
            return 0

        lax.fori_loop(0, 2, z_pass, 0)

        for r in range(rounds - 1):

            @pl.when(st == r)
            def _(r=r):
                add_sums(r)
                send_sums(r + 1)

        @pl.when(st == 0)
        def _():
            north_edge.wait_recv()
            east_edge.wait_recv()

        def finish(s, _):
            t = 2 * st + s

            def y_pass(i, _):
                y_column(st, s, pl.multiple_of(i * 8, 8))
                return 0

            def x_pass(i, e):
                x_column(st, s, pl.multiple_of(i * 8, 8), coef)
                return factor(st * PART + (s * (CY // 8) + i) * UNROLL, e)

            halo(t, 2).wait_recv()
            halo(t, 3).wait_recv()
            lax.fori_loop(0, CX // 8, y_pass, 0)
            for way in range(2):
                halo(t, way).wait_recv()
                halo(t, way).wait_send()
            es[...] = lax.fori_loop(0, CY // 8, x_pass, es[...])

            @pl.when(st < 2)
            def _():
                for way in (2, 3, 0, 1):
                    halo(t + 2, way).start()
                back(s).start()

            return 0

        lax.fori_loop(0, 2, finish, 0)
        return 0

    lax.fori_loop(0, 3, stage, 0)

    add_sums(rounds - 1)
    cells = float(n_x * CX * n_y * CY)
    shift[...] = RELAX * (aro[rounds] * (1.0 / cells) - tg[...])

    def drain(t, _):
        for way in (2, 3):
            halo(t, way).wait_send()
        return 0

    lax.fori_loop(0, 6, drain, 0)

    for r in range(rounds):
        for_peers(r, lambda k, r=r: exchange(r, k).wait_send())
    east_edge.wait_send()
    north_edge.wait_send()


def solve(adv, shift, im, av, cp, out, rh, ob, osem):
    for s in range(2):
        for c in range(TILES):
            value = adv[s, pl.ds(c * 128, 128), :] - shift[s : s + 1, :]
            rh[s, pl.ds(c, NZ, stride=8), :] = jnp.transpose(value)

    zero = jnp.zeros((8, 128), jnp.float32)

    def forward(k8, carry):
        d0, d1 = carry
        base = pl.multiple_of(k8 * (TURN * 8), TURN * 8)
        rows = [pl.ds(base + 8 * i, 8) for i in range(TURN)]
        data = [(im[r, :], av[r, :], rh[0, r, :], rh[1, r, :]) for r in rows]
        for i, (inverse, a, r0, r1) in enumerate(data):
            d0 = r0 * inverse + a * d0
            d1 = r1 * inverse + a * d1
            rh[0, rows[i], :] = d0
            rh[1, rows[i], :] = d1
        return d0, d1

    lax.fori_loop(0, NZ // TURN, forward, (zero, zero))

    def backward(j8, carry):
        v0, v1 = carry
        base = pl.multiple_of((NZ // TURN - 1 - j8) * (TURN * 8), TURN * 8)
        rows = [pl.ds(base + 8 * (TURN - 1 - i), 8) for i in range(TURN)]
        data = [(cp[r, :], rh[0, r, :], rh[1, r, :]) for r in rows]
        for i, (c, r0, r1) in enumerate(data):
            v0 = r0 + c * v0
            v1 = r1 + c * v1
            rh[0, rows[i], :] = v0
            rh[1, rows[i], :] = v1
        return v0, v1

    lax.fori_loop(0, NZ // TURN, backward, (zero, zero))
    stores = []
    for s in range(2):
        for c in range(TILES):
            rows = pl.ds(c * 128, 128)
            ob[s, rows, :] = jnp.transpose(rh[s, pl.ds(c, NZ, stride=8), :])
            store = pltpu.make_async_copy(ob.at[s, rows], out.at[s, rows], osem.at[s, c])
            store.start()
            stores.append(store)
    for store in stores:
        store.wait()


def in_hbm(value):
    return pltpu.with_memory_space_constraint(value, pltpu.HBM)


def body(n_x, n_y, scalars, east_wind, north_wind, up_wind, diffusivity, target_profile):
    rounds = len(digits(n_x)) + 1
    hbm = pl.BlockSpec(memory_space=pltpu.HBM)
    f32 = jnp.float32
    vmem = pltpu.VMEM
    dma = pltpu.SemaphoreType.DMA
    resident = pl.BlockSpec(memory_space=pltpu.VMEM)
    columns = jax.ShapeDtypeStruct((LEVELS * 8, 128), f32)
    parts = pl.pallas_call(
        functools.partial(kernel, n_x, n_y),
        out_shape=[
            jax.ShapeDtypeStruct((2, CELLS, NZ), f32), jax.ShapeDtypeStruct((2, NZ), f32), columns, columns, columns,
        ],
        in_specs=[hbm] * 6,
        out_specs=[resident] * 5,
        scratch_shapes=[
            vmem((2, CELLS, NZ), f32),
            vmem((6, 2, H * CY, NZ), f32),
            vmem((2, CELLS, NZ), f32),
            vmem((4, 2, YROWS, NZ), f32),
            vmem((2, CELLS, NZ), f32),
            vmem((CELLS, NZ), f32),
            vmem((CELLS + CY, NZ), f32),
            vmem((CELLS + CX, NZ), f32),
            vmem((CELLS, NZ), f32),
            vmem((CELLS, NZ), f32),
            vmem((CELLS, NZ), f32),
            vmem((2, NZ), f32),
            vmem(((LEVELS + 1) * 8, 128), f32),
            vmem((8, 128), f32),
            vmem((rounds + 1, 2, NZ), f32),
            vmem((rounds, n_y - 1, 2, NZ), f32),
            dma((8,)),
            dma((2,)),
            dma((6, 4)),
            dma((6, 4)),
            dma((2,)),
            dma((2,)),
            dma((rounds, n_y - 1)),
            dma((rounds, n_y - 1)),
        ],
        compiler_params=pltpu.CompilerParams(
            collective_id=0, has_side_effects=True, vmem_limit_bytes=48 * 1024 * 1024
        ),
        cost_estimate=pl.CostEstimate(flops=80_000_000, bytes_accessed=4_000_000, transcendentals=0),
    )(
        in_hbm(scalars.reshape(2, CELLS, NZ)),
        in_hbm(east_wind.reshape(CELLS, NZ)),
        in_hbm(north_wind.reshape(CELLS, NZ)),
        in_hbm(up_wind.reshape(CELLS, NZ)),
        in_hbm(diffusivity.reshape(CELLS, NZ)),
        in_hbm(target_profile),
    )
    result = pl.pallas_call(
        solve,
        out_shape=jax.ShapeDtypeStruct((2, CELLS, NZ), f32),
        in_specs=[resident] * 5,
        out_specs=hbm,
        scratch_shapes=[
            vmem((2, NZ * 8, 128), f32),
            vmem((2, CELLS, NZ), f32),
            dma((2, TILES)),
        ],
        compiler_params=pltpu.CompilerParams(vmem_limit_bytes=32 * 1024 * 1024),
        cost_estimate=pl.CostEstimate(flops=2_000_000, bytes_accessed=4_000_000, transcendentals=0),
    )(*parts)
    return result.reshape(2, CX, CY, NZ)


def solution(mesh):
    placed = (
        P(None, "gx", "gy", None),
        P("gx", "gy", None),
        P("gx", "gy", None),
        P("gx", "gy", None),
        P("gx", "gy", None),
        P(),
    )
    return jax.shard_map(
        functools.partial(body, mesh.shape["gx"], mesh.shape["gy"]),
        mesh=mesh, in_specs=placed, out_specs=P(None, "gx", "gy", None), check_vma=False,
    )
```

```python
import functools

import jax
import jax.numpy as jnp
from jax import lax
from jax.experimental import pallas as pl
from jax.experimental.pallas import tpu as pltpu
from jax.sharding import PartitionSpec as P

STEP = 0.3
RELAX = 0.5
EPSILON = 1e-06
EPS = 0.75 * EPSILON
EPS2 = EPS * EPS

CX, CY, NZ = 24, 32, 128
H = 3
YROWS = (CY + 2 * H) * CX
CELLS = CX * CY
TILES = CELLS // 128
GROUP = 8
ZROWS = 192
TURN = 16
PART = 48
LEVELS = 3 * PART
UNROLL = PART // 8
MESH = pl.DeviceIdType.MESH


def cell(dm, em, dp, ep):
    g = dp - dm
    b = (g * g + EPS) + ep * dm
    g2 = g + g
    left = b - g2 * em
    right = b + g2 * ep
    return g, left * left, b * b, right * right


def face(u, total, g_low, g_high, t_low, t_mid, t_high, r2, r1, c1, c0, l0, l1):
    pos = u > 0.0
    b0 = jnp.where(pos, r2, l1)
    b1 = jnp.where(pos, c1, c0)
    b2 = jnp.where(pos, l0, r1)
    gs = jnp.where(pos, g_low, g_high)
    ts = jnp.where(pos, t_low, t_high)
    b0 = 3.0 * b0
    c2 = b2 + b2
    num = b1 * (c2 * ts + b0 * t_mid)
    den = b1 * (b2 + b0) + b0 * c2
    part = num * pl.reciprocal(den, approx=True)
    return u * (3.0 * total - gs) - jnp.abs(u) * part


def march(load_f, load_u, cells, emit):
    f, d, q, t = {}, {}, {}, {}

    def get_f(i):
        if i not in f:
            f[i] = load_f(i)
        return f[i]

    def get_d(i):
        if i not in d:
            diff = get_f(i) - get_f(i - 1)
            d[i] = (diff, 0.75 * diff)
        return d[i]

    def get_q(i):
        if i not in q:
            q[i] = cell(*get_d(i), *get_d(i + 1))
        return q[i]

    def get_t(i):
        if i not in t:
            t[i] = get_q(i)[0] - get_q(i - 1)[0]
        return t[i]

    lower = None
    for j in range(cells + 1):
        lo2, lo1, hi0, hi1 = get_q(j - 2), get_q(j - 1), get_q(j), get_q(j + 1)
        upper = face(
            load_u(j), get_f(j - 1) + get_f(j), lo1[0], hi0[0], get_t(j - 1), get_t(j), get_t(j + 1),
            lo2[3], lo1[3], lo1[2], hi0[2], hi0[1], hi1[1],
        )
        if j > 0:
            emit(j - 1, lower - upper)
        lower = upper


def shifted_z(f, lane):
    below = pltpu.roll(f, 1, 1)
    d = jnp.where(lane == 0, 0.0, f - below)
    return (
        f + below, d, jnp.where(lane == 1, 0.0, pltpu.roll(d, 2, 1)), pltpu.roll(d, 1, 1), pltpu.roll(d, NZ - 1, 1),
        jnp.where(lane == NZ - 1, 0.0, pltpu.roll(d, NZ - 2, 1)),
    )


def flux_z(u, parts, lane):
    total, d3, low2, low1, high1, high2 = parts
    u = jnp.where(lane == 0, 0.0, u)
    pos = u > 0.0
    d1 = jnp.where(pos, low2, high2)
    d2 = jnp.where(pos, low1, high1)
    d4 = jnp.where(pos, high1, low1)
    g0, g1, g2 = d2 - d1, d3 - d2, d4 - d3
    e2, e3 = 0.75 * d2, 0.75 * d3
    b0 = (g0 * g0 + EPS) + e2 * (d2 + g0)
    b1 = (g1 * g1 + EPS) + e3 * d2
    b2 = (g2 * g2 + EPS) + e3 * (d3 - g2)
    b0 = 3.0 * (b0 * b0)
    b1 = b1 * b1
    b2 = b2 * b2
    c2 = b2 + b2
    num = b1 * (c2 * (g1 - g0) + b0 * (g2 - g1))
    den = b1 * (b2 + b0) + b0 * c2
    return u * (3.0 * total) - jnp.abs(u) * (g1 + num * pl.reciprocal(den, approx=True))


def digits(n):
    out, stride = [], 1
    while stride < n:
        radix = min(4, n // stride)
        out.append((stride, radix))
        stride *= radix
    return out


def kernel(
    n_x, n_y,
    scal, east, north, upw, diff, target, adv, shift, im, av, cp,
    xf, xh, bs, ys, tz, ty, ex, ny, nraw, uz, kd, tg, fk, es, aro, ari,
    lsem, csem, hsend, hrecv, wsend, wrecv, asend, arecv,
):
    mx, my = lax.axis_index("gx"), lax.axis_index("gy")
    x_up, x_dn = lax.rem(mx + 1, n_x), lax.rem(mx + n_x - 1, n_x)
    y_up, y_dn = lax.rem(my + 1, n_y), lax.rem(my + n_y - 1, n_y)
    plan = [("x", d) for d in digits(n_x)] + [("y", d) for d in digits(n_y)]
    rounds = len(plan)

    def partner(r, k):
        axis, (stride, radix) = plan[r]
        me = mx if axis == "x" else my
        digit = lax.rem(lax.div(me, stride), radix)
        other = me + stride * (lax.rem(digit + k, radix) - digit)
        return (other, my) if axis == "x" else (mx, other)

    loads = [
        pltpu.make_async_copy(scal.at[0], xf.at[0], lsem.at[0]),
        pltpu.make_async_copy(scal.at[1], xf.at[1], lsem.at[1]),
        pltpu.make_async_copy(north, nraw, lsem.at[2]),
        pltpu.make_async_copy(east, ex.at[pl.ds(0, CELLS)], lsem.at[3]),
        pltpu.make_async_copy(diff, kd, lsem.at[4]),
        pltpu.make_async_copy(upw, uz, lsem.at[5]),
        pltpu.make_async_copy(target, tg, lsem.at[6]),
        pltpu.make_async_copy(scal, bs, lsem.at[7]),
    ]
    for load in loads:
        load.start()

    barrier = pltpu.get_barrier_semaphore()
    peers = [(x_up, my), (x_dn, my), (mx, y_up), (mx, y_dn)] + [
        partner(r, k) for r in range(rounds) for k in range(1, plan[r][1][1])
    ]
    for peer in peers:
        pl.semaphore_signal(barrier, inc=1, device_id=peer, device_id_type=MESH)

    def halo(t, way, field=adv):
        st, s = lax.div(t, 2), lax.rem(t, 2)
        to = ((x_up, my), (x_dn, my), (mx, y_up), (mx, y_dn))[way]
        if way < 2:
            src, dst = field.at[s, pl.ds((CELLS - H * CY, 0)[way], H * CY)], xh.at[t, way]
        else:
            src = ys.at[st, s, pl.ds((CY, H)[way - 2] * CX, H * CX)]
            dst = ys.at[st, s, pl.ds((0, CY + H)[way - 2] * CX, H * CX)]
        return pltpu.make_async_remote_copy(
            src_ref=src, dst_ref=dst, send_sem=hsend.at[t, way], recv_sem=hrecv.at[t, way],
            device_id=to, device_id_type=MESH,
        )

    def exchange(r):
        return [
            pltpu.make_async_remote_copy(
                src_ref=aro.at[r], dst_ref=ari.at[r, k - 1], send_sem=asend.at[r, k - 1],
                recv_sem=arecv.at[r, k - 1], device_id=partner(r, k), device_id_type=MESH,
            )
            for k in range(1, plan[r][1][1])
        ]

    def send_sums(r):
        for copy in exchange(r):
            copy.start()

    def add_sums(r):
        total = aro[r]
        for k, copy in enumerate(exchange(r)):
            copy.wait_recv()
            total = total + ari[r, k]
        aro[r + 1] = total

    east_edge = pltpu.make_async_remote_copy(
        src_ref=ex.at[pl.ds(0, CY)], dst_ref=ex.at[pl.ds(CELLS, CY)], send_sem=wsend.at[0], recv_sem=wrecv.at[0],
        device_id=(x_dn, my), device_id_type=MESH,
    )
    north_edge = pltpu.make_async_remote_copy(
        src_ref=ny.at[pl.ds(0, CX)], dst_ref=ny.at[pl.ds(CELLS, CX)], send_sem=wsend.at[1], recv_sem=wrecv.at[1],
        device_id=(mx, y_dn), device_id_type=MESH,
    )

    def to_y(st, s, x, value):
        for i in range(CY // 8):
            ys[st, s, pl.ds((H + 8 * i) * CX + x, 8, stride=CX), :] = value[8 * i : 8 * i + 8]

    loads[0].wait()
    loads[1].wait()
    pl.semaphore_wait(barrier, len(peers))

    def first_field(s, _):
        halo(s, 0, xf).start()
        halo(s, 1, xf).start()

        def convert(g, total):
            values = [xf[s, pl.ds(pl.multiple_of((g * GROUP + p) * CY, CY), CY), :] for p in range(GROUP)]
            for p, value in enumerate(values):
                to_y(0, s, g * GROUP + p, value)
            return total + sum(values)

        total = lax.fori_loop(0, CX // GROUP, convert, jnp.zeros((CY, NZ), jnp.float32))
        aro[0, pl.ds(s, 1), :] = jnp.sum(total, axis=0, keepdims=True)
        halo(s, 2).start()
        halo(s, 3).start()
        return 0

    lax.fori_loop(0, 2, first_field, 0)
    send_sums(0)

    loads[2].wait()

    def turn_north(g, _):
        values = [nraw[pl.ds(pl.multiple_of((g * GROUP + p) * CY, CY), CY), :] for p in range(GROUP)]
        for p, value in enumerate(values):
            for i in range(CY // 8):
                ny[pl.ds(8 * i * CX + g * GROUP + p, 8, stride=CX), :] = value[8 * i : 8 * i + 8]
        return 0

    lax.fori_loop(0, CX // GROUP, turn_north, 0)
    north_edge.start()
    loads[3].wait()

    east_edge.start()
    loads[5].wait()
    lane = lax.broadcasted_iota(jnp.int32, (8, NZ), 1)

    loads[4].wait()
    loads[6].wait()
    loads[7].wait()

    def columns_to_lanes(c, _):
        rows = pl.ds(pl.multiple_of(c * 128, 128), 128)
        fk[pl.ds(c, NZ, stride=8), :] = jnp.transpose(kd[rows, :]) * STEP
        return 0

    fk[pl.ds(NZ * 8, fk.shape[0] - NZ * 8), :] = jnp.zeros((fk.shape[0] - NZ * 8, 128), jnp.float32)
    lax.fori_loop(0, TILES, columns_to_lanes, 0)
    fk[pl.ds(0, 8), :] = jnp.zeros((8, 128), jnp.float32)
    es[...] = jnp.zeros((8, 128), jnp.float32)

    def factor(first, e):
        base = pl.multiple_of(first * 8, 8)
        low = fk[pl.ds(base, 8), :]
        for i in range(UNROLL):
            row = pl.ds(base + 8 * i, 8)
            above = fk[pl.ds(base + 8 * i + 8, 8), :]
            g = 1.0 + low * e
            inverse = pl.reciprocal(g + above, approx=True)
            e = g * inverse
            im[row, :] = inverse
            av[row, :] = low * inverse
            cp[row, :] = above * inverse
            low = above
        return e

    def y_column(st, s, row):
        def keep(y, diff):
            ty[pl.ds(row * CY + y, 8, stride=CY), :] = diff

        march(
            lambda y: ys[st, s, pl.ds((H + y) * CX + row, 8), :],
            lambda y: ny[pl.ds(y * CX + row, 8), :],
            CY, keep,
        )

    def x_column(st, s, row, coef):
        t = 2 * st + s

        def load(x):
            if x < 0:
                return xh[t, 0, pl.ds((x + H) * CY + row, 8), :]
            if x >= CX:
                return xh[t, 1, pl.ds((x - CX) * CY + row, 8), :]
            return xf[s, pl.ds(x * CY + row, 8), :]

        def keep(x, diff):
            rows = pl.ds(x * CY + row, 8)
            value = bs[s, rows, :] + coef * (diff + ty[rows, :] + tz[s, rows, :])
            adv[s, rows, :] = value
            ys[st + 1, s, pl.ds((H + row) * CX + x, 8, stride=CX), :] = value

        march(load, lambda x: ex[pl.ds(x * CY + row, 8), :], CX, keep)

    def z_faces(s, first):
        rows = [pl.ds(first + 8 * v, 8) for v in range(ZROWS // 8)]
        parts = [shifted_z(xf[s, pl.ds(first + 8 * v, 8), :], lane) for v in range(ZROWS // 8)]
        flux = [flux_z(uz[r, :], part, lane) for r, part in zip(rows, parts)]
        for r, value in zip(rows, flux):
            tz[s, r, :] = value - pltpu.roll(value, NZ - 1, 1)

    def back(s):
        return pltpu.make_async_copy(adv.at[s], xf.at[s], csem.at[s])

    def stage(st, _):
        coef = jnp.where(st == 0, STEP / 18.0, jnp.where(st == 1, STEP / 12.0, STEP / 6.0)).astype(jnp.float32)

        def z_pass(s, _):
            @pl.when(st > 0)
            def _():
                back(s).wait()

            def group(i, _):
                z_faces(s, pl.multiple_of(i * ZROWS, ZROWS))
                return 0

            lax.fori_loop(0, CELLS // ZROWS, group, 0)
            return 0

        lax.fori_loop(0, 2, z_pass, 0)

        for r in range(rounds - 1):

            @pl.when(st == r)
            def _(r=r):
                add_sums(r)
                send_sums(r + 1)

        @pl.when(st == 0)
        def _():
            north_edge.wait_recv()
            east_edge.wait_recv()

        def finish(s, _):
            t = 2 * st + s

            def y_pass(i, _):
                y_column(st, s, pl.multiple_of(i * 8, 8))
                return 0

            def x_pass(i, e):
                x_column(st, s, pl.multiple_of(i * 8, 8), coef)
                return factor(st * PART + (s * (CY // 8) + i) * UNROLL, e)

            halo(t, 2).wait_recv()
            halo(t, 3).wait_recv()
            lax.fori_loop(0, CX // 8, y_pass, 0)
            for way in range(2):
                halo(t, way).wait_recv()
                halo(t, way).wait_send()
            es[...] = lax.fori_loop(0, CY // 8, x_pass, es[...])

            @pl.when(st < 2)
            def _():
                for way in range(4):
                    halo(t + 2, way).start()
                back(s).start()

            return 0

        lax.fori_loop(0, 2, finish, 0)
        return 0

    lax.fori_loop(0, 3, stage, 0)

    add_sums(rounds - 1)
    cells = float(n_x * CX * n_y * CY)
    shift[...] = RELAX * (aro[rounds] * (1.0 / cells) - tg[...])

    def drain(t, _):
        for way in (2, 3):
            halo(t, way).wait_send()
        return 0

    lax.fori_loop(0, 6, drain, 0)

    for r in range(rounds):
        for copy in exchange(r):
            copy.wait_send()
    east_edge.wait_send()
    north_edge.wait_send()


def solve(adv, shift, im, av, cp, out, rh, ob, osem):
    for s in range(2):
        for c in range(TILES):
            value = adv[s, pl.ds(c * 128, 128), :] - shift[s : s + 1, :]
            rh[s, pl.ds(c, NZ, stride=8), :] = jnp.transpose(value)

    zero = jnp.zeros((8, 128), jnp.float32)

    def forward(k8, carry):
        d0, d1 = carry
        base = pl.multiple_of(k8 * (TURN * 8), TURN * 8)
        rows = [pl.ds(base + 8 * i, 8) for i in range(TURN)]
        data = [(im[r, :], av[r, :], rh[0, r, :], rh[1, r, :]) for r in rows]
        for i, (inverse, a, r0, r1) in enumerate(data):
            d0 = r0 * inverse + a * d0
            d1 = r1 * inverse + a * d1
            rh[0, rows[i], :] = d0
            rh[1, rows[i], :] = d1
        return d0, d1

    lax.fori_loop(0, NZ // TURN, forward, (zero, zero))

    def backward(j8, carry):
        v0, v1 = carry
        base = pl.multiple_of((NZ // TURN - 1 - j8) * (TURN * 8), TURN * 8)
        rows = [pl.ds(base + 8 * (TURN - 1 - i), 8) for i in range(TURN)]
        data = [(cp[r, :], rh[0, r, :], rh[1, r, :]) for r in rows]
        for i, (c, r0, r1) in enumerate(data):
            v0 = r0 + c * v0
            v1 = r1 + c * v1
            rh[0, rows[i], :] = v0
            rh[1, rows[i], :] = v1
        return v0, v1

    lax.fori_loop(0, NZ // TURN, backward, (zero, zero))
    stores = []
    for s in range(2):
        for c in range(TILES):
            rows = pl.ds(c * 128, 128)
            ob[s, rows, :] = jnp.transpose(rh[s, pl.ds(c, NZ, stride=8), :])
            store = pltpu.make_async_copy(ob.at[s, rows], out.at[s, rows], osem.at[s, c])
            store.start()
            stores.append(store)
    for store in stores:
        store.wait()


def in_hbm(value):
    return pltpu.with_memory_space_constraint(value, pltpu.HBM)


def body(n_x, n_y, scalars, east_wind, north_wind, up_wind, diffusivity, target_profile):
    rounds = len(digits(n_x)) + len(digits(n_y))
    hbm = pl.BlockSpec(memory_space=pltpu.HBM)
    f32 = jnp.float32
    vmem = pltpu.VMEM
    dma = pltpu.SemaphoreType.DMA
    resident = pl.BlockSpec(memory_space=pltpu.VMEM)
    columns = jax.ShapeDtypeStruct((LEVELS * 8, 128), f32)
    parts = pl.pallas_call(
        functools.partial(kernel, n_x, n_y),
        out_shape=[
            jax.ShapeDtypeStruct((2, CELLS, NZ), f32), jax.ShapeDtypeStruct((2, NZ), f32), columns, columns, columns,
        ],
        in_specs=[hbm] * 6,
        out_specs=[resident] * 5,
        scratch_shapes=[
            vmem((2, CELLS, NZ), f32),
            vmem((6, 2, H * CY, NZ), f32),
            vmem((2, CELLS, NZ), f32),
            vmem((4, 2, YROWS, NZ), f32),
            vmem((2, CELLS, NZ), f32),
            vmem((CELLS, NZ), f32),
            vmem((CELLS + CY, NZ), f32),
            vmem((CELLS + CX, NZ), f32),
            vmem((CELLS, NZ), f32),
            vmem((CELLS, NZ), f32),
            vmem((CELLS, NZ), f32),
            vmem((2, NZ), f32),
            vmem(((LEVELS + 1) * 8, 128), f32),
            vmem((8, 128), f32),
            vmem((rounds + 1, 2, NZ), f32),
            vmem((rounds, 3, 2, NZ), f32),
            dma((8,)),
            dma((2,)),
            dma((6, 4)),
            dma((6, 4)),
            dma((2,)),
            dma((2,)),
            dma((rounds, 3)),
            dma((rounds, 3)),
        ],
        compiler_params=pltpu.CompilerParams(
            collective_id=0, has_side_effects=True, vmem_limit_bytes=48 * 1024 * 1024
        ),
        cost_estimate=pl.CostEstimate(flops=80_000_000, bytes_accessed=4_000_000, transcendentals=0),
    )(
        in_hbm(scalars.reshape(2, CELLS, NZ)),
        in_hbm(east_wind.reshape(CELLS, NZ)),
        in_hbm(north_wind.reshape(CELLS, NZ)),
        in_hbm(up_wind.reshape(CELLS, NZ)),
        in_hbm(diffusivity.reshape(CELLS, NZ)),
        in_hbm(target_profile),
    )
    result = pl.pallas_call(
        solve,
        out_shape=jax.ShapeDtypeStruct((2, CELLS, NZ), f32),
        in_specs=[resident] * 5,
        out_specs=hbm,
        scratch_shapes=[
            vmem((2, NZ * 8, 128), f32),
            vmem((2, CELLS, NZ), f32),
            dma((2, TILES)),
        ],
        compiler_params=pltpu.CompilerParams(vmem_limit_bytes=32 * 1024 * 1024),
        cost_estimate=pl.CostEstimate(flops=2_000_000, bytes_accessed=4_000_000, transcendentals=0),
    )(*parts)
    return result.reshape(2, CX, CY, NZ)


def solution(mesh):
    placed = (
        P(None, "gx", "gy", None),
        P("gx", "gy", None),
        P("gx", "gy", None),
        P("gx", "gy", None),
        P("gx", "gy", None),
        P(),
    )
    return jax.shard_map(
        functools.partial(body, mesh.shape["gx"], mesh.shape["gy"]),
        mesh=mesh, in_specs=placed, out_specs=P(None, "gx", "gy", None), check_vma=False,
    )
```

```python
import functools

import jax
import jax.numpy as jnp
from jax import lax
from jax.experimental import pallas as pl
from jax.experimental.pallas import tpu as pltpu
from jax.sharding import PartitionSpec as P

STEP = 0.3
RELAX = 0.5
EPSILON = 1e-06
EPS = 0.75 * EPSILON
EPS2 = EPS * EPS

CX, CY, NZ = 24, 32, 128
H = 3
YROWS = (CY + 2 * H) * CX
CELLS = CX * CY
TILES = CELLS // 128
GROUP = 8
ZROWS = 192
TURN = 16
PART = 48
LEVELS = 3 * PART
UNROLL = PART // 8
MESH = pl.DeviceIdType.MESH


def cell(dm, em, dp, ep):
    g = dp - dm
    b = (g * g + EPS) + ep * dm
    g2 = g + g
    left = b - g2 * em
    right = b + g2 * ep
    return g, left * left, b * b, right * right


def face(u, total, g_low, g_high, t_low, t_mid, t_high, r2, r1, c1, c0, l0, l1):
    pos = u > 0.0
    b0 = jnp.where(pos, r2, l1)
    b1 = jnp.where(pos, c1, c0)
    b2 = jnp.where(pos, l0, r1)
    gs = jnp.where(pos, g_low, g_high)
    ts = jnp.where(pos, t_low, t_high)
    b0 = 3.0 * b0
    c2 = b2 + b2
    num = b1 * (c2 * ts + b0 * t_mid)
    den = b1 * (b2 + b0) + b0 * c2
    part = num * pl.reciprocal(den, approx=True)
    return u * (3.0 * total - gs) - jnp.abs(u) * part


def march(load_f, load_u, cells, emit):
    f, d, q, t = {}, {}, {}, {}

    def get_f(i):
        if i not in f:
            f[i] = load_f(i)
        return f[i]

    def get_d(i):
        if i not in d:
            diff = get_f(i) - get_f(i - 1)
            d[i] = (diff, 0.75 * diff)
        return d[i]

    def get_q(i):
        if i not in q:
            q[i] = cell(*get_d(i), *get_d(i + 1))
        return q[i]

    def get_t(i):
        if i not in t:
            t[i] = get_q(i)[0] - get_q(i - 1)[0]
        return t[i]

    lower = None
    for j in range(cells + 1):
        lo2, lo1, hi0, hi1 = get_q(j - 2), get_q(j - 1), get_q(j), get_q(j + 1)
        upper = face(
            load_u(j), get_f(j - 1) + get_f(j), lo1[0], hi0[0], get_t(j - 1), get_t(j), get_t(j + 1),
            lo2[3], lo1[3], lo1[2], hi0[2], hi0[1], hi1[1],
        )
        if j > 0:
            emit(j - 1, lower - upper)
        lower = upper


def shifted_z(f, lane):
    below = pltpu.roll(f, 1, 1)
    d = jnp.where(lane == 0, 0.0, f - below)
    return (
        f + below, d, jnp.where(lane == 1, 0.0, pltpu.roll(d, 2, 1)), pltpu.roll(d, 1, 1), pltpu.roll(d, NZ - 1, 1),
        jnp.where(lane == NZ - 1, 0.0, pltpu.roll(d, NZ - 2, 1)),
    )


def flux_z(u, parts, lane):
    total, d3, low2, low1, high1, high2 = parts
    u = jnp.where(lane == 0, 0.0, u)
    pos = u > 0.0
    d1 = jnp.where(pos, low2, high2)
    d2 = jnp.where(pos, low1, high1)
    d4 = jnp.where(pos, high1, low1)
    g0, g1, g2 = d2 - d1, d3 - d2, d4 - d3
    e2, e3 = 0.75 * d2, 0.75 * d3
    b0 = (g0 * g0 + EPS) + e2 * (d2 + g0)
    b1 = (g1 * g1 + EPS) + e3 * d2
    b2 = (g2 * g2 + EPS) + e3 * (d3 - g2)
    b0 = 3.0 * (b0 * b0)
    b1 = b1 * b1
    b2 = b2 * b2
    c2 = b2 + b2
    num = b1 * (c2 * (g1 - g0) + b0 * (g2 - g1))
    den = b1 * (b2 + b0) + b0 * c2
    return u * (3.0 * total) - jnp.abs(u) * (g1 + num * pl.reciprocal(den, approx=True))


def digits(n):
    radix, count = min(4, n), 1
    while radix**count < n:
        count += 1
    return count, radix


def kernel(
    n_x, n_y,
    scal, east, north, upw, diff, target, adv, shift, im, av, cp,
    xf, xh, bs, ys, tz, ty, ex, ny, nraw, uz, kd, tg, fk, es, aro, ari,
    lsem, csem, hsend, hrecv, wsend, wrecv, asend, arecv,
):
    mx, my = lax.axis_index("gx"), lax.axis_index("gy")
    x_up, x_dn = lax.rem(mx + 1, n_x), lax.rem(mx + n_x - 1, n_x)
    y_up, y_dn = lax.rem(my + 1, n_y), lax.rem(my + n_y - 1, n_y)
    per_axis, radix = digits(n_x)
    rounds = 2 * per_axis

    def partner(r, k):
        on_x, stride = 1 - r // per_axis, 1 + (r % per_axis) * (radix - 1)
        me = on_x * mx + (1 - on_x) * my
        digit = lax.rem(lax.div(me, stride), radix)
        other = me + stride * (lax.rem(digit + k, radix) - digit)
        return on_x * other + (1 - on_x) * mx, on_x * my + (1 - on_x) * other

    loads = [
        pltpu.make_async_copy(scal.at[0], xf.at[0], lsem.at[0]),
        pltpu.make_async_copy(scal.at[1], xf.at[1], lsem.at[1]),
        pltpu.make_async_copy(north, nraw, lsem.at[2]),
        pltpu.make_async_copy(east, ex.at[pl.ds(0, CELLS)], lsem.at[3]),
        pltpu.make_async_copy(diff, kd, lsem.at[4]),
        pltpu.make_async_copy(upw, uz, lsem.at[5]),
        pltpu.make_async_copy(target, tg, lsem.at[6]),
        pltpu.make_async_copy(scal, bs, lsem.at[7]),
    ]
    for load in loads:
        load.start()

    barrier = pltpu.get_barrier_semaphore()
    peers = [(x_up, my), (x_dn, my), (mx, y_up), (mx, y_dn)] + [
        partner(r, k) for r in range(rounds) for k in range(1, radix)
    ]
    for peer in peers:
        pl.semaphore_signal(barrier, inc=1, device_id=peer, device_id_type=MESH)

    def halo(t, way, field=adv, row=None):
        st, s = lax.div(t, 2), lax.rem(t, 2)
        to = ((x_up, my), (x_dn, my), (mx, y_up), (mx, y_dn))[way]
        if way < 2:
            rows = pl.ds(0, CY) if row is None else pl.ds(row, 8)
            src, dst = field.at[s, pl.ds((CX - H, 0)[way], H), rows], xh.at[t, way, :, rows]
        else:
            src = ys.at[st, s, pl.ds((CY, H)[way - 2] * CX, H * CX)]
            dst = ys.at[st, s, pl.ds((0, CY + H)[way - 2] * CX, H * CX)]
        return pltpu.make_async_remote_copy(
            src_ref=src, dst_ref=dst, send_sem=hsend.at[t, way], recv_sem=hrecv.at[t, way],
            device_id=to, device_id_type=MESH,
        )

    def exchange(r):
        return [
            pltpu.make_async_remote_copy(
                src_ref=aro.at[r], dst_ref=ari.at[r, k - 1], send_sem=asend.at[r, k - 1],
                recv_sem=arecv.at[r, k - 1], device_id=partner(r, k), device_id_type=MESH,
            )
            for k in range(1, radix)
        ]

    def send_sums(r):
        for copy in exchange(r):
            copy.start()

    def add_sums(r):
        total = aro[r]
        for k, copy in enumerate(exchange(r)):
            copy.wait_recv()
            total = total + ari[r, k]
        aro[r + 1] = total

    east_edge = pltpu.make_async_remote_copy(
        src_ref=ex.at[pl.ds(0, CY)], dst_ref=ex.at[pl.ds(CELLS, CY)], send_sem=wsend.at[0], recv_sem=wrecv.at[0],
        device_id=(x_dn, my), device_id_type=MESH,
    )
    north_edge = pltpu.make_async_remote_copy(
        src_ref=ny.at[pl.ds(0, CX)], dst_ref=ny.at[pl.ds(CELLS, CX)], send_sem=wsend.at[1], recv_sem=wrecv.at[1],
        device_id=(mx, y_dn), device_id_type=MESH,
    )

    def to_y(st, s, x, value):
        for i in range(CY // 8):
            ys[st, s, pl.ds((H + 8 * i) * CX + x, 8, stride=CX), :] = value[8 * i : 8 * i + 8]

    loads[0].wait()
    loads[1].wait()
    pl.semaphore_wait(barrier, len(peers))

    def first_field(s, _):
        halo(s, 0, xf).start()
        halo(s, 1, xf).start()

        def convert(g, total):
            values = [xf[s, g * GROUP + p] for p in range(GROUP)]
            for p, value in enumerate(values):
                to_y(0, s, g * GROUP + p, value)
            return total + sum(values)

        total = lax.fori_loop(0, CX // GROUP, convert, jnp.zeros((CY, NZ), jnp.float32))
        aro[0, pl.ds(s, 1), :] = jnp.sum(total, axis=0, keepdims=True)
        halo(s, 2).start()
        halo(s, 3).start()
        return 0

    lax.fori_loop(0, 2, first_field, 0)
    send_sums(0)

    loads[2].wait()

    def turn_north(g, _):
        values = [nraw[pl.ds(pl.multiple_of((g * GROUP + p) * CY, CY), CY), :] for p in range(GROUP)]
        for p, value in enumerate(values):
            for i in range(CY // 8):
                ny[pl.ds(8 * i * CX + g * GROUP + p, 8, stride=CX), :] = value[8 * i : 8 * i + 8]
        return 0

    lax.fori_loop(0, CX // GROUP, turn_north, 0)
    north_edge.start()
    loads[3].wait()

    east_edge.start()
    loads[5].wait()
    lane = lax.broadcasted_iota(jnp.int32, (8, NZ), 1)

    loads[4].wait()
    loads[6].wait()
    loads[7].wait()

    def columns_to_lanes(c, _):
        rows = pl.ds(pl.multiple_of(c * 128, 128), 128)
        fk[pl.ds(c, NZ, stride=8), :] = jnp.transpose(kd[rows, :]) * STEP
        return 0

    fk[pl.ds(NZ * 8, fk.shape[0] - NZ * 8), :] = jnp.zeros((fk.shape[0] - NZ * 8, 128), jnp.float32)
    lax.fori_loop(0, TILES, columns_to_lanes, 0)
    fk[pl.ds(0, 8), :] = jnp.zeros((8, 128), jnp.float32)
    es[...] = jnp.zeros((8, 128), jnp.float32)

    def factor(first, e):
        base = pl.multiple_of(first * 8, 8)
        low = fk[pl.ds(base, 8), :]
        for i in range(UNROLL):
            row = pl.ds(base + 8 * i, 8)
            above = fk[pl.ds(base + 8 * i + 8, 8), :]
            g = 1.0 + low * e
            inverse = pl.reciprocal(g + above, approx=True)
            e = g * inverse
            im[row, :] = inverse
            av[row, :] = low * inverse
            cp[row, :] = above * inverse
            low = above
        return e

    def y_column(st, s, row):
        def keep(y, diff):
            ty[pl.ds(row * CY + y, 8, stride=CY), :] = diff

        march(
            lambda y: ys[st, s, pl.ds((H + y) * CX + row, 8), :],
            lambda y: ny[pl.ds(y * CX + row, 8), :],
            CY, keep,
        )

    def x_column(st, s, row, coef):
        t = 2 * st + s

        def load(x):
            if x < 0:
                return xh[t, 0, x + H, pl.ds(row, 8), :]
            if x >= CX:
                return xh[t, 1, x - CX, pl.ds(row, 8), :]
            return xf[s, x, pl.ds(row, 8), :]

        def keep(x, diff):
            rows = pl.ds(x * CY + row, 8)
            value = bs[s, x, pl.ds(row, 8), :] + coef * (diff + ty[rows, :] + tz[s, rows, :])
            adv[s, x, pl.ds(row, 8), :] = value
            ys[st + 1, s, pl.ds((H + row) * CX + x, 8, stride=CX), :] = value

        march(load, lambda x: ex[pl.ds(x * CY + row, 8), :], CX, keep)

    def z_faces(s, group):
        planes = ZROWS // CY
        x = [group * planes + v // (CY // 8) for v in range(ZROWS // 8)]
        rows = [pl.ds(pl.multiple_of(group * ZROWS, ZROWS) + 8 * v, 8) for v in range(ZROWS // 8)]
        parts = [shifted_z(xf[s, x[v], pl.ds(8 * v % CY, 8), :], lane) for v in range(ZROWS // 8)]
        flux = [flux_z(uz[r, :], part, lane) for r, part in zip(rows, parts)]
        for r, value in zip(rows, flux):
            tz[s, r, :] = value - pltpu.roll(value, NZ - 1, 1)

    def back(s):
        return pltpu.make_async_copy(adv.at[s], xf.at[s], csem.at[s])

    def stage(st, _):
        coef = jnp.where(st == 0, STEP / 18.0, jnp.where(st == 1, STEP / 12.0, STEP / 6.0)).astype(jnp.float32)

        def z_pass(s, _):
            @pl.when(st > 0)
            def _():
                back(s).wait()

            def group(i, _):
                z_faces(s, i)
                return 0

            lax.fori_loop(0, CELLS // ZROWS, group, 0)
            return 0

        lax.fori_loop(0, 2, z_pass, 0)

        @pl.when(st < rounds - 1)
        def _():
            add_sums(st)
            send_sums(st + 1)

        @pl.when(st == 0)
        def _():
            north_edge.wait_recv()
            east_edge.wait_recv()

        def finish(s, _):
            t = 2 * st + s

            def y_pass(i, _):
                y_column(st, s, pl.multiple_of(i * 8, 8))
                return 0

            def x_pass(i, e):
                row = pl.multiple_of(i * 8, 8)
                x_column(st, s, row, coef)
                e = factor(st * PART + (s * (CY // 8) + i) * UNROLL, e)

                @pl.when(st < 2)
                def _():
                    halo(t + 2, 0, row=row).start()
                    halo(t + 2, 1, row=row).start()

                    @pl.when(i == 0)
                    def _():
                        halo(t + 2, 3).start()

                    @pl.when(i == CY // 8 - 1)
                    def _():
                        halo(t + 2, 2).start()

                return e

            halo(t, 2).wait_recv()
            halo(t, 3).wait_recv()
            lax.fori_loop(0, CX // 8, y_pass, 0)
            for way in range(2):
                halo(t, way).wait_recv()
                halo(t, way).wait_send()
            es[...] = lax.fori_loop(0, CY // 8, x_pass, es[...])

            @pl.when(st < 2)
            def _():
                back(s).start()

            return 0

        lax.fori_loop(0, 2, finish, 0)
        return 0

    lax.fori_loop(0, 3, stage, 0)

    add_sums(rounds - 1)
    cells = float(n_x * CX * n_y * CY)
    shift[...] = RELAX * (aro[rounds] * (1.0 / cells) - tg[...])

    def drain(t, _):
        for way in (2, 3):
            halo(t, way).wait_send()
        return 0

    lax.fori_loop(0, 6, drain, 0)

    for r in range(rounds):
        for copy in exchange(r):
            copy.wait_send()
    east_edge.wait_send()
    north_edge.wait_send()


def solve(adv, shift, im, av, cp, out, rh, ob, osem):
    for s in range(2):
        for c in range(TILES):
            value = adv[s, pl.ds(c * 128, 128), :] - shift[s : s + 1, :]
            rh[s, pl.ds(c, NZ, stride=8), :] = jnp.transpose(value)

    zero = jnp.zeros((8, 128), jnp.float32)

    def forward(k8, carry):
        d0, d1 = carry
        base = pl.multiple_of(k8 * (TURN * 8), TURN * 8)
        rows = [pl.ds(base + 8 * i, 8) for i in range(TURN)]
        data = [(im[r, :], av[r, :], rh[0, r, :], rh[1, r, :]) for r in rows]
        for i, (inverse, a, r0, r1) in enumerate(data):
            d0 = r0 * inverse + a * d0
            d1 = r1 * inverse + a * d1
            rh[0, rows[i], :] = d0
            rh[1, rows[i], :] = d1
        return d0, d1

    lax.fori_loop(0, NZ // TURN, forward, (zero, zero))

    def backward(j8, carry):
        v0, v1 = carry
        base = pl.multiple_of((NZ // TURN - 1 - j8) * (TURN * 8), TURN * 8)
        rows = [pl.ds(base + 8 * (TURN - 1 - i), 8) for i in range(TURN)]
        data = [(cp[r, :], rh[0, r, :], rh[1, r, :]) for r in rows]
        for i, (c, r0, r1) in enumerate(data):
            v0 = r0 + c * v0
            v1 = r1 + c * v1
            rh[0, rows[i], :] = v0
            rh[1, rows[i], :] = v1
        return v0, v1

    lax.fori_loop(0, NZ // TURN, backward, (zero, zero))
    stores = []
    for s in range(2):
        for c in range(TILES):
            rows = pl.ds(c * 128, 128)
            ob[s, rows, :] = jnp.transpose(rh[s, pl.ds(c, NZ, stride=8), :])
            store = pltpu.make_async_copy(ob.at[s, rows], out.at[s, rows], osem.at[s, c])
            store.start()
            stores.append(store)
    for store in stores:
        store.wait()


def in_hbm(value):
    return pltpu.with_memory_space_constraint(value, pltpu.HBM)


def body(n_x, n_y, scalars, east_wind, north_wind, up_wind, diffusivity, target_profile):
    rounds = 2 * digits(n_x)[0]
    hbm = pl.BlockSpec(memory_space=pltpu.HBM)
    f32 = jnp.float32
    vmem = pltpu.VMEM
    dma = pltpu.SemaphoreType.DMA
    resident = pl.BlockSpec(memory_space=pltpu.VMEM)
    columns = jax.ShapeDtypeStruct((LEVELS * 8, 128), f32)
    parts = pl.pallas_call(
        functools.partial(kernel, n_x, n_y),
        out_shape=[
            jax.ShapeDtypeStruct((2, CX, CY, NZ), f32), jax.ShapeDtypeStruct((2, NZ), f32), columns, columns, columns,
        ],
        in_specs=[hbm] * 6,
        out_specs=[resident] * 5,
        scratch_shapes=[
            vmem((2, CX, CY, NZ), f32),
            vmem((6, 2, H, CY, NZ), f32),
            vmem((2, CX, CY, NZ), f32),
            vmem((4, 2, YROWS, NZ), f32),
            vmem((2, CELLS, NZ), f32),
            vmem((CELLS, NZ), f32),
            vmem((CELLS + CY, NZ), f32),
            vmem((CELLS + CX, NZ), f32),
            vmem((CELLS, NZ), f32),
            vmem((CELLS, NZ), f32),
            vmem((CELLS, NZ), f32),
            vmem((2, NZ), f32),
            vmem(((LEVELS + 1) * 8, 128), f32),
            vmem((8, 128), f32),
            vmem((rounds + 1, 2, NZ), f32),
            vmem((rounds, 3, 2, NZ), f32),
            dma((8,)),
            dma((2,)),
            dma((6, 4)),
            dma((6, 4)),
            dma((2,)),
            dma((2,)),
            dma((rounds, 3)),
            dma((rounds, 3)),
        ],
        compiler_params=pltpu.CompilerParams(
            collective_id=0, has_side_effects=True, vmem_limit_bytes=48 * 1024 * 1024
        ),
        cost_estimate=pl.CostEstimate(flops=80_000_000, bytes_accessed=4_000_000, transcendentals=0),
    )(
        in_hbm(scalars),
        in_hbm(east_wind.reshape(CELLS, NZ)),
        in_hbm(north_wind.reshape(CELLS, NZ)),
        in_hbm(up_wind.reshape(CELLS, NZ)),
        in_hbm(diffusivity.reshape(CELLS, NZ)),
        in_hbm(target_profile),
    )
    result = pl.pallas_call(
        solve,
        out_shape=jax.ShapeDtypeStruct((2, CELLS, NZ), f32),
        in_specs=[resident] * 5,
        out_specs=hbm,
        scratch_shapes=[
            vmem((2, NZ * 8, 128), f32),
            vmem((2, CELLS, NZ), f32),
            dma((2, TILES)),
        ],
        compiler_params=pltpu.CompilerParams(vmem_limit_bytes=32 * 1024 * 1024),
        cost_estimate=pl.CostEstimate(flops=2_000_000, bytes_accessed=4_000_000, transcendentals=0),
    )(parts[0].reshape(2, CELLS, NZ), *parts[1:])
    return result.reshape(2, CX, CY, NZ)


def solution(mesh):
    placed = (
        P(None, "gx", "gy", None),
        P("gx", "gy", None),
        P("gx", "gy", None),
        P("gx", "gy", None),
        P("gx", "gy", None),
        P(),
    )
    return jax.shard_map(
        functools.partial(body, mesh.shape["gx"], mesh.shape["gy"]),
        mesh=mesh, in_specs=placed, out_specs=P(None, "gx", "gy", None), check_vma=False,
    )
```

```python
import functools

import jax
import jax.numpy as jnp
from jax import lax
from jax.experimental import pallas as pl
from jax.experimental.pallas import tpu as pltpu
from jax.sharding import PartitionSpec as P

STEP = 0.3
RELAX = 0.5
EPSILON = 1e-06
EPS = 0.75 * EPSILON
EPS2 = EPS * EPS

CX, CY, NZ = 24, 32, 128
H = 3
YROWS = (CY + 2 * H) * CX
CELLS = CX * CY
TILES = CELLS // 128
GROUP = 8
ZROWS = 192
TURN = 16
PART = 48
LEVELS = 3 * PART
UNROLL = PART // 8
MESH = pl.DeviceIdType.MESH


def cell(dm, em, dp, ep):
    g = dp - dm
    b = (g * g + EPS) + ep * dm
    g2 = g + g
    left = b - g2 * em
    right = b + g2 * ep
    return g, left * left, b * b, right * right


def face(u, total, g_low, g_high, t_low, t_mid, t_high, r2, r1, c1, c0, l0, l1):
    pos = u > 0.0
    b0 = jnp.where(pos, r2, l1)
    b1 = jnp.where(pos, c1, c0)
    b2 = jnp.where(pos, l0, r1)
    gs = jnp.where(pos, g_low, g_high)
    ts = jnp.where(pos, t_low, t_high)
    b0 = 3.0 * b0
    c2 = b2 + b2
    num = b1 * (c2 * ts + b0 * t_mid)
    den = b1 * (b2 + b0) + b0 * c2
    part = num * pl.reciprocal(den, approx=True)
    return u * (3.0 * total - gs) - jnp.abs(u) * part


def march(load_f, load_u, cells, emit):
    f, d, q, t = {}, {}, {}, {}

    def get_f(i):
        if i not in f:
            f[i] = load_f(i)
        return f[i]

    def get_d(i):
        if i not in d:
            diff = get_f(i) - get_f(i - 1)
            d[i] = (diff, 0.75 * diff)
        return d[i]

    def get_q(i):
        if i not in q:
            q[i] = cell(*get_d(i), *get_d(i + 1))
        return q[i]

    def get_t(i):
        if i not in t:
            t[i] = get_q(i)[0] - get_q(i - 1)[0]
        return t[i]

    lower = None
    for j in range(cells + 1):
        lo2, lo1, hi0, hi1 = get_q(j - 2), get_q(j - 1), get_q(j), get_q(j + 1)
        upper = face(
            load_u(j), get_f(j - 1) + get_f(j), lo1[0], hi0[0], get_t(j - 1), get_t(j), get_t(j + 1),
            lo2[3], lo1[3], lo1[2], hi0[2], hi0[1], hi1[1],
        )
        if j > 0:
            emit(j - 1, lower - upper)
        lower = upper


def shifted_z(f, lane):
    below = pltpu.roll(f, 1, 1)
    d = jnp.where(lane == 0, 0.0, f - below)
    return (
        f + below, d, jnp.where(lane == 1, 0.0, pltpu.roll(d, 2, 1)), pltpu.roll(d, 1, 1), pltpu.roll(d, NZ - 1, 1),
        jnp.where(lane == NZ - 1, 0.0, pltpu.roll(d, NZ - 2, 1)),
    )


def flux_z(u, parts, lane):
    total, d3, low2, low1, high1, high2 = parts
    u = jnp.where(lane == 0, 0.0, u)
    pos = u > 0.0
    d1 = jnp.where(pos, low2, high2)
    d2 = jnp.where(pos, low1, high1)
    d4 = jnp.where(pos, high1, low1)
    g0, g1, g2 = d2 - d1, d3 - d2, d4 - d3
    e2, e3 = 0.75 * d2, 0.75 * d3
    b0 = (g0 * g0 + EPS) + e2 * (d2 + g0)
    b1 = (g1 * g1 + EPS) + e3 * d2
    b2 = (g2 * g2 + EPS) + e3 * (d3 - g2)
    b0 = 3.0 * (b0 * b0)
    b1 = b1 * b1
    b2 = b2 * b2
    c2 = b2 + b2
    num = b1 * (c2 * (g1 - g0) + b0 * (g2 - g1))
    den = b1 * (b2 + b0) + b0 * c2
    return u * (3.0 * total) - jnp.abs(u) * (g1 + num * pl.reciprocal(den, approx=True))


def digits(n):
    radix, count = min(4, n), 1
    while radix**count < n:
        count += 1
    return count, radix


def kernel(
    n_x, n_y,
    scal, east, north, upw, diff, target, adv, shift, im, av, cp,
    xf, xh, bs, ys, tz, ty, ex, ny, nraw, uz, kd, tg, fk, es, aro, ari,
    lsem, csem, hsend, hrecv, wsend, wrecv, asend, arecv,
):
    mx, my = lax.axis_index("gx"), lax.axis_index("gy")
    x_up, x_dn = lax.rem(mx + 1, n_x), lax.rem(mx + n_x - 1, n_x)
    y_up, y_dn = lax.rem(my + 1, n_y), lax.rem(my + n_y - 1, n_y)
    per_axis, radix = digits(n_x)
    rounds = 2 * per_axis

    def partner(r, k):
        on_x, stride = 1 - r // per_axis, 1 + (r % per_axis) * (radix - 1)
        me = on_x * mx + (1 - on_x) * my
        digit = lax.rem(lax.div(me, stride), radix)
        other = me + stride * (lax.rem(digit + k, radix) - digit)
        return on_x * other + (1 - on_x) * mx, on_x * my + (1 - on_x) * other

    loads = [
        pltpu.make_async_copy(scal.at[0], xf.at[0], lsem.at[0]),
        pltpu.make_async_copy(scal.at[1], xf.at[1], lsem.at[1]),
        pltpu.make_async_copy(north, nraw, lsem.at[2]),
        pltpu.make_async_copy(east, ex.at[pl.ds(0, CELLS)], lsem.at[3]),
        pltpu.make_async_copy(diff, kd, lsem.at[4]),
        pltpu.make_async_copy(upw, uz, lsem.at[5]),
        pltpu.make_async_copy(target, tg, lsem.at[6]),
        pltpu.make_async_copy(scal, bs, lsem.at[7]),
    ]
    for load in loads:
        load.start()

    barrier = pltpu.get_barrier_semaphore()
    peers = [(x_up, my), (x_dn, my), (mx, y_up), (mx, y_dn)] + [
        partner(r, k) for r in range(rounds) for k in range(1, radix)
    ]
    for peer in peers:
        pl.semaphore_signal(barrier, inc=1, device_id=peer, device_id_type=MESH)

    def halo(t, way, field=adv, row=None):
        st, s = lax.div(t, 2), lax.rem(t, 2)
        to = ((x_up, my), (x_dn, my), (mx, y_up), (mx, y_dn))[way]
        if way < 2:
            rows = pl.ds(0, CY) if row is None else pl.ds(row, 8)
            src, dst = field.at[s, pl.ds((CX - H, 0)[way], H), rows], xh.at[t, way, :, rows]
        else:
            src = ys.at[st, s, pl.ds((CY, H)[way - 2] * CX, H * CX)]
            dst = ys.at[st, s, pl.ds((0, CY + H)[way - 2] * CX, H * CX)]
        return pltpu.make_async_remote_copy(
            src_ref=src, dst_ref=dst, send_sem=hsend.at[t, way], recv_sem=hrecv.at[t, way],
            device_id=to, device_id_type=MESH,
        )

    def exchange(r):
        return [
            pltpu.make_async_remote_copy(
                src_ref=aro.at[r], dst_ref=ari.at[r, k - 1], send_sem=asend.at[r, k - 1],
                recv_sem=arecv.at[r, k - 1], device_id=partner(r, k), device_id_type=MESH,
            )
            for k in range(1, radix)
        ]

    def send_sums(r):
        for copy in exchange(r):
            copy.start()

    def add_sums(r):
        total = aro[r]
        for k, copy in enumerate(exchange(r)):
            copy.wait_recv()
            total = total + ari[r, k]
        aro[r + 1] = total

    east_edge = pltpu.make_async_remote_copy(
        src_ref=ex.at[pl.ds(0, CY)], dst_ref=ex.at[pl.ds(CELLS, CY)], send_sem=wsend.at[0], recv_sem=wrecv.at[0],
        device_id=(x_dn, my), device_id_type=MESH,
    )
    north_edge = pltpu.make_async_remote_copy(
        src_ref=ny.at[pl.ds(0, CX)], dst_ref=ny.at[pl.ds(CELLS, CX)], send_sem=wsend.at[1], recv_sem=wrecv.at[1],
        device_id=(mx, y_dn), device_id_type=MESH,
    )

    def to_y(st, s, x, value):
        for i in range(CY // 8):
            ys[st, s, pl.ds((H + 8 * i) * CX + x, 8, stride=CX), :] = value[8 * i : 8 * i + 8]

    loads[0].wait()
    loads[1].wait()
    pl.semaphore_wait(barrier, len(peers))

    def first_field(s, _):
        halo(s, 0, xf).start()
        halo(s, 1, xf).start()

        def convert(g, total):
            values = [xf[s, g * GROUP + p] for p in range(GROUP)]
            for p, value in enumerate(values):
                to_y(0, s, g * GROUP + p, value)
            return total + sum(values)

        total = lax.fori_loop(0, CX // GROUP, convert, jnp.zeros((CY, NZ), jnp.float32))
        aro[0, pl.ds(s, 1), :] = jnp.sum(total, axis=0, keepdims=True)
        halo(s, 2).start()
        halo(s, 3).start()
        return 0

    lax.fori_loop(0, 2, first_field, 0)
    send_sums(0)

    loads[2].wait()

    def turn_north(g, _):
        values = [nraw[pl.ds(pl.multiple_of((g * GROUP + p) * CY, CY), CY), :] for p in range(GROUP)]
        for p, value in enumerate(values):
            for i in range(CY // 8):
                ny[pl.ds(8 * i * CX + g * GROUP + p, 8, stride=CX), :] = value[8 * i : 8 * i + 8]
        return 0

    lax.fori_loop(0, CX // GROUP, turn_north, 0)
    north_edge.start()
    loads[3].wait()

    east_edge.start()
    loads[5].wait()
    lane = lax.broadcasted_iota(jnp.int32, (8, NZ), 1)

    loads[4].wait()
    loads[6].wait()
    loads[7].wait()

    def columns_to_lanes(c, _):
        rows = pl.ds(pl.multiple_of(c * 128, 128), 128)
        fk[pl.ds(c, NZ, stride=8), :] = jnp.transpose(kd[rows, :]) * STEP
        return 0

    fk[pl.ds(NZ * 8, fk.shape[0] - NZ * 8), :] = jnp.zeros((fk.shape[0] - NZ * 8, 128), jnp.float32)
    lax.fori_loop(0, TILES, columns_to_lanes, 0)
    fk[pl.ds(0, 8), :] = jnp.zeros((8, 128), jnp.float32)
    es[...] = jnp.zeros((8, 128), jnp.float32)

    def factor(first, e):
        base = pl.multiple_of(first * 8, 8)
        low = fk[pl.ds(base, 8), :]
        for i in range(UNROLL):
            row = pl.ds(base + 8 * i, 8)
            above = fk[pl.ds(base + 8 * i + 8, 8), :]
            g = 1.0 + low * e
            inverse = pl.reciprocal(g + above, approx=True)
            e = g * inverse
            im[row, :] = inverse
            av[row, :] = low * inverse
            cp[row, :] = above * inverse
            low = above
        return e

    def y_column(st, s, row):
        def keep(y, diff):
            ty[pl.ds(row * CY + y, 8, stride=CY), :] = diff

        march(
            lambda y: ys[st, s, pl.ds((H + y) * CX + row, 8), :],
            lambda y: ny[pl.ds(y * CX + row, 8), :],
            CY, keep,
        )

    def x_column(st, s, row, coef):
        t = 2 * st + s

        def load(x):
            if x < 0:
                return xh[t, 0, x + H, pl.ds(row, 8), :]
            if x >= CX:
                return xh[t, 1, x - CX, pl.ds(row, 8), :]
            return xf[s, x, pl.ds(row, 8), :]

        def keep(x, diff):
            rows = pl.ds(x * CY + row, 8)
            value = bs[s, x, pl.ds(row, 8), :] + coef * (diff + ty[rows, :] + tz[s, rows, :])
            adv[s, x, pl.ds(row, 8), :] = value
            ys[st + 1, s, pl.ds((H + row) * CX + x, 8, stride=CX), :] = value

        march(load, lambda x: ex[pl.ds(x * CY + row, 8), :], CX, keep)

    def z_faces(s, group):
        planes = ZROWS // CY
        x = [group * planes + v // (CY // 8) for v in range(ZROWS // 8)]
        rows = [pl.ds(pl.multiple_of(group * ZROWS, ZROWS) + 8 * v, 8) for v in range(ZROWS // 8)]
        parts = [shifted_z(xf[s, x[v], pl.ds(8 * v % CY, 8), :], lane) for v in range(ZROWS // 8)]
        flux = [flux_z(uz[r, :], part, lane) for r, part in zip(rows, parts)]
        for r, value in zip(rows, flux):
            tz[s, r, :] = value - pltpu.roll(value, NZ - 1, 1)

    def back(s):
        return pltpu.make_async_copy(adv.at[s], xf.at[s], csem.at[s])

    def stage(st, _):
        coef = jnp.where(st == 0, STEP / 18.0, jnp.where(st == 1, STEP / 12.0, STEP / 6.0)).astype(jnp.float32)

        def z_pass(s, _):
            @pl.when(st > 0)
            def _():
                back(s).wait()

            def group(i, _):
                z_faces(s, i)
                return 0

            lax.fori_loop(0, CELLS // ZROWS, group, 0)
            return 0

        lax.fori_loop(0, 2, z_pass, 0)

        @pl.when(st < min(2, rounds - 1))
        def _():
            add_sums(st)
            send_sums(st + 1)

        @pl.when(st == 0)
        def _():
            north_edge.wait_recv()
            east_edge.wait_recv()

        def finish(s, _):
            t = 2 * st + s

            def y_pass(i, _):
                y_column(st, s, pl.multiple_of(i * 8, 8))
                return 0

            def x_pass(i, e):
                row = pl.multiple_of(i * 8, 8)
                x_column(st, s, row, coef)
                e = factor(st * PART + (s * (CY // 8) + i) * UNROLL, e)

                @pl.when(st < 2)
                def _():
                    halo(t + 2, 0, row=row).start()
                    halo(t + 2, 1, row=row).start()

                    @pl.when(i == 0)
                    def _():
                        halo(t + 2, 3).start()

                    @pl.when(i == CY // 8 - 1)
                    def _():
                        halo(t + 2, 2).start()

                return e

            halo(t, 2).wait_recv()
            halo(t, 3).wait_recv()
            lax.fori_loop(0, CX // 8, y_pass, 0)
            for way in range(2):
                halo(t, way).wait_recv()
                halo(t, way).wait_send()
            es[...] = lax.fori_loop(0, CY // 8, x_pass, es[...])

            @pl.when(st < 2)
            def _():
                back(s).start()

            return 0

        lax.fori_loop(0, 2, finish, 0)
        if rounds > 3:

            @pl.when(st == 1)
            def _():
                add_sums(2)
                send_sums(3)

        return 0

    lax.fori_loop(0, 3, stage, 0)

    add_sums(rounds - 1)
    cells = float(n_x * CX * n_y * CY)
    shift[...] = RELAX * (aro[rounds] * (1.0 / cells) - tg[...])

    def drain(t, _):
        for way in (2, 3):
            halo(t, way).wait_send()
        return 0

    lax.fori_loop(0, 6, drain, 0)

    for r in range(rounds):
        for copy in exchange(r):
            copy.wait_send()
    east_edge.wait_send()
    north_edge.wait_send()


def solve(adv, shift, im, av, cp, out, rh, ob, osem):
    for s in range(2):
        for c in range(TILES):
            value = adv[s, pl.ds(c * 128, 128), :] - shift[s : s + 1, :]
            rh[s, pl.ds(c, NZ, stride=8), :] = jnp.transpose(value)

    zero = jnp.zeros((8, 128), jnp.float32)

    def forward(k8, carry):
        d0, d1 = carry
        base = pl.multiple_of(k8 * (TURN * 8), TURN * 8)
        rows = [pl.ds(base + 8 * i, 8) for i in range(TURN)]
        data = [(im[r, :], av[r, :], rh[0, r, :], rh[1, r, :]) for r in rows]
        for i, (inverse, a, r0, r1) in enumerate(data):
            d0 = r0 * inverse + a * d0
            d1 = r1 * inverse + a * d1
            rh[0, rows[i], :] = d0
            rh[1, rows[i], :] = d1
        return d0, d1

    lax.fori_loop(0, NZ // TURN, forward, (zero, zero))

    def backward(j8, carry):
        v0, v1 = carry
        base = pl.multiple_of((NZ // TURN - 1 - j8) * (TURN * 8), TURN * 8)
        rows = [pl.ds(base + 8 * (TURN - 1 - i), 8) for i in range(TURN)]
        data = [(cp[r, :], rh[0, r, :], rh[1, r, :]) for r in rows]
        for i, (c, r0, r1) in enumerate(data):
            v0 = r0 + c * v0
            v1 = r1 + c * v1
            rh[0, rows[i], :] = v0
            rh[1, rows[i], :] = v1
        return v0, v1

    lax.fori_loop(0, NZ // TURN, backward, (zero, zero))
    stores = []
    for s in range(2):
        for c in range(TILES):
            rows = pl.ds(c * 128, 128)
            ob[s, rows, :] = jnp.transpose(rh[s, pl.ds(c, NZ, stride=8), :])
            store = pltpu.make_async_copy(ob.at[s, rows], out.at[s, rows], osem.at[s, c])
            store.start()
            stores.append(store)
    for store in stores:
        store.wait()


def in_hbm(value):
    return pltpu.with_memory_space_constraint(value, pltpu.HBM)


def body(n_x, n_y, scalars, east_wind, north_wind, up_wind, diffusivity, target_profile):
    rounds = 2 * digits(n_x)[0]
    hbm = pl.BlockSpec(memory_space=pltpu.HBM)
    f32 = jnp.float32
    vmem = pltpu.VMEM
    dma = pltpu.SemaphoreType.DMA
    resident = pl.BlockSpec(memory_space=pltpu.VMEM)
    columns = jax.ShapeDtypeStruct((LEVELS * 8, 128), f32)
    parts = pl.pallas_call(
        functools.partial(kernel, n_x, n_y),
        out_shape=[
            jax.ShapeDtypeStruct((2, CX, CY, NZ), f32), jax.ShapeDtypeStruct((2, NZ), f32), columns, columns, columns,
        ],
        in_specs=[hbm] * 6,
        out_specs=[resident] * 5,
        scratch_shapes=[
            vmem((2, CX, CY, NZ), f32),
            vmem((6, 2, H, CY, NZ), f32),
            vmem((2, CX, CY, NZ), f32),
            vmem((4, 2, YROWS, NZ), f32),
            vmem((2, CELLS, NZ), f32),
            vmem((CELLS, NZ), f32),
            vmem((CELLS + CY, NZ), f32),
            vmem((CELLS + CX, NZ), f32),
            vmem((CELLS, NZ), f32),
            vmem((CELLS, NZ), f32),
            vmem((CELLS, NZ), f32),
            vmem((2, NZ), f32),
            vmem(((LEVELS + 1) * 8, 128), f32),
            vmem((8, 128), f32),
            vmem((rounds + 1, 2, NZ), f32),
            vmem((rounds, 3, 2, NZ), f32),
            dma((8,)),
            dma((2,)),
            dma((6, 4)),
            dma((6, 4)),
            dma((2,)),
            dma((2,)),
            dma((rounds, 3)),
            dma((rounds, 3)),
        ],
        compiler_params=pltpu.CompilerParams(
            collective_id=0, has_side_effects=True, vmem_limit_bytes=48 * 1024 * 1024
        ),
        cost_estimate=pl.CostEstimate(flops=80_000_000, bytes_accessed=4_000_000, transcendentals=0),
    )(
        in_hbm(scalars),
        in_hbm(east_wind.reshape(CELLS, NZ)),
        in_hbm(north_wind.reshape(CELLS, NZ)),
        in_hbm(up_wind.reshape(CELLS, NZ)),
        in_hbm(diffusivity.reshape(CELLS, NZ)),
        in_hbm(target_profile),
    )
    result = pl.pallas_call(
        solve,
        out_shape=jax.ShapeDtypeStruct((2, CELLS, NZ), f32),
        in_specs=[resident] * 5,
        out_specs=hbm,
        scratch_shapes=[
            vmem((2, NZ * 8, 128), f32),
            vmem((2, CELLS, NZ), f32),
            dma((2, TILES)),
        ],
        compiler_params=pltpu.CompilerParams(vmem_limit_bytes=32 * 1024 * 1024),
        cost_estimate=pl.CostEstimate(flops=2_000_000, bytes_accessed=4_000_000, transcendentals=0),
    )(parts[0].reshape(2, CELLS, NZ), *parts[1:])
    return result.reshape(2, CX, CY, NZ)


def solution(mesh):
    placed = (
        P(None, "gx", "gy", None),
        P("gx", "gy", None),
        P("gx", "gy", None),
        P("gx", "gy", None),
        P("gx", "gy", None),
        P(),
    )
    return jax.shard_map(
        functools.partial(body, mesh.shape["gx"], mesh.shape["gy"]),
        mesh=mesh, in_specs=placed, out_specs=P(None, "gx", "gy", None), check_vma=False,
    )
```

```python
import functools

import jax
import jax.numpy as jnp
from jax import lax
from jax.experimental import pallas as pl
from jax.experimental.pallas import tpu as pltpu
from jax.sharding import PartitionSpec as P

STEP = 0.3
RELAX = 0.5
EPSILON = 1e-06
EPS = 0.75 * EPSILON
EPS2 = EPS * EPS

CX, CY, NZ = 24, 32, 128
H = 3
YROWS = (CY + 2 * H) * CX
CELLS = CX * CY
TILES = CELLS // 128
GROUP = 8
ZROWS = 192
TURN = 16
PART = 64
LEVELS = 2 * PART
UNROLL = PART // 8
MESH = pl.DeviceIdType.MESH


def cell(dm, em, dp, ep):
    g = dp - dm
    b = (g * g + EPS) + ep * dm
    g2 = g + g
    left = b - g2 * em
    right = b + g2 * ep
    return g, left * left, b * b, right * right


def face(u, total, g_low, g_high, t_low, t_mid, t_high, r2, r1, c1, c0, l0, l1):
    pos = u > 0.0
    b0 = jnp.where(pos, r2, l1)
    b1 = jnp.where(pos, c1, c0)
    b2 = jnp.where(pos, l0, r1)
    gs = jnp.where(pos, g_low, g_high)
    ts = jnp.where(pos, t_low, t_high)
    b0 = 3.0 * b0
    c2 = b2 + b2
    num = b1 * (c2 * ts + b0 * t_mid)
    den = b1 * (b2 + b0) + b0 * c2
    part = num * pl.reciprocal(den, approx=True)
    return u * (3.0 * total - gs) - jnp.abs(u) * part


def march(load_f, load_u, cells, emit):
    f, d, q, t = {}, {}, {}, {}

    def get_f(i):
        if i not in f:
            f[i] = load_f(i)
        return f[i]

    def get_d(i):
        if i not in d:
            diff = get_f(i) - get_f(i - 1)
            d[i] = (diff, 0.75 * diff)
        return d[i]

    def get_q(i):
        if i not in q:
            q[i] = cell(*get_d(i), *get_d(i + 1))
        return q[i]

    def get_t(i):
        if i not in t:
            t[i] = get_q(i)[0] - get_q(i - 1)[0]
        return t[i]

    lower = None
    for j in range(cells + 1):
        lo2, lo1, hi0, hi1 = get_q(j - 2), get_q(j - 1), get_q(j), get_q(j + 1)
        upper = face(
            load_u(j), get_f(j - 1) + get_f(j), lo1[0], hi0[0], get_t(j - 1), get_t(j), get_t(j + 1),
            lo2[3], lo1[3], lo1[2], hi0[2], hi0[1], hi1[1],
        )
        if j > 0:
            emit(j - 1, lower - upper)
        lower = upper


def shifted_z(f, lane):
    below = pltpu.roll(f, 1, 1)
    d = jnp.where(lane == 0, 0.0, f - below)
    return (
        f + below, d, jnp.where(lane == 1, 0.0, pltpu.roll(d, 2, 1)), pltpu.roll(d, 1, 1), pltpu.roll(d, NZ - 1, 1),
        jnp.where(lane == NZ - 1, 0.0, pltpu.roll(d, NZ - 2, 1)),
    )


def flux_z(u, parts, lane):
    total, d3, low2, low1, high1, high2 = parts
    u = jnp.where(lane == 0, 0.0, u)
    pos = u > 0.0
    d1 = jnp.where(pos, low2, high2)
    d2 = jnp.where(pos, low1, high1)
    d4 = jnp.where(pos, high1, low1)
    g0, g1, g2 = d2 - d1, d3 - d2, d4 - d3
    e2, e3 = 0.75 * d2, 0.75 * d3
    b0 = (g0 * g0 + EPS) + e2 * (d2 + g0)
    b1 = (g1 * g1 + EPS) + e3 * d2
    b2 = (g2 * g2 + EPS) + e3 * (d3 - g2)
    b0 = 3.0 * (b0 * b0)
    b1 = b1 * b1
    b2 = b2 * b2
    c2 = b2 + b2
    num = b1 * (c2 * (g1 - g0) + b0 * (g2 - g1))
    den = b1 * (b2 + b0) + b0 * c2
    return u * (3.0 * total) - jnp.abs(u) * (g1 + num * pl.reciprocal(den, approx=True))


def digits(n):
    radix, count = min(4, n), 1
    while radix**count < n:
        count += 1
    return count, radix


def kernel(
    n_x, n_y,
    scal, east, north, upw, diff, target, adv, shift, im, av, cp,
    xf, xh, bs, ys, tz, ty, ex, ny, nraw, uz, kd, tg, fk, es, aro, ari,
    lsem, csem, hsend, hrecv, wsend, wrecv, asend, arecv,
):
    mx, my = lax.axis_index("gx"), lax.axis_index("gy")
    x_up, x_dn = lax.rem(mx + 1, n_x), lax.rem(mx + n_x - 1, n_x)
    y_up, y_dn = lax.rem(my + 1, n_y), lax.rem(my + n_y - 1, n_y)
    per_axis, radix = digits(n_x)
    rounds = 2 * per_axis

    def partner(r, k):
        on_x, stride = 1 - r // per_axis, 1 + (r % per_axis) * (radix - 1)
        me = on_x * mx + (1 - on_x) * my
        digit = lax.rem(lax.div(me, stride), radix)
        other = me + stride * (lax.rem(digit + k, radix) - digit)
        return on_x * other + (1 - on_x) * mx, on_x * my + (1 - on_x) * other

    loads = [
        pltpu.make_async_copy(scal.at[0], xf.at[0], lsem.at[0]),
        pltpu.make_async_copy(scal.at[1], xf.at[1], lsem.at[1]),
        pltpu.make_async_copy(north, nraw, lsem.at[2]),
        pltpu.make_async_copy(east, ex.at[pl.ds(0, CELLS)], lsem.at[3]),
        pltpu.make_async_copy(diff, kd, lsem.at[4]),
        pltpu.make_async_copy(upw, uz, lsem.at[5]),
        pltpu.make_async_copy(target, tg, lsem.at[6]),
        pltpu.make_async_copy(scal, bs, lsem.at[7]),
    ]
    for load in loads:
        load.start()

    barrier = pltpu.get_barrier_semaphore()
    peers = [(x_up, my), (x_dn, my), (mx, y_up), (mx, y_dn)] + [
        partner(r, k) for r in range(rounds) for k in range(1, radix)
    ]
    for peer in peers:
        pl.semaphore_signal(barrier, inc=1, device_id=peer, device_id_type=MESH)

    def halo(t, way, field=adv, row=None):
        st, s = lax.div(t, 2), lax.rem(t, 2)
        to = ((x_up, my), (x_dn, my), (mx, y_up), (mx, y_dn))[way]
        if way < 2:
            rows = pl.ds(0, CY) if row is None else pl.ds(row, 8)
            src, dst = field.at[s, pl.ds((CX - H, 0)[way], H), rows], xh.at[t, way, :, rows]
        else:
            src = ys.at[st, s, pl.ds((CY, H)[way - 2] * CX, H * CX)]
            dst = ys.at[st, s, pl.ds((0, CY + H)[way - 2] * CX, H * CX)]
        return pltpu.make_async_remote_copy(
            src_ref=src, dst_ref=dst, send_sem=hsend.at[t, way], recv_sem=hrecv.at[t, way],
            device_id=to, device_id_type=MESH,
        )

    def exchange(r):
        return [
            pltpu.make_async_remote_copy(
                src_ref=aro.at[r], dst_ref=ari.at[r, k - 1], send_sem=asend.at[r, k - 1],
                recv_sem=arecv.at[r, k - 1], device_id=partner(r, k), device_id_type=MESH,
            )
            for k in range(1, radix)
        ]

    def send_sums(r):
        for copy in exchange(r):
            copy.start()

    def add_sums(r):
        total = aro[r]
        for k, copy in enumerate(exchange(r)):
            copy.wait_recv()
            total = total + ari[r, k]
        aro[r + 1] = total

    east_edge = pltpu.make_async_remote_copy(
        src_ref=ex.at[pl.ds(0, CY)], dst_ref=ex.at[pl.ds(CELLS, CY)], send_sem=wsend.at[0], recv_sem=wrecv.at[0],
        device_id=(x_dn, my), device_id_type=MESH,
    )
    north_edge = pltpu.make_async_remote_copy(
        src_ref=ny.at[pl.ds(0, CX)], dst_ref=ny.at[pl.ds(CELLS, CX)], send_sem=wsend.at[1], recv_sem=wrecv.at[1],
        device_id=(mx, y_dn), device_id_type=MESH,
    )

    def to_y(st, s, x, value):
        for i in range(CY // 8):
            ys[st, s, pl.ds((H + 8 * i) * CX + x, 8, stride=CX), :] = value[8 * i : 8 * i + 8]

    loads[0].wait()
    loads[1].wait()
    pl.semaphore_wait(barrier, len(peers))

    def first_field(s, _):
        halo(s, 0, xf).start()
        halo(s, 1, xf).start()

        def convert(g, total):
            values = [xf[s, g * GROUP + p] for p in range(GROUP)]
            for p, value in enumerate(values):
                to_y(0, s, g * GROUP + p, value)
            return total + sum(values)

        total = lax.fori_loop(0, CX // GROUP, convert, jnp.zeros((CY, NZ), jnp.float32))
        aro[0, pl.ds(s, 1), :] = jnp.sum(total, axis=0, keepdims=True)
        halo(s, 2).start()
        halo(s, 3).start()
        return 0

    lax.fori_loop(0, 2, first_field, 0)
    send_sums(0)

    loads[2].wait()

    def turn_north(g, _):
        values = [nraw[pl.ds(pl.multiple_of((g * GROUP + p) * CY, CY), CY), :] for p in range(GROUP)]
        for p, value in enumerate(values):
            for i in range(CY // 8):
                ny[pl.ds(8 * i * CX + g * GROUP + p, 8, stride=CX), :] = value[8 * i : 8 * i + 8]
        return 0

    lax.fori_loop(0, CX // GROUP, turn_north, 0)
    north_edge.start()
    loads[3].wait()

    east_edge.start()
    loads[5].wait()
    lane = lax.broadcasted_iota(jnp.int32, (8, NZ), 1)

    loads[6].wait()
    loads[7].wait()
    es[...] = jnp.zeros((8, 128), jnp.float32)
    clear = 16

    def zero_factors(i, _):
        fk[pl.ds(pl.multiple_of(i * (clear * 8), 8), clear * 8), :] = jnp.zeros((clear * 8, 128), jnp.float32)
        return 0

    lax.fori_loop(0, NZ // clear, zero_factors, 0)
    fk[pl.ds(NZ * 8, 8), :] = jnp.zeros((8, 128), jnp.float32)

    def start_factors():
        def columns_to_lanes(c, _):
            rows = pl.ds(pl.multiple_of(c * 128, 128), 128)
            fk[pl.ds(c, NZ, stride=8), :] = jnp.transpose(kd[rows, :]) * STEP
            return 0

        loads[4].wait()
        lax.fori_loop(0, TILES, columns_to_lanes, 0)
        fk[pl.ds(0, 8), :] = jnp.zeros((8, 128), jnp.float32)
        es[...] = jnp.zeros((8, 128), jnp.float32)

    def factor(first, e):
        base = pl.multiple_of(first * 8, 8)
        low = fk[pl.ds(base, 8), :]
        for i in range(UNROLL):
            row = pl.ds(base + 8 * i, 8)
            above = fk[pl.ds(base + 8 * i + 8, 8), :]
            g = 1.0 + low * e
            inverse = pl.reciprocal(g + above, approx=True)
            e = g * inverse
            im[row, :] = inverse
            av[row, :] = low * inverse
            cp[row, :] = above * inverse
            low = above
        return e

    def y_column(st, s, row):
        def keep(y, diff):
            ty[pl.ds(row * CY + y, 8, stride=CY), :] = diff

        march(
            lambda y: ys[st, s, pl.ds((H + y) * CX + row, 8), :],
            lambda y: ny[pl.ds(y * CX + row, 8), :],
            CY, keep,
        )

    def x_column(st, s, row, coef):
        t = 2 * st + s

        def load(x):
            if x < 0:
                return xh[t, 0, x + H, pl.ds(row, 8), :]
            if x >= CX:
                return xh[t, 1, x - CX, pl.ds(row, 8), :]
            return xf[s, x, pl.ds(row, 8), :]

        def keep(x, diff):
            rows = pl.ds(x * CY + row, 8)
            value = bs[s, x, pl.ds(row, 8), :] + coef * (diff + ty[rows, :] + tz[s, rows, :])
            adv[s, x, pl.ds(row, 8), :] = value
            ys[st + 1, s, pl.ds((H + row) * CX + x, 8, stride=CX), :] = value

        march(load, lambda x: ex[pl.ds(x * CY + row, 8), :], CX, keep)

    def z_faces(s, group):
        planes = ZROWS // CY
        x = [group * planes + v // (CY // 8) for v in range(ZROWS // 8)]
        rows = [pl.ds(pl.multiple_of(group * ZROWS, ZROWS) + 8 * v, 8) for v in range(ZROWS // 8)]
        parts = [shifted_z(xf[s, x[v], pl.ds(8 * v % CY, 8), :], lane) for v in range(ZROWS // 8)]
        flux = [flux_z(uz[r, :], part, lane) for r, part in zip(rows, parts)]
        for r, value in zip(rows, flux):
            tz[s, r, :] = value - pltpu.roll(value, NZ - 1, 1)

    def back(s):
        return pltpu.make_async_copy(adv.at[s], xf.at[s], csem.at[s])

    def stage(st, _):
        coef = jnp.where(st == 0, STEP / 18.0, jnp.where(st == 1, STEP / 12.0, STEP / 6.0)).astype(jnp.float32)

        def z_pass(s, _):
            @pl.when(st > 0)
            def _():
                back(s).wait()

            def group(i, _):
                z_faces(s, i)
                return 0

            lax.fori_loop(0, CELLS // ZROWS, group, 0)
            return 0

        lax.fori_loop(0, 2, z_pass, 0)

        @pl.when(st < min(2, rounds - 1))
        def _():
            add_sums(st)
            send_sums(st + 1)

        @pl.when(st == 0)
        def _():
            north_edge.wait_recv()
            east_edge.wait_recv()

        @pl.when(st == 1)
        def _():
            start_factors()

        def finish(s, _):
            t = 2 * st + s

            def y_pass(i, _):
                y_column(st, s, pl.multiple_of(i * 8, 8))
                return 0

            def x_pass(i, e):
                row = pl.multiple_of(i * 8, 8)
                x_column(st, s, row, coef)
                e = factor(lax.max(st - 1, 0) * PART + (s * (CY // 8) + i) * UNROLL, e)

                @pl.when(st < 2)
                def _():
                    halo(t + 2, 0, row=row).start()
                    halo(t + 2, 1, row=row).start()

                    @pl.when(i == 0)
                    def _():
                        halo(t + 2, 3).start()

                    @pl.when(i == CY // 8 - 1)
                    def _():
                        halo(t + 2, 2).start()

                return e

            halo(t, 2).wait_recv()
            halo(t, 3).wait_recv()
            lax.fori_loop(0, CX // 8, y_pass, 0)
            for way in range(2):
                halo(t, way).wait_recv()
                halo(t, way).wait_send()
            es[...] = lax.fori_loop(0, CY // 8, x_pass, es[...])

            @pl.when(st < 2)
            def _():
                back(s).start()

            return 0

        lax.fori_loop(0, 2, finish, 0)
        if rounds > 3:

            @pl.when(st == 1)
            def _():
                add_sums(2)
                send_sums(3)

        return 0

    lax.fori_loop(0, 3, stage, 0)

    add_sums(rounds - 1)
    cells = float(n_x * CX * n_y * CY)
    shift[...] = RELAX * (aro[rounds] * (1.0 / cells) - tg[...])

    def drain(t, _):
        for way in (2, 3):
            halo(t, way).wait_send()
        return 0

    lax.fori_loop(0, 6, drain, 0)

    for r in range(rounds):
        for copy in exchange(r):
            copy.wait_send()
    east_edge.wait_send()
    north_edge.wait_send()


def solve(adv, shift, im, av, cp, out, rh, ob, osem):
    for s in range(2):
        for c in range(TILES):
            value = adv[s, pl.ds(c * 128, 128), :] - shift[s : s + 1, :]
            rh[s, pl.ds(c, NZ, stride=8), :] = jnp.transpose(value)

    zero = jnp.zeros((8, 128), jnp.float32)

    def forward(k8, carry):
        d0, d1 = carry
        base = pl.multiple_of(k8 * (TURN * 8), TURN * 8)
        rows = [pl.ds(base + 8 * i, 8) for i in range(TURN)]
        data = [(im[r, :], av[r, :], rh[0, r, :], rh[1, r, :]) for r in rows]
        for i, (inverse, a, r0, r1) in enumerate(data):
            d0 = r0 * inverse + a * d0
            d1 = r1 * inverse + a * d1
            rh[0, rows[i], :] = d0
            rh[1, rows[i], :] = d1
        return d0, d1

    lax.fori_loop(0, NZ // TURN, forward, (zero, zero))

    def backward(j8, carry):
        v0, v1 = carry
        base = pl.multiple_of((NZ // TURN - 1 - j8) * (TURN * 8), TURN * 8)
        rows = [pl.ds(base + 8 * (TURN - 1 - i), 8) for i in range(TURN)]
        data = [(cp[r, :], rh[0, r, :], rh[1, r, :]) for r in rows]
        for i, (c, r0, r1) in enumerate(data):
            v0 = r0 + c * v0
            v1 = r1 + c * v1
            rh[0, rows[i], :] = v0
            rh[1, rows[i], :] = v1
        return v0, v1

    lax.fori_loop(0, NZ // TURN, backward, (zero, zero))
    stores = []
    for s in range(2):
        for c in range(TILES):
            rows = pl.ds(c * 128, 128)
            ob[s, rows, :] = jnp.transpose(rh[s, pl.ds(c, NZ, stride=8), :])
            store = pltpu.make_async_copy(ob.at[s, rows], out.at[s, rows], osem.at[s, c])
            store.start()
            stores.append(store)
    for store in stores:
        store.wait()


def in_hbm(value):
    return pltpu.with_memory_space_constraint(value, pltpu.HBM)


def body(n_x, n_y, scalars, east_wind, north_wind, up_wind, diffusivity, target_profile):
    rounds = 2 * digits(n_x)[0]
    hbm = pl.BlockSpec(memory_space=pltpu.HBM)
    f32 = jnp.float32
    vmem = pltpu.VMEM
    dma = pltpu.SemaphoreType.DMA
    resident = pl.BlockSpec(memory_space=pltpu.VMEM)
    columns = jax.ShapeDtypeStruct((LEVELS * 8, 128), f32)
    parts = pl.pallas_call(
        functools.partial(kernel, n_x, n_y),
        out_shape=[
            jax.ShapeDtypeStruct((2, CX, CY, NZ), f32), jax.ShapeDtypeStruct((2, NZ), f32), columns, columns, columns,
        ],
        in_specs=[hbm] * 6,
        out_specs=[resident] * 5,
        scratch_shapes=[
            vmem((2, CX, CY, NZ), f32),
            vmem((6, 2, H, CY, NZ), f32),
            vmem((2, CX, CY, NZ), f32),
            vmem((4, 2, YROWS, NZ), f32),
            vmem((2, CELLS, NZ), f32),
            vmem((CELLS, NZ), f32),
            vmem((CELLS + CY, NZ), f32),
            vmem((CELLS + CX, NZ), f32),
            vmem((CELLS, NZ), f32),
            vmem((CELLS, NZ), f32),
            vmem((CELLS, NZ), f32),
            vmem((2, NZ), f32),
            vmem(((LEVELS + 1) * 8, 128), f32),
            vmem((8, 128), f32),
            vmem((rounds + 1, 2, NZ), f32),
            vmem((rounds, 3, 2, NZ), f32),
            dma((8,)),
            dma((2,)),
            dma((6, 4)),
            dma((6, 4)),
            dma((2,)),
            dma((2,)),
            dma((rounds, 3)),
            dma((rounds, 3)),
        ],
        compiler_params=pltpu.CompilerParams(
            collective_id=0, has_side_effects=True, vmem_limit_bytes=48 * 1024 * 1024
        ),
        cost_estimate=pl.CostEstimate(flops=80_000_000, bytes_accessed=4_000_000, transcendentals=0),
    )(
        in_hbm(scalars),
        in_hbm(east_wind.reshape(CELLS, NZ)),
        in_hbm(north_wind.reshape(CELLS, NZ)),
        in_hbm(up_wind.reshape(CELLS, NZ)),
        in_hbm(diffusivity.reshape(CELLS, NZ)),
        in_hbm(target_profile),
    )
    result = pl.pallas_call(
        solve,
        out_shape=jax.ShapeDtypeStruct((2, CELLS, NZ), f32),
        in_specs=[resident] * 5,
        out_specs=hbm,
        scratch_shapes=[
            vmem((2, NZ * 8, 128), f32),
            vmem((2, CELLS, NZ), f32),
            dma((2, TILES)),
        ],
        compiler_params=pltpu.CompilerParams(vmem_limit_bytes=32 * 1024 * 1024),
        cost_estimate=pl.CostEstimate(flops=2_000_000, bytes_accessed=4_000_000, transcendentals=0),
    )(parts[0].reshape(2, CELLS, NZ), *parts[1:])
    return result.reshape(2, CX, CY, NZ)


def solution(mesh):
    placed = (
        P(None, "gx", "gy", None),
        P("gx", "gy", None),
        P("gx", "gy", None),
        P("gx", "gy", None),
        P("gx", "gy", None),
        P(),
    )
    return jax.shard_map(
        functools.partial(body, mesh.shape["gx"], mesh.shape["gy"]),
        mesh=mesh, in_specs=placed, out_specs=P(None, "gx", "gy", None), check_vma=False,
    )
```

```python
import functools

import jax
import jax.numpy as jnp
from jax import lax
from jax.experimental import pallas as pl
from jax.experimental.pallas import tpu as pltpu
from jax.sharding import PartitionSpec as P

STEP = 0.3
RELAX = 0.5
EPSILON = 1e-06
EPS = 0.75 * EPSILON
EPS2 = EPS * EPS

CX, CY, NZ = 24, 32, 128
H = 3
YROWS = (CY + 2 * H) * CX
CELLS = CX * CY
TILES = CELLS // 128
GROUP = 8
ZROWS = 192
TURN = 16
PART = 48
LEVELS = 3 * PART
UNROLL = PART // 8
MESH = pl.DeviceIdType.MESH


def cell(dm, em, dp, ep):
    g = dp - dm
    b = (g * g + EPS) + ep * dm
    g2 = g + g
    left = b - g2 * em
    right = b + g2 * ep
    return g, left * left, b * b, right * right


def face(u, total, g_low, g_high, t_low, t_mid, t_high, r2, r1, c1, c0, l0, l1):
    pos = u > 0.0
    b0 = jnp.where(pos, r2, l1)
    b1 = jnp.where(pos, c1, c0)
    b2 = jnp.where(pos, l0, r1)
    gs = jnp.where(pos, g_low, g_high)
    ts = jnp.where(pos, t_low, t_high)
    b0 = 3.0 * b0
    c2 = b2 + b2
    num = b1 * (c2 * ts + b0 * t_mid)
    den = b1 * (b2 + b0) + b0 * c2
    part = num * pl.reciprocal(den, approx=True)
    return u * (3.0 * total - gs) - jnp.abs(u) * part


def march(load_f, load_u, cells, emit):
    f, d, q, t = {}, {}, {}, {}

    def get_f(i):
        if i not in f:
            f[i] = load_f(i)
        return f[i]

    def get_d(i):
        if i not in d:
            diff = get_f(i) - get_f(i - 1)
            d[i] = (diff, 0.75 * diff)
        return d[i]

    def get_q(i):
        if i not in q:
            q[i] = cell(*get_d(i), *get_d(i + 1))
        return q[i]

    def get_t(i):
        if i not in t:
            t[i] = get_q(i)[0] - get_q(i - 1)[0]
        return t[i]

    lower = None
    for j in range(cells + 1):
        lo2, lo1, hi0, hi1 = get_q(j - 2), get_q(j - 1), get_q(j), get_q(j + 1)
        upper = face(
            load_u(j), get_f(j - 1) + get_f(j), lo1[0], hi0[0], get_t(j - 1), get_t(j), get_t(j + 1),
            lo2[3], lo1[3], lo1[2], hi0[2], hi0[1], hi1[1],
        )
        if j > 0:
            emit(j - 1, lower - upper)
        lower = upper


def shifted_z(f, lane):
    below = pltpu.roll(f, 1, 1)
    d = jnp.where(lane == 0, 0.0, f - below)
    return (
        f + below, d, jnp.where(lane == 1, 0.0, pltpu.roll(d, 2, 1)), pltpu.roll(d, 1, 1), pltpu.roll(d, NZ - 1, 1),
        jnp.where(lane == NZ - 1, 0.0, pltpu.roll(d, NZ - 2, 1)),
    )


def flux_z(u, parts, lane):
    total, d3, low2, low1, high1, high2 = parts
    u = jnp.where(lane == 0, 0.0, u)
    pos = u > 0.0
    d1 = jnp.where(pos, low2, high2)
    d2 = jnp.where(pos, low1, high1)
    d4 = jnp.where(pos, high1, low1)
    g0, g1, g2 = d2 - d1, d3 - d2, d4 - d3
    e2, e3 = 0.75 * d2, 0.75 * d3
    b0 = (g0 * g0 + EPS) + e2 * (d2 + g0)
    b1 = (g1 * g1 + EPS) + e3 * d2
    b2 = (g2 * g2 + EPS) + e3 * (d3 - g2)
    b0 = 3.0 * (b0 * b0)
    b1 = b1 * b1
    b2 = b2 * b2
    c2 = b2 + b2
    num = b1 * (c2 * (g1 - g0) + b0 * (g2 - g1))
    den = b1 * (b2 + b0) + b0 * c2
    return u * (3.0 * total) - jnp.abs(u) * (g1 + num * pl.reciprocal(den, approx=True))


def digits(n):
    radix, count = min(4, n), 1
    while radix**count < n:
        count += 1
    return count, radix


def kernel(
    n_x, n_y,
    scal, east, north, upw, diff, target, adv, shift, im, av, cp,
    xf, xh, bs, ys, tz, ty, ex, ny, nraw, uz, kd, tg, fk, es, aro, ari,
    lsem, csem, hsend, hrecv, wsend, wrecv, asend, arecv,
):
    mx, my = lax.axis_index("gx"), lax.axis_index("gy")
    x_up, x_dn = lax.rem(mx + 1, n_x), lax.rem(mx + n_x - 1, n_x)
    y_up, y_dn = lax.rem(my + 1, n_y), lax.rem(my + n_y - 1, n_y)
    per_axis, radix = digits(n_x)
    rounds = 2 * per_axis

    def partner(r, k):
        on_x, stride = 1 - r // per_axis, 1 + (r % per_axis) * (radix - 1)
        me = on_x * mx + (1 - on_x) * my
        digit = lax.rem(lax.div(me, stride), radix)
        other = me + stride * (lax.rem(digit + k, radix) - digit)
        return on_x * other + (1 - on_x) * mx, on_x * my + (1 - on_x) * other

    loads = [
        pltpu.make_async_copy(scal.at[0], xf.at[0], lsem.at[0]),
        pltpu.make_async_copy(scal.at[1], xf.at[1], lsem.at[1]),
        pltpu.make_async_copy(north, nraw, lsem.at[2]),
        pltpu.make_async_copy(east, ex.at[pl.ds(0, CELLS)], lsem.at[3]),
        pltpu.make_async_copy(diff, kd, lsem.at[4]),
        pltpu.make_async_copy(upw, uz, lsem.at[5]),
        pltpu.make_async_copy(target, tg, lsem.at[6]),
        pltpu.make_async_copy(scal, bs, lsem.at[7]),
    ]
    for load in loads:
        load.start()

    barrier = pltpu.get_barrier_semaphore()
    peers = [(x_up, my), (x_dn, my), (mx, y_up), (mx, y_dn)] + [
        partner(r, k) for r in range(rounds) for k in range(1, radix)
    ]
    for peer in peers:
        pl.semaphore_signal(barrier, inc=1, device_id=peer, device_id_type=MESH)

    def halo(t, way, field=adv, row=None):
        st, s = lax.div(t, 2), lax.rem(t, 2)
        to = ((x_up, my), (x_dn, my), (mx, y_up), (mx, y_dn))[way]
        if way < 2:
            rows = pl.ds(0, CY) if row is None else pl.ds(row, 8)
            src, dst = field.at[s, pl.ds((CX - H, 0)[way], H), rows], xh.at[t, way, :, rows]
        else:
            src = ys.at[st, s, pl.ds((CY, H)[way - 2] * CX, H * CX)]
            dst = ys.at[st, s, pl.ds((0, CY + H)[way - 2] * CX, H * CX)]
        return pltpu.make_async_remote_copy(
            src_ref=src, dst_ref=dst, send_sem=hsend.at[t, way], recv_sem=hrecv.at[t, way],
            device_id=to, device_id_type=MESH,
        )

    def exchange(r):
        return [
            pltpu.make_async_remote_copy(
                src_ref=aro.at[r], dst_ref=ari.at[r, k - 1], send_sem=asend.at[r, k - 1],
                recv_sem=arecv.at[r, k - 1], device_id=partner(r, k), device_id_type=MESH,
            )
            for k in range(1, radix)
        ]

    def send_sums(r):
        for copy in exchange(r):
            copy.start()

    def add_sums(r):
        total = aro[r]
        for k, copy in enumerate(exchange(r)):
            copy.wait_recv()
            total = total + ari[r, k]
        aro[r + 1] = total

    east_edge = pltpu.make_async_remote_copy(
        src_ref=ex.at[pl.ds(0, CY)], dst_ref=ex.at[pl.ds(CELLS, CY)], send_sem=wsend.at[0], recv_sem=wrecv.at[0],
        device_id=(x_dn, my), device_id_type=MESH,
    )
    north_edge = pltpu.make_async_remote_copy(
        src_ref=ny.at[pl.ds(0, CX)], dst_ref=ny.at[pl.ds(CELLS, CX)], send_sem=wsend.at[1], recv_sem=wrecv.at[1],
        device_id=(mx, y_dn), device_id_type=MESH,
    )

    def to_y(st, s, x, value):
        for i in range(CY // 8):
            ys[st, s, pl.ds((H + 8 * i) * CX + x, 8, stride=CX), :] = value[8 * i : 8 * i + 8]

    loads[0].wait()
    loads[1].wait()
    pl.semaphore_wait(barrier, len(peers))

    def first_field(s, _):
        halo(s, 0, xf).start()
        halo(s, 1, xf).start()

        def convert(g, total):
            values = [xf[s, g * GROUP + p] for p in range(GROUP)]
            for p, value in enumerate(values):
                to_y(0, s, g * GROUP + p, value)
            return total + sum(values)

        total = lax.fori_loop(0, CX // GROUP, convert, jnp.zeros((CY, NZ), jnp.float32))
        aro[0, pl.ds(s, 1), :] = jnp.sum(total, axis=0, keepdims=True)
        halo(s, 2).start()
        halo(s, 3).start()
        return 0

    lax.fori_loop(0, 2, first_field, 0)
    send_sums(0)

    loads[2].wait()

    def turn_north(g, _):
        values = [nraw[pl.ds(pl.multiple_of((g * GROUP + p) * CY, CY), CY), :] for p in range(GROUP)]
        for p, value in enumerate(values):
            for i in range(CY // 8):
                ny[pl.ds(8 * i * CX + g * GROUP + p, 8, stride=CX), :] = value[8 * i : 8 * i + 8]
        return 0

    lax.fori_loop(0, CX // GROUP, turn_north, 0)
    north_edge.start()
    loads[3].wait()

    east_edge.start()
    loads[5].wait()
    lane = lax.broadcasted_iota(jnp.int32, (8, NZ), 1)

    loads[4].wait()
    loads[6].wait()
    loads[7].wait()

    def columns_to_lanes(c, _):
        rows = pl.ds(pl.multiple_of(c * 128, 128), 128)
        fk[pl.ds(c, NZ, stride=8), :] = jnp.transpose(kd[rows, :]) * STEP
        return 0

    fk[pl.ds(NZ * 8, fk.shape[0] - NZ * 8), :] = jnp.zeros((fk.shape[0] - NZ * 8, 128), jnp.float32)
    lax.fori_loop(0, TILES, columns_to_lanes, 0)
    fk[pl.ds(0, 8), :] = jnp.zeros((8, 128), jnp.float32)
    es[...] = jnp.zeros((8, 128), jnp.float32)

    def factor_levels(first, e):
        base = pl.multiple_of(first * 8, 8)
        state = {"e": e, "low": fk[pl.ds(base, 8), :]}

        def level(i):
            row = pl.ds(base + 8 * i, 8)
            low = state["low"]
            above = fk[pl.ds(base + 8 * i + 8, 8), :]
            g = 1.0 + low * state["e"]
            inverse = pl.reciprocal(g + above, approx=True)
            im[row, :] = inverse
            av[row, :] = low * inverse
            cp[row, :] = above * inverse
            state["e"], state["low"] = g * inverse, above

        return state, level

    def y_column(st, s, row):
        def keep(y, diff):
            ty[pl.ds(row * CY + y, 8, stride=CY), :] = diff

        march(
            lambda y: ys[st, s, pl.ds((H + y) * CX + row, 8), :],
            lambda y: ny[pl.ds(y * CX + row, 8), :],
            CY, keep,
        )

    def x_column(st, s, row, coef, level):
        t = 2 * st + s

        def load(x):
            if x < 0:
                return xh[t, 0, x + H, pl.ds(row, 8), :]
            if x >= CX:
                return xh[t, 1, x - CX, pl.ds(row, 8), :]
            return xf[s, x, pl.ds(row, 8), :]

        def keep(x, diff):
            rows = pl.ds(x * CY + row, 8)
            value = bs[s, x, pl.ds(row, 8), :] + coef * (diff + ty[rows, :] + tz[s, rows, :])
            adv[s, x, pl.ds(row, 8), :] = value
            ys[st + 1, s, pl.ds((H + row) * CX + x, 8, stride=CX), :] = value
            if x % 4 == 3:
                level(x // 4)

        march(load, lambda x: ex[pl.ds(x * CY + row, 8), :], CX, keep)

    def z_faces(s, group):
        planes = ZROWS // CY
        x = [group * planes + v // (CY // 8) for v in range(ZROWS // 8)]
        rows = [pl.ds(pl.multiple_of(group * ZROWS, ZROWS) + 8 * v, 8) for v in range(ZROWS // 8)]
        parts = [shifted_z(xf[s, x[v], pl.ds(8 * v % CY, 8), :], lane) for v in range(ZROWS // 8)]
        flux = [flux_z(uz[r, :], part, lane) for r, part in zip(rows, parts)]
        for r, value in zip(rows, flux):
            tz[s, r, :] = value - pltpu.roll(value, NZ - 1, 1)

    def back(s):
        return pltpu.make_async_copy(adv.at[s], xf.at[s], csem.at[s])

    def stage(st, _):
        coef = jnp.where(st == 0, STEP / 18.0, jnp.where(st == 1, STEP / 12.0, STEP / 6.0)).astype(jnp.float32)

        def z_pass(s, _):
            @pl.when(st > 0)
            def _():
                back(s).wait()

            def group(i, _):
                z_faces(s, i)
                return 0

            lax.fori_loop(0, CELLS // ZROWS, group, 0)
            return 0

        lax.fori_loop(0, 2, z_pass, 0)

        @pl.when(st < min(2, rounds - 1))
        def _():
            add_sums(st)
            send_sums(st + 1)

        @pl.when(st == 0)
        def _():
            north_edge.wait_recv()
            east_edge.wait_recv()

        def finish(s, _):
            t = 2 * st + s

            def y_pass(i, _):
                y_column(st, s, pl.multiple_of(i * 8, 8))
                return 0

            def x_pass(i, e):
                row = pl.multiple_of(i * 8, 8)
                state, level = factor_levels(st * PART + (s * (CY // 8) + i) * UNROLL, e)
                x_column(st, s, row, coef, level)
                e = state["e"]

                @pl.when(st < 2)
                def _():
                    halo(t + 2, 0, row=row).start()
                    halo(t + 2, 1, row=row).start()

                    @pl.when(i == 0)
                    def _():
                        halo(t + 2, 3).start()

                    @pl.when(i == CY // 8 - 1)
                    def _():
                        halo(t + 2, 2).start()

                return e

            halo(t, 2).wait_recv()
            halo(t, 3).wait_recv()
            lax.fori_loop(0, CX // 8, y_pass, 0)
            for way in range(2):
                halo(t, way).wait_recv()
                halo(t, way).wait_send()
            es[...] = lax.fori_loop(0, CY // 8, x_pass, es[...])

            @pl.when(st < 2)
            def _():
                back(s).start()

            return 0

        lax.fori_loop(0, 2, finish, 0)
        if rounds > 3:

            @pl.when(st == 1)
            def _():
                add_sums(2)
                send_sums(3)

        return 0

    lax.fori_loop(0, 3, stage, 0)

    add_sums(rounds - 1)
    cells = float(n_x * CX * n_y * CY)
    shift[...] = RELAX * (aro[rounds] * (1.0 / cells) - tg[...])

    def drain(t, _):
        for way in (2, 3):
            halo(t, way).wait_send()
        return 0

    lax.fori_loop(0, 6, drain, 0)

    for r in range(rounds):
        for copy in exchange(r):
            copy.wait_send()
    east_edge.wait_send()
    north_edge.wait_send()


def solve(adv, shift, im, av, cp, out, rh, ob, osem):
    for s in range(2):
        for c in range(TILES):
            value = adv[s, pl.ds(c * 128, 128), :] - shift[s : s + 1, :]
            rh[s, pl.ds(c, NZ, stride=8), :] = jnp.transpose(value)

    zero = jnp.zeros((8, 128), jnp.float32)

    def forward(k8, carry):
        d0, d1 = carry
        base = pl.multiple_of(k8 * (TURN * 8), TURN * 8)
        rows = [pl.ds(base + 8 * i, 8) for i in range(TURN)]
        data = [(im[r, :], av[r, :], rh[0, r, :], rh[1, r, :]) for r in rows]
        for i, (inverse, a, r0, r1) in enumerate(data):
            d0 = r0 * inverse + a * d0
            d1 = r1 * inverse + a * d1
            rh[0, rows[i], :] = d0
            rh[1, rows[i], :] = d1
        return d0, d1

    lax.fori_loop(0, NZ // TURN, forward, (zero, zero))

    def backward(j8, carry):
        v0, v1 = carry
        base = pl.multiple_of((NZ // TURN - 1 - j8) * (TURN * 8), TURN * 8)
        rows = [pl.ds(base + 8 * (TURN - 1 - i), 8) for i in range(TURN)]
        data = [(cp[r, :], rh[0, r, :], rh[1, r, :]) for r in rows]
        for i, (c, r0, r1) in enumerate(data):
            v0 = r0 + c * v0
            v1 = r1 + c * v1
            rh[0, rows[i], :] = v0
            rh[1, rows[i], :] = v1
        return v0, v1

    lax.fori_loop(0, NZ // TURN, backward, (zero, zero))
    stores = []
    for s in range(2):
        for c in range(TILES):
            rows = pl.ds(c * 128, 128)
            ob[s, rows, :] = jnp.transpose(rh[s, pl.ds(c, NZ, stride=8), :])
            store = pltpu.make_async_copy(ob.at[s, rows], out.at[s, rows], osem.at[s, c])
            store.start()
            stores.append(store)
    for store in stores:
        store.wait()


def in_hbm(value):
    return pltpu.with_memory_space_constraint(value, pltpu.HBM)


def body(n_x, n_y, scalars, east_wind, north_wind, up_wind, diffusivity, target_profile):
    rounds = 2 * digits(n_x)[0]
    hbm = pl.BlockSpec(memory_space=pltpu.HBM)
    f32 = jnp.float32
    vmem = pltpu.VMEM
    dma = pltpu.SemaphoreType.DMA
    resident = pl.BlockSpec(memory_space=pltpu.VMEM)
    columns = jax.ShapeDtypeStruct((LEVELS * 8, 128), f32)
    parts = pl.pallas_call(
        functools.partial(kernel, n_x, n_y),
        out_shape=[
            jax.ShapeDtypeStruct((2, CX, CY, NZ), f32), jax.ShapeDtypeStruct((2, NZ), f32), columns, columns, columns,
        ],
        in_specs=[hbm] * 6,
        out_specs=[resident] * 5,
        scratch_shapes=[
            vmem((2, CX, CY, NZ), f32),
            vmem((6, 2, H, CY, NZ), f32),
            vmem((2, CX, CY, NZ), f32),
            vmem((4, 2, YROWS, NZ), f32),
            vmem((2, CELLS, NZ), f32),
            vmem((CELLS, NZ), f32),
            vmem((CELLS + CY, NZ), f32),
            vmem((CELLS + CX, NZ), f32),
            vmem((CELLS, NZ), f32),
            vmem((CELLS, NZ), f32),
            vmem((CELLS, NZ), f32),
            vmem((2, NZ), f32),
            vmem(((LEVELS + 1) * 8, 128), f32),
            vmem((8, 128), f32),
            vmem((rounds + 1, 2, NZ), f32),
            vmem((rounds, 3, 2, NZ), f32),
            dma((8,)),
            dma((2,)),
            dma((6, 4)),
            dma((6, 4)),
            dma((2,)),
            dma((2,)),
            dma((rounds, 3)),
            dma((rounds, 3)),
        ],
        compiler_params=pltpu.CompilerParams(
            collective_id=0, has_side_effects=True, vmem_limit_bytes=48 * 1024 * 1024
        ),
        cost_estimate=pl.CostEstimate(flops=80_000_000, bytes_accessed=4_000_000, transcendentals=0),
    )(
        in_hbm(scalars),
        in_hbm(east_wind.reshape(CELLS, NZ)),
        in_hbm(north_wind.reshape(CELLS, NZ)),
        in_hbm(up_wind.reshape(CELLS, NZ)),
        in_hbm(diffusivity.reshape(CELLS, NZ)),
        in_hbm(target_profile),
    )
    result = pl.pallas_call(
        solve,
        out_shape=jax.ShapeDtypeStruct((2, CELLS, NZ), f32),
        in_specs=[resident] * 5,
        out_specs=hbm,
        scratch_shapes=[
            vmem((2, NZ * 8, 128), f32),
            vmem((2, CELLS, NZ), f32),
            dma((2, TILES)),
        ],
        compiler_params=pltpu.CompilerParams(vmem_limit_bytes=32 * 1024 * 1024),
        cost_estimate=pl.CostEstimate(flops=2_000_000, bytes_accessed=4_000_000, transcendentals=0),
    )(parts[0].reshape(2, CELLS, NZ), *parts[1:])
    return result.reshape(2, CX, CY, NZ)


def solution(mesh):
    placed = (
        P(None, "gx", "gy", None),
        P("gx", "gy", None),
        P("gx", "gy", None),
        P("gx", "gy", None),
        P("gx", "gy", None),
        P(),
    )
    return jax.shard_map(
        functools.partial(body, mesh.shape["gx"], mesh.shape["gy"]),
        mesh=mesh, in_specs=placed, out_specs=P(None, "gx", "gy", None), check_vma=False,
    )
```
